256 devices in a mesh: dp: 32 (over z, y), height: 8 (over x, core).
Axes of the slice: x: 4, y: 4, z: 8, core: 2. Of those that a mesh axis runs over, the one named last changes fastest.
Arguments:
- inputs: bfloat16 [64, 48, 72, 1024], P('dp', 'height'), may hold values from -6 to 6
- conv_out: bfloat16 [64, 48, 72, 256], P('dp', 'height'), may hold values from -70 to 70
- grad_out: bfloat16 [64, 48, 72, 256], P('dp', 'height'), may hold values from -12 to 12
- relu_mask: int32 [64, 48, 72, 256], P('dp', 'height'), may hold values 0 or 1
- norm_gain: float32 [256], replicated, may hold values from 0.5 to 2
- weight: bfloat16 [1024, 9, 256], replicated, may hold values from -0.0625 to 0.0625
Outputs:
- input_grad: bfloat16 [64, 48, 72, 1024], P('dp', 'height')
- weight_grad: float32 [1024, 9, 256], P(('dp', 'height'))
The draws below stay inside these ranges and needn't reach their ends.
All inputs are finite; a program needn't handle non-finite values. No bound on the sum of `relu_mask` on one device may be relied on, other than what follows from the above.
Results may differ from the reference program's by a relative error of at most 0.0049.
Values may be sent and summed in bfloat16 or wider, within the bound.
No kernel may reach another device: no remote copies, remote signals or barrier semaphores. Data moves between devices by JAX's collectives and lax.ppermute only.
A program may use at most 128 MiB of HBM per device.

```python
import math
import jax
import jax.numpy as jnp
from jax import lax

HEIGHT = 48
COLS = 72
CIN = 1024
COUT = 256
RATE = 18
IMAGES = 64


def draw_conv_out(key, part):
    key = jax.random.fold_in(key, 11)
    first_key, second_key, third_key = jax.random.split(key, 3)
    row_scale = 3.0 ** (jnp.arange(HEIGHT, dtype=jnp.float32) / (HEIGHT - 1))
    spread = jnp.exp(jax.random.uniform(second_key, (COUT,), jnp.float32, jnp.log(0.5), jnp.log(5.0)))
    offset = jnp.clip(jax.random.normal(third_key, (COUT,), jnp.float32), -2.0, 2.0)
    noise_base = jnp.clip(jax.random.normal(first_key, (IMAGES, HEIGHT, COLS, COUT), jnp.float32), -4.0, 4.0)
    return ((noise_base * spread + offset) * row_scale[None, :, None, None]).astype(jnp.bfloat16)


def draw_grad_out(key, part):
    key = jax.random.fold_in(key, 12)
    row_scale = 3.0 ** (1.0 - jnp.arange(HEIGHT, dtype=jnp.float32) / (HEIGHT - 1))
    noise_base = jnp.clip(jax.random.normal(key, (IMAGES, HEIGHT, COLS, COUT), jnp.float32), -4.0, 4.0)
    return (noise_base * row_scale[None, :, None, None]).astype(jnp.bfloat16)


def set_ends(entries, stream_key, smallest, high):
    shape = entries.shape
    index_at = [jax.random.randint(jax.random.fold_in(stream_key, axis), (), 0, shape[axis]) for axis in range(len(shape))]
    entries = entries.at[tuple(index_at)].set(smallest)
    longest = shape.index(max(shape))
    index_at[longest] = (index_at[longest] + 1) % shape[longest]
    return entries.at[tuple(index_at)].set(high)


def steps_of(stream_key, extent, cuts, low, top_value):
    level, own = 1.0, jax.random.fold_in(stream_key, 6)
    for dim, shards_of in cuts:
        steps = jnp.exp(jax.random.uniform(jax.random.fold_in(own, dim), (shards_of,), jnp.float32, low / len(cuts), top_value / len(cuts)))
        level = level * jnp.repeat(steps, extent[dim] // shards_of).reshape([-1 if axis == dim else 1 for axis in range(len(extent))])
    return level


def scatter_about(key, dims, scale, limit, cuts=(), held_as=jnp.bfloat16):
    result = scale * jax.random.normal(key, dims, jnp.float32)
    if cuts:
        result = result * steps_of(key, dims, cuts, -0.22, 0.18)
    return jnp.clip(result, -limit, limit).astype(held_as)


def setup_inputs(seed: int = 0) -> dict:
    splits = jax.random.split(jax.random.key(seed), 7)
    inputs = scatter_about(splits[0], (IMAGES, HEIGHT, COLS, CIN), 1.0, 6.0, ((0, 32), (1, 8)))
    conv_out = draw_conv_out(jax.random.fold_in(splits[6], 71), 0)
    grad_out = draw_grad_out(jax.random.fold_in(splits[6], 71), 0)
    relu_mask = set_ends((jax.random.randint(splits[3], (IMAGES, HEIGHT, COLS, COUT), 0, 2) < 1).astype(jnp.int32), jax.random.fold_in(splits[3], 1), 0, 1)
    norm_gain = jnp.clip(jnp.exp(jax.random.uniform(splits[4], (COUT,), jnp.float32, math.log(0.5), math.log(2.0))), 0.5, 2.0)
    weight = scatter_about(splits[5], (CIN, 9, COUT), (9 * CIN) ** -0.5, 0.0625)
    return {"inputs": inputs, "conv_out": conv_out, "grad_out": grad_out, "relu_mask": relu_mask, "norm_gain": norm_gain, "weight": weight}


EPSILON = 1e-05

def shifted_taps(grad_block):
    padded = jnp.pad(grad_block, ((RATE, RATE), (RATE, RATE), (0, 0)))
    pieces = []
    for row_step in (-1, 0, 1):
        for col_step in (-1, 0, 1):
            row_start = RATE - RATE * row_step
            col_start = RATE - RATE * col_step
            pieces.append(padded[row_start:row_start + HEIGHT, col_start:col_start + COLS, :])
    return jnp.concatenate(pieces, axis=2)

def reference(inputs, conv_out, grad_out, relu_mask, norm_gain, weight):
    weight_flat = weight.reshape(CIN, 9 * COUT)

    def one_image(running, sliced):
        sample, forward, cotangent, passed = sliced
        values = forward.astype(jnp.float32)
        chan_mean = lax.optimization_barrier(jnp.mean(values, axis=(0, 1)))
        second = lax.optimization_barrier(jnp.mean(values * values, axis=(0, 1)))
        inv_std = 1.0 / jnp.sqrt(second - chan_mean * chan_mean + EPSILON)
        normed = (values - chan_mean) * inv_std
        scaled = norm_gain * (cotangent.astype(jnp.float32) * passed.astype(jnp.float32))
        pre_grad = (inv_std * (scaled - lax.optimization_barrier(jnp.mean(scaled, axis=(0, 1))) - normed * lax.optimization_barrier(jnp.mean(scaled * normed, axis=(0, 1))))).astype(jnp.bfloat16)
        stacked = shifted_taps(pre_grad).reshape(HEIGHT * COLS, 9 * COUT)
        sample_grad = lax.dot_general(stacked, weight_flat, (((1,), (1,)), ((), ())), preferred_element_type=jnp.float32).astype(jnp.bfloat16)
        running = running + lax.dot_general(sample.reshape(HEIGHT * COLS, CIN), stacked, (((0,), (0,)), ((), ())), preferred_element_type=jnp.float32)
        return (running, sample_grad.reshape(HEIGHT, COLS, CIN))
    summed, input_grad = lax.scan(one_image, jnp.zeros((CIN, 9 * COUT), jnp.float32), (inputs, conv_out, grad_out, relu_mask))
    return (input_grad, (summed * (1.0 / IMAGES)).reshape(CIN, 9, COUT))
```

```python
import jax
import jax.numpy as jnp
from jax import lax
from jax.sharding import Mesh, PartitionSpec as P

RATE = 18
EPSILON = 1e-05
F32 = jnp.float32
BF16 = jnp.bfloat16


def ring(axis, steps):
    count = lax.axis_size(axis)
    return [(source, (source + steps) % count) for source in range(count)]


def rotated(value, axis, steps):
    return lax.ppermute(value, axis, ring(axis, steps))


def shifted(value, axis, steps):
    count = lax.axis_size(axis)
    first, last = (max(0, -steps), min(count, count - steps))
    return lax.ppermute(value, axis, [(source, source + steps) for source in range(first, last)])


def others(axis):
    count = lax.axis_size(axis)
    return sorted(range(1, count), key=lambda step: min(step, count - step))


def summed(value, axis):
    total = value
    for step in others(axis):
        total = total + rotated(value, axis, step)
    return total


def scattered(value, axis, dim):
    count = lax.axis_size(axis)
    index = lax.axis_index(axis)
    total = lax.dynamic_index_in_dim(value, index, dim, keepdims=False)
    terms = []
    for step in others(axis):
        block = lax.dynamic_index_in_dim(value, lax.rem(index + step, count), dim, keepdims=False)
        terms.append(rotated(block.astype(BF16), axis, step))
    for term in terms:
        total = total + term.astype(F32)
    return total


def column_taps(block):
    image_count, row_count, col_count, channels = block.shape
    padded = jnp.pad(block, ((0, 0), (0, 0), (RATE, RATE), (0, 0)))
    pieces = [
        padded[:, :, RATE - RATE * step : RATE - RATE * step + col_count, :] for step in (-1, 0, 1)
    ]
    return jnp.concatenate(pieces, axis=3).reshape(
        image_count * row_count * col_count, 3 * channels
    )


def per_device(inputs, conv_out, grad_out, relu_mask, norm_gain, weight):
    image_count, row_count, col_count, channels_in = inputs.shape
    channels_out = conv_out.shape[3]
    z_size, y_size, x_size = (lax.axis_size(axis) for axis in ("z", "y", "x"))
    height = ("x", "core")
    cell_count = row_count * col_count * lax.axis_size(height)
    core = lax.axis_index("core")
    values = conv_out.astype(F32)
    passed = grad_out.astype(F32) * relu_mask.astype(F32)
    sums = jnp.stack(
        [
            jnp.sum(values, axis=(1, 2)),
            jnp.sum(values * values, axis=(1, 2)),
            jnp.sum(passed, axis=(1, 2)),
            jnp.sum(passed * values, axis=(1, 2)),
        ]
    )
    sums = sums + rotated(sums, "core", 1)
    means = summed(sums, "x") / cell_count
    chan_mean, second, passed_mean, product_mean = (means[n] for n in range(4))
    inv_std = 1.0 / jnp.sqrt(second - chan_mean * chan_mean + EPSILON)
    grad_mean = norm_gain * passed_mean
    cross_mean = norm_gain * (product_mean - chan_mean * passed_mean) * inv_std

    def spread(value):
        return value[:, None, None, :]

    normed = (values - spread(chan_mean)) * spread(inv_std)
    pre_grad = (
        spread(inv_std) * (norm_gain * passed - spread(grad_mean) - normed * spread(cross_mean))
    ).astype(BF16)
    distance = RATE // row_count
    below = shifted(pre_grad, height, -distance)
    above = shifted(pre_grad, height, distance)
    taps = [column_taps(block) for block in (below, pre_grad, above)]

    input_flat = inputs.reshape(image_count * row_count * col_count, channels_in)
    half = 3 * channels_out // 2

    def kernel_grad(stacked):
        def product(which):
            columns = lax.dynamic_slice_in_dim(stacked, which * half, half, axis=1)
            return lax.dot_general(
                input_flat, columns, (((0,), (0,)), ((), ())), preferred_element_type=F32
            )

        sent = product(1 - core).astype(BF16)
        total = product(core) + rotated(sent, "core", 1).astype(F32)
        return total.reshape(z_size, y_size, x_size, -1, half)

    middle = scattered(scattered(kernel_grad(taps[1]), "y", 1), "x", 1)
    first = scattered(scattered(kernel_grad(taps[0]), "x", 2), "y", 1)
    last = scattered(scattered(kernel_grad(taps[2]), "y", 1), "x", 1)
    merged = jnp.concatenate([first, middle, last], axis=2)
    rows = merged.shape[1] // 2
    merged = merged.reshape(z_size, 2, rows, 3 * half).astype(BF16).reshape(z_size * 2, rows, 3 * half)
    merged = lax.all_to_all(merged, ("z", "core"), 0, 0)
    merged = jnp.sum(merged.reshape(z_size, 2, rows, 3, half).astype(F32), axis=0)
    inv_images = 1.0 / (image_count * lax.axis_size(("z", "y")))
    weight_grad = jnp.moveaxis(merged, 0, 2).reshape(rows, 9, channels_out) * inv_images

    weight_flat = weight.reshape(channels_in, 9 * channels_out)
    input_grad = lax.dot_general(
        jnp.concatenate(taps, axis=1), weight_flat, (((1,), (1,)), ((), ())), preferred_element_type=F32
    ).astype(BF16)
    return (input_grad.reshape(inputs.shape), weight_grad)


def solution(mesh):
    cores = 2
    x_size = mesh.shape["height"] // cores
    y_size = 4
    z_size = mesh.shape["dp"] // y_size
    parted = Mesh(
        mesh.devices.reshape(z_size, y_size, x_size, cores), ("z", "y", "x", "core")
    )
    cells = P(("z", "y"), ("x", "core"), None, None)
    return jax.shard_map(
        per_device,
        mesh=parted,
        in_specs=(cells, cells, cells, cells, P(), P()),
        out_specs=(cells, P(("z", "y", "x", "core"), None, None)),
        check_vma=False,
    )
```

```python
import jax
import jax.numpy as jnp
from jax import lax
from jax.experimental import pallas as pl
from jax.experimental.pallas import tpu as pltpu
from jax.sharding import Mesh, PartitionSpec as P

RATE = 18
EPSILON = 1e-05
F32 = jnp.float32
BF16 = jnp.bfloat16
VMEM_LIMIT = 48 * 1024 * 1024


def swapped(value):
    return lax.ppermute(value, "core", [(0, 1), (1, 0)])


def around(value, steps):
    return lax.ppermute(value, "x", [(source, (source + steps) % 4) for source in range(4)])


def along(value, steps):
    pairs = [(source, source + steps) for source in range(4) if 0 <= source + steps < 4]
    return lax.ppermute(value, "x", pairs)


def column_taps(block, col_count):
    cells, channels = block.shape
    wide = block.astype(F32)
    column = lax.broadcasted_iota(jnp.int32, (cells // col_count, col_count, channels), 1)
    column = column.reshape(cells, channels)
    before = jnp.where(column < col_count - RATE, pltpu.roll(wide, cells - RATE, 0), 0.0)
    after = jnp.where(column >= RATE, pltpu.roll(wide, RATE, 0), 0.0)
    return [before.astype(BF16), block, after.astype(BF16)]


def transposed(value):
    rows, columns = value.shape
    width = 256

    def body(in_ref, out_ref):
        out_ref[...] = in_ref[...].T

    return pl.pallas_call(
        body,
        grid=(columns // width,),
        in_specs=[pl.BlockSpec((rows, width), lambda i: (0, i))],
        out_specs=pl.BlockSpec((width, rows), lambda i: (i, 0)),
        out_shape=jax.ShapeDtypeStruct((columns, rows), value.dtype),
        compiler_params=pltpu.CompilerParams(vmem_limit_bytes=VMEM_LIMIT),
        cost_estimate=pl.CostEstimate(flops=0, bytes_accessed=4 * rows * columns, transcendentals=0),
    )(value)


def product_call(body, whole, fixed, lhs, blocks, columns, extra):
    channels_in, cells = lhs[0].shape
    steps = 4
    tall = channels_in // steps
    deep = channels_in // blocks // steps
    resident = lambda value: pl.BlockSpec(value.shape, lambda i: (0,) * value.ndim)
    return pl.pallas_call(
        body,
        grid=(steps,),
        in_specs=[pl.BlockSpec(memory_space=pltpu.SMEM)] * len(whole)
        + [resident(value) for value in fixed]
        + [pl.BlockSpec((tall, cells), lambda i: (i, 0)) for _ in lhs],
        out_specs=[pl.BlockSpec((blocks, deep, columns), lambda i: (0, i, 0))]
        + [resident(value) for value in extra],
        out_shape=[jax.ShapeDtypeStruct((blocks, deep * steps, columns), BF16)] + extra,
        scratch_shapes=[pltpu.VMEM((2, cells, columns), BF16)],
        compiler_params=pltpu.CompilerParams(vmem_limit_bytes=VMEM_LIMIT),
        cost_estimate=pl.CostEstimate(
            flops=4 * channels_in * cells * columns,
            bytes_accessed=4 * channels_in * cells + 2 * channels_in * columns,
            transcendentals=0,
        ),
    )(*whole, *fixed, *lhs)


def multiply(own_ref, other_ref, stacked, out_ref):
    total = jnp.dot(own_ref[...], stacked[0], preferred_element_type=F32)
    total = total + jnp.dot(other_ref[...], stacked[1], preferred_element_type=F32)
    blocks, deep, columns = out_ref.shape
    total = total.reshape(deep // 8, blocks, 8, columns)
    for group in range(deep // 16):
        pair = jnp.concatenate([total[2 * group], total[2 * group + 1]], axis=1)
        out_ref[:, group * 16 : group * 16 + 16, :] = pair.astype(BF16)


def middle_terms(pre_own, pre_other, own, other, col_count, blocks):
    width = pre_own.shape[1]

    def body(a_ref, b_ref, own_ref, other_ref, out_ref, stacked):
        @pl.when(pl.program_id(0) == 0)
        def _():
            for which, ref in enumerate((a_ref, b_ref)):
                for place, tap in enumerate(column_taps(ref[...], col_count)):
                    stacked[which, :, place * width : (place + 1) * width] = tap

        multiply(own_ref, other_ref, stacked, out_ref)

    return product_call(body, [], [pre_own, pre_other], [own, other], blocks, 3 * width, [])[0]


def side_terms(place, up, down, far, own, other, col_count, blocks):
    width = up.shape[1]

    def body(place_ref, up_ref, down_ref, far_ref, own_ref, other_ref, out_ref, mine_ref, theirs_ref, stacked):
        @pl.when(pl.program_id(0) == 0)
        def _():
            first = place_ref[1] == 0
            early = place_ref[0] < 2
            far_block = far_ref[...]
            zero = jnp.zeros_like(far_block)
            far_down = jnp.where(early, far_block, zero)
            far_up = jnp.where(early, zero, far_block)
            up_block, down_block = up_ref[...], down_ref[...]
            mine_ref[0] = jnp.where(first, down_block, far_down)
            theirs_ref[0] = jnp.where(first, far_down, down_block)
            mine_ref[1] = jnp.where(first, far_up, up_block)
            theirs_ref[1] = jnp.where(first, up_block, far_up)
            for which, ref in enumerate((mine_ref, theirs_ref)):
                for side in range(2):
                    for spot, tap in enumerate(column_taps(ref[side], col_count)):
                        at = (3 * side + spot) * width
                        stacked[which, :, at : at + width] = tap

        multiply(own_ref, other_ref, stacked, out_ref)

    pair = jax.ShapeDtypeStruct((2,) + up.shape, BF16)
    return product_call(body, [place], [up, down, far], [own, other], blocks, 6 * width, [pair, pair])


def per_device(inputs, conv_out, grad_out, relu_mask, norm_gain, weight):
    image_count, row_count, col_count, channels_in = inputs.shape
    channels_out = conv_out.shape[3]
    z_size, y_size, x_size = (lax.axis_size(axis) for axis in ("z", "y", "x"))
    cell_count = row_count * col_count * x_size * 2
    cells = image_count * row_count * col_count
    half = channels_out // 2
    core = lax.axis_index("core")
    x_place = lax.axis_index("x")

    input_flat = inputs.reshape(cells, channels_in)
    input_other = swapped(input_flat)
    passed = grad_out * relu_mask.astype(BF16)
    raw = jnp.stack([conv_out.reshape(cells, channels_out), passed.reshape(cells, channels_out)])
    mine = lax.dynamic_slice_in_dim(raw, core * half, half, axis=2)
    theirs = swapped(lax.dynamic_slice_in_dim(raw, (1 - core) * half, half, axis=2))
    both = jnp.stack([mine, theirs]).reshape(2, 2, image_count, row_count * col_count, half).astype(F32)
    values, passed = both[:, 0], both[:, 1]
    sums = jnp.stack(
        [jnp.sum(term, axis=(0, 2)) for term in (values, values * values, passed, passed * values)]
    )
    received = [around(sums, steps) for steps in (2, 1, 3)]
    means = (sums + received[0] + received[1] + received[2]) / cell_count
    chan_mean, second, passed_mean, product_mean = (means[n] for n in range(4))
    gain = lax.dynamic_slice_in_dim(norm_gain, core * half, half, axis=0)
    inv_std = 1.0 / jnp.sqrt(second - chan_mean * chan_mean + EPSILON)
    grad_mean = gain * passed_mean
    cross_mean = gain * (product_mean - chan_mean * passed_mean) * inv_std

    def spread(value):
        return value[None, :, None, :]

    normed = (values - spread(chan_mean)) * spread(inv_std)
    pre_grad = spread(inv_std) * (gain * passed - spread(grad_mean) - normed * spread(cross_mean))
    pre_grad = pre_grad.astype(BF16).reshape(2, cells, half)
    pre_own, pre_other = pre_grad[0], pre_grad[1]
    even = jnp.where(core == 0, pre_own, pre_other)
    odd = jnp.where(core == 0, pre_other, pre_own)
    far = around(jnp.where(x_place < 2, odd, even), 2)
    up = along(even, 1)
    down = along(odd, -1)

    own_t, other_t = transposed(input_flat), transposed(input_other)
    blocks = y_size * x_size
    middle = middle_terms(pre_own, pre_other, own_t, other_t, col_count, blocks)
    middle = lax.all_to_all(middle, ("y", "x"), 0, 0)
    place = jnp.stack([x_place, core]).astype(jnp.int32)
    sides, side_own, side_other = side_terms(
        place, up, down, far, own_t, other_t, col_count, blocks
    )
    sides = lax.all_to_all(sides, ("y", "x"), 0, 0)
    middle = jnp.sum(middle.astype(F32), axis=0)
    sides = jnp.sum(sides.astype(F32), axis=0)
    merged = jnp.concatenate([sides[:, : 3 * half], middle, sides[:, 3 * half :]], axis=1)
    rows = merged.shape[0] // z_size // 2
    merged = merged.astype(BF16).reshape(z_size * 2, rows, 9 * half)
    merged = lax.all_to_all(merged, ("z", "core"), 0, 0)
    merged = jnp.sum(merged.reshape(z_size, 2, rows, 9, half).astype(F32), axis=0)
    inv_images = 1.0 / (image_count * lax.axis_size(("z", "y")))
    weight_grad = jnp.moveaxis(merged, 0, 2).reshape(rows, 9, channels_out) * inv_images

    held = jnp.stack([side_own[0], pre_own, side_own[1]])
    got = swapped(jnp.stack([side_other[0], pre_other, side_other[1]]))
    lower = jnp.where(core == 0, held, got)
    upper = jnp.where(core == 0, got, held)
    full = jnp.concatenate([lower, upper], axis=2).reshape(
        3, image_count, row_count, col_count, channels_out
    )
    padded = jnp.pad(full, ((0, 0), (0, 0), (0, 0), (RATE, RATE), (0, 0)))
    pieces = [
        padded[n, :, :, RATE - RATE * step : RATE - RATE * step + col_count, :]
        for n in range(3)
        for step in (-1, 0, 1)
    ]
    stacked = jnp.concatenate(pieces, axis=3).reshape(cells, 9 * channels_out)
    weight, _ = lax.optimization_barrier((weight, pre_own))
    input_grad = lax.dot_general(
        stacked,
        weight.reshape(channels_in, 9 * channels_out),
        (((1,), (1,)), ((), ())),
        preferred_element_type=F32,
    ).astype(BF16)
    return (input_grad.reshape(inputs.shape), weight_grad)


def solution(mesh):
    parted = Mesh(mesh.devices.reshape(8, 4, 4, 2), ("z", "y", "x", "core"))
    cells = P(("z", "y"), ("x", "core"), None, None)
    return jax.shard_map(
        per_device,
        mesh=parted,
        in_specs=(cells, cells, cells, cells, P(), P()),
        out_specs=(cells, P(("z", "y", "x", "core"), None, None)),
        check_vma=False,
    )
```

```python
import jax
import jax.numpy as jnp
from jax import lax
from jax.experimental import pallas as pl
from jax.experimental.pallas import tpu as pltpu
from jax.sharding import Mesh, PartitionSpec as P

RATE = 18
EPSILON = 1e-05
F32 = jnp.float32
BF16 = jnp.bfloat16
VMEM_LIMIT = 40 * 1024 * 1024
AXES = ("z", "y", "x", "core")
Z, Y, X, CORES = 8, 4, 4, 2
SMEM = pl.BlockSpec(memory_space=pltpu.SMEM)


def device(z, y, x, core):
    return ((z * Y + y) * X + x) * CORES + core


def swapped(value):
    return lax.ppermute(value, "core", [(0, 1), (1, 0)])


def around(value, steps):
    return lax.ppermute(value, "x", [(source, (source + steps) % X) for source in range(X)])


def along(value, steps):
    pairs = [(source, source + steps) for source in range(X) if 0 <= source + steps < X]
    return lax.ppermute(value, "x", pairs)


def crossed(value, steps):
    pairs = []
    for z in range(Z):
        for y in range(Y):
            for x in range(X):
                pairs.append((device(z, y, x, 0), device(z, (y + steps) % Y, x, 0)))
                pairs.append((device(z, y, x, 1), device(z, y, (x + steps) % X, 1)))
    return lax.ppermute(value, AXES, pairs)


def exchanged(value):
    groups = [[device(z, y, x, 0) for z in range(Z) for x in range(X)] for y in range(Y)]
    groups += [[device(z, y, x, 1) for z in range(Z) for y in range(Y)] for x in range(X)]
    return lax.all_to_all(value, AXES, 0, 0, axis_index_groups=groups)


def whole(shape):
    return pl.BlockSpec(shape, lambda *_: (0,) * len(shape))


def kernel_call(body, operands, in_specs, out_shape, out_specs, grid=(1,), scratch=(), flops=0):
    moved = sum(value.size * value.dtype.itemsize for value in operands)
    moved += sum(value.size * value.dtype.itemsize for value in out_shape)
    return pl.pallas_call(
        body,
        grid=grid,
        in_specs=in_specs,
        out_specs=out_specs,
        out_shape=out_shape,
        scratch_shapes=list(scratch),
        compiler_params=pltpu.CompilerParams(vmem_limit_bytes=VMEM_LIMIT),
        cost_estimate=pl.CostEstimate(flops=flops, bytes_accessed=moved, transcendentals=0),
    )(*operands)


def prepare(place, conv, grad, mask):
    cells, channels = conv.shape
    half = channels // 2
    steps = 2
    tall = cells // steps

    def body(place_ref, conv_ref, grad_ref, mask_ref, mine_ref, sent_ref):
        core = place_ref[2]
        passed = (grad_ref[...].astype(F32) * mask_ref[...].astype(F32)).astype(BF16)
        conv_block = conv_ref[...]
        first = core == 0
        for which, value in enumerate((conv_block, passed)):
            lower, upper = value[:, :half], value[:, half:]
            mine_ref[which] = jnp.where(first, lower, upper)
            sent_ref[which] = jnp.where(first, upper, lower)

    rows = pl.BlockSpec((tall, channels), lambda i: (i, 0))
    out = jax.ShapeDtypeStruct((2, cells, half), BF16)
    spec = pl.BlockSpec((2, tall, half), lambda i: (0, i, 0))
    return kernel_call(
        body, (place, conv, grad, mask), [SMEM, rows, rows, rows], [out, out], [spec, spec], (steps,)
    )


def statistics(mine, theirs, images):
    _, cells, half = mine.shape
    each = cells // images

    def body(mine_ref, theirs_ref, out_ref):
        for image in range(images):
            rows = pl.ds(image * each, each)
            total = [jnp.zeros((1, half), F32)] * 4
            for ref in (mine_ref, theirs_ref):
                values, passed = ref[0, rows, :].astype(F32), ref[1, rows, :].astype(F32)
                terms = (values, values * values, passed, passed * values)
                total = [old + jnp.sum(new, axis=0, keepdims=True) for old, new in zip(total, terms)]
            for kind in range(4):
                out_ref[pl.ds(kind * images + image, 1), :] = total[kind]

    out = jax.ShapeDtypeStruct((4 * images, half), F32)
    return kernel_call(
        body, (mine, theirs), [whole(mine.shape)] * 2, [out], [whole(out.shape)]
    )[0]


def pre_gradient(place, gain, sums, mine, theirs, images, cell_count):
    _, cells, half = mine.shape
    each = cells // images

    def body(place_ref, gain_ref, a_ref, b_ref, c_ref, d_ref, mine_ref, theirs_ref, even_ref, odd_ref, far_ref):
        first = place_ref[2] == 0
        early = place_ref[1] < X // 2
        means = (a_ref[...] + b_ref[...] + c_ref[...] + d_ref[...]) / cell_count
        gain_row = gain_ref[...]
        for image in range(images):
            rows = pl.ds(image * each, each)
            chan_mean, second, passed_mean, product_mean = (
                means[kind * images + image : kind * images + image + 1] for kind in range(4)
            )
            inv_std = 1.0 / jnp.sqrt(second - chan_mean * chan_mean + EPSILON)
            grad_mean = gain_row * passed_mean
            cross_mean = gain_row * (product_mean - chan_mean * passed_mean) * inv_std
            blocks = []
            for ref in (mine_ref, theirs_ref):
                values, passed = ref[0, rows, :].astype(F32), ref[1, rows, :].astype(F32)
                normed = (values - chan_mean) * inv_std
                blocks.append(inv_std * (gain_row * passed - grad_mean - normed * cross_mean))
            even = jnp.where(first, blocks[0], blocks[1])
            odd = jnp.where(first, blocks[1], blocks[0])
            even_ref[rows, :] = even.astype(BF16)
            odd_ref[rows, :] = odd.astype(BF16)
            far_ref[rows, :] = jnp.where(early, odd, even).astype(BF16)

    out = jax.ShapeDtypeStruct((cells, half), BF16)
    return kernel_call(
        body,
        (place, gain, *sums, mine, theirs),
        [SMEM, whole(gain.shape)] + [whole(sums[0].shape)] * 4 + [whole(mine.shape)] * 2,
        [out] * 3,
        [whole(out.shape)] * 3,
    )


def padded_count(cells):
    return -(-cells // 128) * 128


def transposed(own, other):
    cells, channels = own.shape
    deep = padded_count(cells)
    width = 256

    def body(own_ref, other_ref, out_ref):
        for which, ref in enumerate((own_ref, other_ref)):
            block = jnp.concatenate([ref[...], jnp.zeros((deep - cells, width), BF16)], axis=0)
            out_ref[:, which * deep : (which + 1) * deep] = block.T

    spec = pl.BlockSpec((cells, width), lambda i: (0, i))
    return kernel_call(
        body,
        (own, other),
        [spec, spec],
        [jax.ShapeDtypeStruct((channels, 2 * deep), BF16)],
        [pl.BlockSpec((width, 2 * deep), lambda i: (i, 0))],
        (channels // width,),
    )[0]


def column_taps(block, col_count):
    cells, channels = block.shape
    wide = block.astype(F32)
    column = lax.broadcasted_iota(jnp.int32, (cells // col_count, col_count, channels), 1)
    column = column.reshape(cells, channels)
    before = jnp.where(column < col_count - RATE, pltpu.roll(wide, cells - RATE, 0), 0.0)
    after = jnp.where(column >= RATE, pltpu.roll(wide, RATE, 0), 0.0)
    return before.astype(BF16), block, after.astype(BF16)


def fill(stacked, slot, place, block, col_count):
    cells, width = block.shape
    deep = padded_count(cells)
    for spot, tap in enumerate(column_taps(block, col_count)):
        columns = slice((place + spot) * width, (place + spot + 1) * width)
        stacked[slot * deep : slot * deep + cells, columns] = tap


def multiply(place_ref, lhs_ref, stacked, total, out_refs):
    columns = stacked.shape[1]
    product = jnp.dot(lhs_ref[...], stacked[...], preferred_element_type=F32)
    total[...] = product.reshape(total.shape)
    tall = total.shape[0] * 32

    @pl.when(place_ref[2] == 0)
    def _():
        for steps, ref in enumerate(out_refs):
            chunk = total[:, lax.rem(place_ref[0] + steps, Y), :, :, :]
            ref[...] = chunk.reshape(tall, columns).astype(BF16)

    @pl.when(place_ref[2] != 0)
    def _():
        for steps, ref in enumerate(out_refs):
            chunk = total[:, :, lax.rem(place_ref[1] + steps, X), :, :]
            ref[...] = chunk.reshape(tall, columns).astype(BF16)


def product_call(body, place, fixed, lhs, columns, extra):
    channels_in, deep = lhs.shape
    steps = 2
    tall = channels_in // steps
    chunk = jax.ShapeDtypeStruct((channels_in // 4, columns), BF16)
    return kernel_call(
        body,
        (place, *fixed, lhs),
        [SMEM] + [whole(value.shape) for value in fixed] + [pl.BlockSpec((tall, deep), lambda i: (i, 0))],
        [chunk] * 4 + extra,
        [pl.BlockSpec((tall // 4, columns), lambda i: (i, 0))] * 4 + [whole(value.shape) for value in extra],
        (steps,),
        [pltpu.VMEM((deep, columns), BF16), pltpu.VMEM((tall // 128, Y, X, 8, columns), F32)],
        2 * channels_in * deep * columns,
    )


def middle_terms(place, even, odd, lhs, col_count):
    cells, width = even.shape

    def body(place_ref, even_ref, odd_ref, lhs_ref, *rest):
        stacked, total = rest[4:]

        @pl.when(pl.program_id(0) == 0)
        def _():
            stacked[...] = jnp.zeros_like(stacked)
            first = place_ref[2] == 0
            even_block, odd_block = even_ref[...], odd_ref[...]
            fill(stacked, 0, 0, jnp.where(first, even_block, odd_block), col_count)
            fill(stacked, 1, 0, jnp.where(first, odd_block, even_block), col_count)

        multiply(place_ref, lhs_ref, stacked, total, rest[:4])

    return product_call(body, place, [even, odd], lhs, 3 * width, [])


def side_terms(place, even, odd, up, down, far, lhs, col_count):
    cells, width = up.shape

    def body(place_ref, even_ref, odd_ref, up_ref, down_ref, far_ref, lhs_ref, *rest):
        mine_ref, theirs_ref, stacked, total = rest[4:]

        @pl.when(pl.program_id(0) == 0)
        def _():
            stacked[...] = jnp.zeros_like(stacked)
            first = place_ref[2] == 0
            early = place_ref[1] < X // 2
            far_block = far_ref[...]
            zero = jnp.zeros_like(far_block)
            far_down = jnp.where(early, far_block, zero)
            far_up = jnp.where(early, zero, far_block)
            pairs = ((down_ref[...], far_down), (even_ref[...], odd_ref[...]), (far_up, up_ref[...]))
            for side, (lower, upper) in enumerate(pairs):
                mine = jnp.where(first, lower, upper)
                theirs = jnp.where(first, upper, lower)
                mine_ref[side] = mine
                theirs_ref[side] = theirs
                if side != 1:
                    fill(stacked, 0, 3 * (side // 2), mine, col_count)
                    fill(stacked, 1, 3 * (side // 2), theirs, col_count)

        multiply(place_ref, lhs_ref, stacked, total, rest[:4])

    triple = jax.ShapeDtypeStruct((3, cells, width), BF16)
    return product_call(body, place, [even, odd, up, down, far], lhs, 6 * width, [triple, triple])


def first_sum(middle, sides):
    rows, third = middle[0].shape

    def body(*refs):
        out_ref = refs[-1]
        middle_total = sum(ref[...].astype(F32) for ref in refs[:4])
        side_total = sum(ref[...].astype(F32) for ref in refs[4:8])
        out_ref[:, :third] = side_total[:, :third].astype(BF16)
        out_ref[:, third : 2 * third] = middle_total.astype(BF16)
        out_ref[:, 2 * third :] = side_total[:, third:].astype(BF16)

    steps = 2
    spec = lambda columns: pl.BlockSpec((rows // steps, columns), lambda i: (i, 0))
    return kernel_call(
        body,
        (*middle, *sides),
        [spec(third)] * 4 + [spec(2 * third)] * 4,
        [jax.ShapeDtypeStruct((rows, 3 * third), BF16)],
        [spec(3 * third)],
        (steps,),
    )[0]


def input_gradient(place, held, got, weight, col_count):
    _, cells, half = held.shape
    channels_in, deep = weight.shape
    width = 256

    def body(place_ref, held_ref, got_ref, weight_ref, out_ref, stacked):
        @pl.when(pl.program_id(0) == 0)
        def _():
            first = place_ref[2] == 0
            for side in range(3):
                mine, theirs = held_ref[side], got_ref[side]
                lower, upper = jnp.where(first, mine, theirs), jnp.where(first, theirs, mine)
                for part, block in enumerate((lower, upper)):
                    for spot, tap in enumerate(column_taps(block, col_count)):
                        start = (2 * (3 * side + spot) + part) * half
                        stacked[:, start : start + half] = tap

        out_ref[...] = lax.dot_general(
            stacked[...], weight_ref[...], (((1,), (1,)), ((), ())), preferred_element_type=F32
        ).astype(BF16)

    return kernel_call(
        body,
        (place, held, got, weight),
        [SMEM, whole(held.shape), whole(got.shape), pl.BlockSpec((width, deep), lambda i: (i, 0))],
        [jax.ShapeDtypeStruct((cells, channels_in), BF16)],
        [pl.BlockSpec((cells, width), lambda i: (0, i))],
        (channels_in // width,),
        [pltpu.VMEM((cells, deep), BF16)],
        2 * cells * deep * channels_in,
    )[0]


def per_device(inputs, conv_out, grad_out, relu_mask, norm_gain, weight):
    image_count, row_count, col_count, channels_in = inputs.shape
    channels_out = conv_out.shape[3]
    cell_count = row_count * col_count * X * CORES
    cells = image_count * row_count * col_count
    half = channels_out // 2
    core = lax.axis_index("core")
    place = jnp.stack([lax.axis_index("y"), lax.axis_index("x"), core]).astype(jnp.int32)

    input_flat = inputs.reshape(cells, channels_in)
    mine, sent = prepare(
        place,
        *(value.reshape(cells, channels_out) for value in (conv_out, grad_out, relu_mask)),
    )
    theirs = swapped(sent)
    input_other = swapped(input_flat)
    sums = statistics(mine, theirs, image_count)
    sums = [sums] + [around(sums, steps) for steps in (2, 1, 3)]
    gain = lax.dynamic_slice_in_dim(norm_gain, core * half, half, axis=0).reshape(1, half)
    even, odd, far = pre_gradient(place, gain, sums, mine, theirs, image_count, cell_count)
    far = around(far, 2)
    up = along(even, 1)
    down = along(odd, -1)

    lhs = transposed(input_flat, input_other)
    middle = middle_terms(place, even, odd, lhs, col_count)
    middle = [middle[0]] + [crossed(middle[steps], steps) for steps in (2, 1, 3)]
    *sides, held, sent = side_terms(place, even, odd, up, down, far, lhs, col_count)
    sides = [sides[0]] + [crossed(sides[steps], steps) for steps in (2, 1, 3)]
    merged = first_sum(middle, sides)
    merged = exchanged(merged.reshape(Z * 4, 8, 9 * half))
    inv_images = 1.0 / (image_count * Z * Y)
    merged = jnp.sum(merged.astype(F32), axis=0) * inv_images
    rows = merged.shape[0] // CORES
    kept = lax.dynamic_slice_in_dim(merged, core * rows, rows, axis=0)
    came = swapped(lax.dynamic_slice_in_dim(merged, (1 - core) * rows, rows, axis=0))
    kept, came = kept.reshape(rows, 9, half), came.reshape(rows, 9, half)
    weight_grad = jnp.concatenate(
        [jnp.where(core == 0, kept, came), jnp.where(core == 0, came, kept)], axis=2
    )

    weight, sent, _ = lax.optimization_barrier((weight, sent, sides[1]))
    got = swapped(sent)
    input_grad = input_gradient(
        place, held, got, weight.reshape(channels_in, 9 * channels_out), col_count
    )
    return (input_grad.reshape(inputs.shape), weight_grad)


def solution(mesh):
    parted = Mesh(mesh.devices.reshape(Z, Y, X, CORES), AXES)
    cells = P(("z", "y"), ("x", "core"), None, None)
    return jax.shard_map(
        per_device,
        mesh=parted,
        in_specs=(cells, cells, cells, cells, P(), P()),
        out_specs=(cells, P(AXES, None, None)),
        check_vma=False,
    )
```

```python
import jax
import jax.numpy as jnp
from jax import lax
from jax.experimental import pallas as pl
from jax.experimental.pallas import tpu as pltpu
from jax.sharding import Mesh, PartitionSpec as P

RATE = 18
EPSILON = 1e-05
F32 = jnp.float32
BF16 = jnp.bfloat16
MIB = 1024 * 1024
AXES = ("z", "y", "x", "core")
Z, Y, X, CORES = 8, 4, 4, 2
SMEM = pl.BlockSpec(memory_space=pltpu.SMEM)


def device(z, y, x, core):
    return ((z * Y + y) * X + x) * CORES + core


def swapped(value):
    return lax.ppermute(value, "core", [(0, 1), (1, 0)])


def around(value, steps):
    return lax.ppermute(value, "x", [(source, (source + steps) % X) for source in range(X)])


def along(value, steps):
    pairs = [(source, source + steps) for source in range(X) if 0 <= source + steps < X]
    return lax.ppermute(value, "x", pairs)


def crossed(value, steps):
    pairs = []
    for z in range(Z):
        for y in range(Y):
            for x in range(X):
                pairs.append((device(z, y, x, 0), device(z, (y + steps) % Y, x, 0)))
                pairs.append((device(z, y, x, 1), device(z, y, (x + steps) % X, 1)))
    return lax.ppermute(value, AXES, pairs)


def exchanged(value):
    groups = [[device(z, y, x, 0) for z in range(Z) for x in range(X)] for y in range(Y)]
    groups += [[device(z, y, x, 1) for z in range(Z) for y in range(Y)] for x in range(X)]
    return lax.all_to_all(value, AXES, 0, 0, axis_index_groups=groups)


def whole(shape):
    return pl.BlockSpec(shape, lambda *_: (0,) * len(shape))


def kernel_call(body, operands, in_specs, out_shape, out_specs, grid=(1,), scratch=(), flops=0, vmem=8, light=False):
    moved = sum(value.size * value.dtype.itemsize for value in operands)
    moved += sum(value.size * value.dtype.itemsize for value in out_shape)
    if light:
        moved, flops = 0, 0
    return pl.pallas_call(
        body,
        grid=grid,
        in_specs=in_specs,
        out_specs=out_specs,
        out_shape=out_shape,
        scratch_shapes=list(scratch),
        compiler_params=pltpu.CompilerParams(vmem_limit_bytes=vmem * MIB),
        cost_estimate=pl.CostEstimate(flops=flops, bytes_accessed=moved, transcendentals=0),
    )(*operands)


def prepare(place, conv, grad, mask, images):
    channels = conv.shape[3]
    half = channels // 2
    each = conv.shape[1] * conv.shape[2]
    cells = images * each

    def body(place_ref, *refs):
        sources, (mine_ref, sent_ref, mine_sum_ref, sent_sum_ref) = refs[:3], refs[3:7]
        buffers, sems = refs[7:10], refs[10]
        first = place_ref[2] == 0
        copies = [
            [
                pltpu.make_async_copy(source.at[image], buffer.at[image], sems.at[image, n])
                for n, (source, buffer) in enumerate(zip(sources, buffers))
            ]
            for image in range(images)
        ]
        for group in copies:
            for copy in group:
                copy.start()
        for image in range(images):
            for copy in copies[image]:
                copy.wait()
            rows = slice(image * each, (image + 1) * each)
            conv_block, grad_block, mask_block = (buffer[image].reshape(each, channels) for buffer in buffers)
            passed = grad_block.astype(F32) * mask_block.astype(F32)
            values = conv_block.astype(F32)
            for which, value in enumerate((conv_block, passed.astype(BF16))):
                lower, upper = value[:, :half], value[:, half:]
                mine_ref[which, rows, :] = jnp.where(first, lower, upper)
                sent_ref[which, rows, :] = jnp.where(first, upper, lower)
            for kind, term in enumerate((values, values * values, passed, passed * values)):
                total = jnp.sum(term, axis=0, keepdims=True)
                lower, upper = total[:, :half], total[:, half:]
                row = slice(kind * images + image, kind * images + image + 1)
                mine_sum_ref[row, :] = jnp.where(first, lower, upper)
                sent_sum_ref[row, :] = jnp.where(first, upper, lower)

    out = jax.ShapeDtypeStruct((2, cells, half), BF16)
    total = jax.ShapeDtypeStruct((4 * images, half), F32)
    outs = [out, out, total, total]
    return kernel_call(
        body,
        (place, conv, grad, mask),
        [SMEM] + [pl.BlockSpec(memory_space=pltpu.HBM)] * 3,
        outs,
        [whole(value.shape) for value in outs],
        scratch=[pltpu.VMEM(value.shape, value.dtype) for value in (conv, grad, mask)]
        + [pltpu.SemaphoreType.DMA((images, 3))],
        vmem=60,
    )


def pre_gradient(place, gain, sums, mine, theirs, images, cell_count):
    _, cells, half = mine.shape
    each = cells // images

    def body(place_ref, gain_ref, a_ref, b_ref, c_ref, d_ref, mine_ref, theirs_ref, even_ref, odd_ref, far_ref):
        first = place_ref[2] == 0
        early = place_ref[1] < X // 2
        means = (a_ref[...] + b_ref[...] + c_ref[...] + d_ref[...]) / cell_count
        gain_row = gain_ref[...]
        for image in range(images):
            rows = pl.ds(image * each, each)
            chan_mean, second, passed_mean, product_mean = (
                means[kind * images + image : kind * images + image + 1] for kind in range(4)
            )
            inv_std = 1.0 / jnp.sqrt(second - chan_mean * chan_mean + EPSILON)
            grad_mean = gain_row * passed_mean
            cross_mean = gain_row * (product_mean - chan_mean * passed_mean) * inv_std
            blocks = []
            for ref in (mine_ref, theirs_ref):
                values, passed = ref[0, rows, :].astype(F32), ref[1, rows, :].astype(F32)
                normed = (values - chan_mean) * inv_std
                blocks.append(inv_std * (gain_row * passed - grad_mean - normed * cross_mean))
            even = jnp.where(first, blocks[0], blocks[1])
            odd = jnp.where(first, blocks[1], blocks[0])
            even_ref[rows, :] = even.astype(BF16)
            odd_ref[rows, :] = odd.astype(BF16)
            far_ref[rows, :] = jnp.where(early, odd, even).astype(BF16)

    out = jax.ShapeDtypeStruct((cells, half), BF16)
    return kernel_call(
        body,
        (place, gain, *sums, mine, theirs),
        [SMEM, whole(gain.shape)] + [whole(sums[0].shape)] * 4 + [whole(mine.shape)] * 2,
        [out] * 3,
        [whole(out.shape)] * 3,
    )


def padded_count(cells):
    return -(-cells // 128) * 128


def transposed(own, other):
    cells, channels = own.shape
    deep = padded_count(cells)
    width = 256

    def body(own_ref, other_ref, out_ref):
        for which, ref in enumerate((own_ref, other_ref)):
            block = jnp.concatenate([ref[...], jnp.zeros((deep - cells, width), BF16)], axis=0)
            out_ref[:, which * deep : (which + 1) * deep] = block.T

    spec = pl.BlockSpec((cells, width), lambda i: (0, i))
    return kernel_call(
        body,
        (own, other),
        [spec, spec],
        [jax.ShapeDtypeStruct((channels, 2 * deep), BF16)],
        [pl.BlockSpec((width, 2 * deep), lambda i: (i, 0))],
        (channels // width,),
        light=True,
    )[0]


def column_taps(block, col_count):
    cells, channels = block.shape
    wide = block.astype(F32)
    column = lax.broadcasted_iota(jnp.int32, (cells // col_count, col_count, channels), 1)
    column = column.reshape(cells, channels)
    before = jnp.where(column < col_count - RATE, pltpu.roll(wide, cells - RATE, 0), 0.0)
    after = jnp.where(column >= RATE, pltpu.roll(wide, RATE, 0), 0.0)
    return before.astype(BF16), block, after.astype(BF16)


def fill(stacked, slot, place, block, col_count):
    cells, width = block.shape
    deep = padded_count(cells)
    for spot, tap in enumerate(column_taps(block, col_count)):
        columns = slice((place + spot) * width, (place + spot + 1) * width)
        stacked[slot * deep : slot * deep + cells, columns] = tap


def clear_padding(stacked, cells):
    deep, columns = stacked.shape
    block = deep // 2
    for slot in range(2):
        stacked[slot * block + cells : (slot + 1) * block, :] = jnp.zeros((block - cells, columns), BF16)


def multiply(place_ref, lhs_ref, stacked, total, store):
    columns = stacked.shape[1]
    product = jnp.dot(lhs_ref[...], stacked[...], preferred_element_type=F32)
    total[...] = product.reshape(total.shape)
    tall = total.shape[0] * 32

    @pl.when(place_ref[2] == 0)
    def _():
        for steps in range(Y):
            chunk = total[:, lax.rem(place_ref[0] + steps, Y), :, :, :]
            store(steps, chunk.reshape(tall, columns).astype(BF16))

    @pl.when(place_ref[2] != 0)
    def _():
        for steps in range(X):
            chunk = total[:, :, lax.rem(place_ref[1] + steps, X), :, :]
            store(steps, chunk.reshape(tall, columns).astype(BF16))


def product_call(body, place, fixed, lhs, terms, columns, wide, extra, light=False):
    channels_in, deep = lhs.shape
    steps = 2
    tall = channels_in // steps
    chunk = lambda width: pl.BlockSpec((tall // 4, width), lambda i: (i, 0))
    return kernel_call(
        body,
        (place, *fixed, lhs, *terms),
        [SMEM] + [whole(value.shape) for value in fixed] + [pl.BlockSpec((tall, deep), lambda i: (i, 0))]
        + [chunk(value.shape[1]) for value in terms],
        [jax.ShapeDtypeStruct((channels_in // 4, wide), BF16)] * 4 + extra,
        [chunk(wide)] * 4 + [whole(value.shape) for value in extra],
        (steps,),
        [pltpu.VMEM((deep, columns), BF16), pltpu.VMEM((tall // 128, Y, X, 8, columns), F32)],
        2 * channels_in * deep * columns,
        24,
        light,
    )


def middle_terms(place, even, odd, lhs, col_count):
    cells, width = even.shape

    def body(place_ref, even_ref, odd_ref, lhs_ref, *rest):
        stacked, total = rest[4:]

        @pl.when(pl.program_id(0) == 0)
        def _():
            clear_padding(stacked, cells)
            first = place_ref[2] == 0
            even_block, odd_block = even_ref[...], odd_ref[...]
            fill(stacked, 0, 0, jnp.where(first, even_block, odd_block), col_count)
            fill(stacked, 1, 0, jnp.where(first, odd_block, even_block), col_count)

        def store(steps, chunk):
            rest[steps][...] = chunk

        multiply(place_ref, lhs_ref, stacked, total, store)

    return product_call(body, place, [even, odd], lhs, [], 3 * width, 3 * width, [], True)


def all_terms(place, even, odd, up, down, far, lhs, middle, col_count):
    cells, width = up.shape
    third = 3 * width

    def body(place_ref, even_ref, odd_ref, up_ref, down_ref, far_ref, lhs_ref, *rest):
        middle_refs, out_refs = rest[:4], rest[4:8]
        mine_ref, theirs_ref, stacked, total = rest[8:]

        @pl.when(pl.program_id(0) == 0)
        def _():
            clear_padding(stacked, cells)
            first = place_ref[2] == 0
            early = place_ref[1] < X // 2
            far_block = far_ref[...]
            zero = jnp.zeros_like(far_block)
            far_down = jnp.where(early, far_block, zero)
            far_up = jnp.where(early, zero, far_block)
            pairs = ((down_ref[...], far_down), (even_ref[...], odd_ref[...]), (far_up, up_ref[...]))
            for side, (lower, upper) in enumerate(pairs):
                mine = jnp.where(first, lower, upper)
                theirs = jnp.where(first, upper, lower)
                mine_ref[side] = mine
                theirs_ref[side] = theirs
                if side != 1:
                    fill(stacked, 0, 3 * (side // 2), mine, col_count)
                    fill(stacked, 1, 3 * (side // 2), theirs, col_count)

        def store(steps, chunk):
            out_refs[steps][:, :third] = chunk[:, :third]
            out_refs[steps][:, third : 2 * third] = middle_refs[steps][...]
            out_refs[steps][:, 2 * third :] = chunk[:, third:]

        multiply(place_ref, lhs_ref, stacked, total, store)

    triple = jax.ShapeDtypeStruct((3, cells, width), BF16)
    return product_call(
        body, place, [even, odd, up, down, far], lhs, middle, 2 * third, 3 * third, [triple, triple]
    )


def first_sum(terms):
    rows, columns = terms[0].shape

    def body(*refs):
        refs[-1][...] = sum(ref[...].astype(F32) for ref in refs[:-1]).astype(BF16)

    steps = 2
    spec = pl.BlockSpec((rows // steps, columns), lambda i: (i, 0))
    return kernel_call(
        body, terms, [spec] * 4, [jax.ShapeDtypeStruct((rows, columns), BF16)], [spec], (steps,)
    )[0]


def input_gradient(place, held, got, weight, col_count):
    _, cells, half = held.shape
    deep, channels_in = weight.shape
    width = 256

    def body(place_ref, held_ref, got_ref, weight_ref, out_ref, stacked):
        @pl.when(pl.program_id(0) == 0)
        def _():
            first = place_ref[2] == 0
            for side in range(3):
                mine, theirs = held_ref[side], got_ref[side]
                lower, upper = jnp.where(first, mine, theirs), jnp.where(first, theirs, mine)
                for part, block in enumerate((lower, upper)):
                    for spot, tap in enumerate(column_taps(block, col_count)):
                        start = (2 * (3 * side + spot) + part) * half
                        stacked[:, start : start + half] = tap

        out_ref[...] = jnp.dot(
            stacked[...], weight_ref[...], preferred_element_type=F32
        ).astype(BF16)

    return kernel_call(
        body,
        (place, held, got, weight),
        [SMEM, whole(held.shape), whole(got.shape), pl.BlockSpec((deep, width), lambda i: (0, i))],
        [jax.ShapeDtypeStruct((cells, channels_in), BF16)],
        [pl.BlockSpec((cells, width), lambda i: (0, i))],
        (channels_in // width,),
        [pltpu.VMEM((cells, deep), BF16)],
        2 * cells * deep * channels_in,
        24,
    )[0]


def per_device(inputs, conv_out, grad_out, relu_mask, norm_gain, weight):
    image_count, row_count, col_count, channels_in = inputs.shape
    channels_out = conv_out.shape[3]
    cell_count = row_count * col_count * X * CORES
    cells = image_count * row_count * col_count
    half = channels_out // 2
    core = lax.axis_index("core")
    place = jnp.stack([lax.axis_index("y"), lax.axis_index("x"), core]).astype(jnp.int32)

    input_flat = inputs.reshape(cells, channels_in)
    mine, sent, sums, sent_sums = prepare(place, conv_out, grad_out, relu_mask, image_count)
    got_sums = swapped(sent_sums)
    input_flat, sent, got_sums = lax.optimization_barrier((input_flat, sent, got_sums))
    theirs = swapped(sent)
    input_other = swapped(input_flat)
    sums = sums + got_sums
    sums = [sums] + [around(sums, steps) for steps in (2, 1, 3)]
    gain = lax.dynamic_slice_in_dim(norm_gain, core * half, half, axis=0).reshape(1, half)
    lhs = transposed(input_flat, input_other)
    even, odd, far = pre_gradient(place, gain, sums, mine, theirs, image_count, cell_count)
    far = around(far, 2)
    up = along(even, 1)
    down = along(odd, -1)

    middle = middle_terms(place, even, odd, lhs, col_count)
    *terms, held, sent = all_terms(place, even, odd, up, down, far, lhs, middle, col_count)
    terms = [terms[0]] + [crossed(terms[steps], steps) for steps in (2, 1, 3)]
    merged = first_sum(terms)
    merged = exchanged(merged.reshape(Z * 4, 8, 9 * half))
    inv_images = 1.0 / (image_count * Z * Y)
    merged = jnp.sum(merged.astype(F32), axis=0) * inv_images
    rows = merged.shape[0] // CORES
    kept = lax.dynamic_slice_in_dim(merged, core * rows, rows, axis=0)
    came = swapped(lax.dynamic_slice_in_dim(merged, (1 - core) * rows, rows, axis=0))
    kept, came = kept.reshape(rows, 9, half), came.reshape(rows, 9, half)
    weight_grad = jnp.concatenate(
        [jnp.where(core == 0, kept, came), jnp.where(core == 0, came, kept)], axis=2
    )

    weight, held = lax.optimization_barrier((weight, held))
    weight = jnp.transpose(weight, (1, 2, 0)).reshape(9 * channels_out, channels_in)
    input_grad = input_gradient(place, held, swapped(sent), weight, col_count)
    return (input_grad.reshape(inputs.shape), weight_grad)


def solution(mesh):
    parted = Mesh(mesh.devices.reshape(Z, Y, X, CORES), AXES)
    cells = P(("z", "y"), ("x", "core"), None, None)
    return jax.shard_map(
        per_device,
        mesh=parted,
        in_specs=(cells, cells, cells, cells, P(), P()),
        out_specs=(cells, P(AXES, None, None)),
        check_vma=False,
    )
```

```python
import jax
import jax.numpy as jnp
from jax import lax
from jax.experimental import pallas as pl
from jax.experimental.pallas import tpu as pltpu
from jax.sharding import Mesh, PartitionSpec as P

RATE = 18
EPSILON = 1e-05
F32 = jnp.float32
BF16 = jnp.bfloat16
MIB = 1024 * 1024
AXES = ("z", "y", "x", "core")
Z, Y, X, CORES = 8, 4, 4, 2
SMEM = pl.BlockSpec(memory_space=pltpu.SMEM)


def device(z, y, x, core):
    return ((z * Y + y) * X + x) * CORES + core


def swapped(value):
    return lax.ppermute(value, "core", [(0, 1), (1, 0)])


def around(value, steps):
    return lax.ppermute(value, "x", [(source, (source + steps) % X) for source in range(X)])


def crossed(value, steps):
    pairs = []
    for z in range(Z):
        for y in range(Y):
            for x in range(X):
                pairs.append((device(z, y, x, 0), device(z, (y + steps) % Y, x, 0)))
                pairs.append((device(z, y, x, 1), device(z, y, (x + steps) % X, 1)))
    return lax.ppermute(value, AXES, pairs)


def exchanged(value):
    groups = [[device(z, y, x, 0) for z in range(Z) for x in range(X)] for y in range(Y)]
    groups += [[device(z, y, x, 1) for z in range(Z) for y in range(Y)] for x in range(X)]
    return lax.all_to_all(value, AXES, 0, 0, axis_index_groups=groups)


def whole(shape):
    return pl.BlockSpec(shape, lambda *_: (0,) * len(shape))


def kernel_call(body, operands, in_specs, out_shape, out_specs, grid=(1,), scratch=(), flops=0, vmem=8, light=False):
    moved = sum(value.size * value.dtype.itemsize for value in operands)
    moved += sum(value.size * value.dtype.itemsize for value in out_shape)
    if light:
        moved, flops = 0, 0
    return pl.pallas_call(
        body,
        grid=grid,
        in_specs=in_specs,
        out_specs=out_specs,
        out_shape=out_shape,
        scratch_shapes=list(scratch),
        compiler_params=pltpu.CompilerParams(vmem_limit_bytes=vmem * MIB),
        cost_estimate=pl.CostEstimate(flops=flops, bytes_accessed=moved, transcendentals=0),
    )(*operands)


def channel_sums(conv, grad, mask):
    values = conv.astype(F32)
    passed = grad.astype(F32) * mask.astype(F32)
    terms = (values, values * values, passed, passed * values)
    return jnp.stack([jnp.sum(term, axis=(1, 2)) for term in terms]).reshape(-1, conv.shape[3])


def prepare(place, conv, grad, mask):
    cells, channels = conv.shape
    half = channels // 2
    steps = 2
    tall = cells // steps

    def body(place_ref, conv_ref, grad_ref, mask_ref, mine_ref, sent_ref):
        first = place_ref[2] == 0
        passed = (grad_ref[...].astype(F32) * mask_ref[...].astype(F32)).astype(BF16)
        for which, value in enumerate((conv_ref[...], passed)):
            lower, upper = value[:, :half], value[:, half:]
            mine_ref[which] = jnp.where(first, lower, upper)
            sent_ref[which] = jnp.where(first, upper, lower)

    rows = pl.BlockSpec((tall, channels), lambda i: (i, 0))
    out = jax.ShapeDtypeStruct((2, cells, half), BF16)
    spec = pl.BlockSpec((2, tall, half), lambda i: (0, i, 0))
    return kernel_call(
        body,
        (place, conv, grad, mask),
        [SMEM, rows, rows, rows],
        [out, out],
        [spec, spec],
        (steps,),
        vmem=60,
    )


def pre_gradient(place, gain, sums, mine, theirs, images, cell_count):
    _, cells, half = mine.shape
    each = cells // images

    def body(place_ref, gain_ref, a_ref, b_ref, c_ref, d_ref, mine_ref, theirs_ref, even_ref, odd_ref, far_ref):
        first = place_ref[2] == 0
        early = place_ref[1] < X // 2
        means = (a_ref[...] + b_ref[...] + c_ref[...] + d_ref[...]) / cell_count
        means = jnp.where(first, means[:, :half], means[:, half:])
        gain_row = jnp.where(first, gain_ref[:, :half], gain_ref[:, half:])
        for image in range(images):
            rows = pl.ds(image * each, each)
            chan_mean, second, passed_mean, product_mean = (
                means[kind * images + image : kind * images + image + 1] for kind in range(4)
            )
            inv_std = 1.0 / jnp.sqrt(second - chan_mean * chan_mean + EPSILON)
            grad_mean = gain_row * passed_mean
            cross_mean = gain_row * (product_mean - chan_mean * passed_mean) * inv_std
            blocks = []
            for ref in (mine_ref, theirs_ref):
                values, passed = ref[0, rows, :].astype(F32), ref[1, rows, :].astype(F32)
                normed = (values - chan_mean) * inv_std
                blocks.append(inv_std * (gain_row * passed - grad_mean - normed * cross_mean))
            even = jnp.where(first, blocks[0], blocks[1])
            odd = jnp.where(first, blocks[1], blocks[0])
            even_ref[rows, :] = even.astype(BF16)
            odd_ref[rows, :] = odd.astype(BF16)
            far_ref[rows, :] = jnp.where(early, odd, even).astype(BF16)

    out = jax.ShapeDtypeStruct((cells, half), BF16)
    return kernel_call(
        body,
        (place, gain, *sums, mine, theirs),
        [SMEM, whole(gain.shape)] + [whole(sums[0].shape)] * 4 + [whole(mine.shape)] * 2,
        [out] * 3,
        [whole(out.shape)] * 3,
    )


def padded_count(cells):
    return -(-cells // 128) * 128


def transposed(own, other):
    cells, channels = own.shape
    deep = padded_count(cells)
    width = 256

    def body(own_ref, other_ref, out_ref):
        for which, ref in enumerate((own_ref, other_ref)):
            block = jnp.concatenate([ref[...], jnp.zeros((deep - cells, width), BF16)], axis=0)
            out_ref[:, which * deep : (which + 1) * deep] = block.T

    spec = pl.BlockSpec((cells, width), lambda i: (0, i))
    return kernel_call(
        body,
        (own, other),
        [spec, spec],
        [jax.ShapeDtypeStruct((channels, 2 * deep), BF16)],
        [pl.BlockSpec((width, 2 * deep), lambda i: (i, 0))],
        (channels // width,),
        light=True,
    )[0]


def column_taps(block, col_count):
    cells, channels = block.shape
    wide = block.astype(F32)
    column = lax.broadcasted_iota(jnp.int32, (cells // col_count, col_count, channels), 1)
    column = column.reshape(cells, channels)
    before = jnp.where(column < col_count - RATE, pltpu.roll(wide, cells - RATE, 0), 0.0)
    after = jnp.where(column >= RATE, pltpu.roll(wide, RATE, 0), 0.0)
    return before.astype(BF16), block, after.astype(BF16)


def fill(stacked, slot, place, block, col_count):
    cells, width = block.shape
    deep = padded_count(cells)
    for spot, tap in enumerate(column_taps(block, col_count)):
        columns = slice((place + spot) * width, (place + spot + 1) * width)
        stacked[slot * deep : slot * deep + cells, columns] = tap


def clear_padding(stacked, cells):
    deep, columns = stacked.shape
    block = deep // 2
    for slot in range(2):
        stacked[slot * block + cells : (slot + 1) * block, :] = jnp.zeros((block - cells, columns), BF16)


def multiply(place_ref, lhs_ref, stacked, total, store):
    columns = stacked.shape[1]
    product = jnp.dot(lhs_ref[...], stacked[...], preferred_element_type=F32)
    total[...] = product.reshape(total.shape)
    tall = total.shape[0] * 32

    @pl.when(place_ref[2] == 0)
    def _():
        for steps in range(Y):
            chunk = total[:, lax.rem(place_ref[0] + steps, Y), :, :, :]
            store(steps, chunk.reshape(tall, columns).astype(BF16))

    @pl.when(place_ref[2] != 0)
    def _():
        for steps in range(X):
            chunk = total[:, :, lax.rem(place_ref[1] + steps, X), :, :]
            store(steps, chunk.reshape(tall, columns).astype(BF16))


def product_call(body, place, fixed, lhs, terms, columns, wide, extra, light=False):
    channels_in, deep = lhs.shape
    steps = 2
    tall = channels_in // steps
    chunk = lambda width: pl.BlockSpec((tall // 4, width), lambda i: (i, 0))
    return kernel_call(
        body,
        (place, *fixed, lhs, *terms),
        [SMEM] + [whole(value.shape) for value in fixed] + [pl.BlockSpec((tall, deep), lambda i: (i, 0))]
        + [chunk(value.shape[1]) for value in terms],
        [jax.ShapeDtypeStruct((channels_in // 4, wide), BF16)] * 4 + extra,
        [chunk(wide)] * 4 + [whole(value.shape) for value in extra],
        (steps,),
        [pltpu.VMEM((deep, columns), BF16), pltpu.VMEM((tall // 128, Y, X, 8, columns), F32)],
        2 * channels_in * deep * columns,
        24,
        light,
    )


def middle_terms(place, even, odd, lhs, col_count):
    cells, width = even.shape

    def body(place_ref, even_ref, odd_ref, lhs_ref, *rest):
        stacked, total = rest[4:]

        @pl.when(pl.program_id(0) == 0)
        def _():
            clear_padding(stacked, cells)
            first = place_ref[2] == 0
            even_block, odd_block = even_ref[...], odd_ref[...]
            fill(stacked, 0, 0, jnp.where(first, even_block, odd_block), col_count)
            fill(stacked, 1, 0, jnp.where(first, odd_block, even_block), col_count)

        def store(steps, chunk):
            rest[steps][...] = chunk

        multiply(place_ref, lhs_ref, stacked, total, store)

    return product_call(body, place, [even, odd], lhs, [], 3 * width, 3 * width, [], True)


def all_terms(place, even, odd, up, down, far, lhs, middle, col_count):
    cells, width = up.shape
    third = 3 * width

    def body(place_ref, even_ref, odd_ref, up_ref, down_ref, far_ref, lhs_ref, *rest):
        middle_refs, out_refs = rest[:4], rest[4:8]
        mine_ref, theirs_ref, stacked, total = rest[8:]

        @pl.when(pl.program_id(0) == 0)
        def _():
            clear_padding(stacked, cells)
            first = place_ref[2] == 0
            early = place_ref[1] < X // 2
            far_block = far_ref[...]
            zero = jnp.zeros_like(far_block)
            far_down = jnp.where(early, far_block, zero)
            far_up = jnp.where(early, zero, far_block)
            down_block = jnp.where(place_ref[1] < X - 1, down_ref[...], zero)
            up_block = jnp.where(place_ref[1] > 0, up_ref[...], zero)
            pairs = ((down_block, far_down), (even_ref[...], odd_ref[...]), (far_up, up_block))
            for side, (lower, upper) in enumerate(pairs):
                mine = jnp.where(first, lower, upper)
                theirs = jnp.where(first, upper, lower)
                mine_ref[side] = mine
                theirs_ref[side] = theirs
                if side != 1:
                    fill(stacked, 0, 3 * (side // 2), mine, col_count)
                    fill(stacked, 1, 3 * (side // 2), theirs, col_count)

        def store(steps, chunk):
            out_refs[steps][:, :third] = chunk[:, :third]
            out_refs[steps][:, third : 2 * third] = middle_refs[steps][...]
            out_refs[steps][:, 2 * third :] = chunk[:, third:]

        multiply(place_ref, lhs_ref, stacked, total, store)

    triple = jax.ShapeDtypeStruct((3, cells, width), BF16)
    return product_call(
        body, place, [even, odd, up, down, far], lhs, middle, 2 * third, 3 * third, [triple, triple]
    )


def first_sum(terms):
    rows, columns = terms[0].shape

    def body(*refs):
        refs[-1][...] = sum(ref[...].astype(F32) for ref in refs[:-1]).astype(BF16)

    steps = 2
    spec = pl.BlockSpec((rows // steps, columns), lambda i: (i, 0))
    return kernel_call(
        body, terms, [spec] * 4, [jax.ShapeDtypeStruct((rows, columns), BF16)], [spec], (steps,)
    )[0]


def input_gradient(place, held, got, weight, col_count):
    _, cells, half = held.shape
    deep, channels_in = weight.shape
    width = 256

    def body(place_ref, held_ref, got_ref, weight_ref, out_ref, stacked):
        @pl.when(pl.program_id(0) == 0)
        def _():
            first = place_ref[2] == 0
            for side in range(3):
                mine, theirs = held_ref[side], got_ref[side]
                lower, upper = jnp.where(first, mine, theirs), jnp.where(first, theirs, mine)
                for part, block in enumerate((lower, upper)):
                    for spot, tap in enumerate(column_taps(block, col_count)):
                        start = (2 * (3 * side + spot) + part) * half
                        stacked[:, start : start + half] = tap

        out_ref[...] = jnp.dot(
            stacked[...], weight_ref[...], preferred_element_type=F32
        ).astype(BF16)

    return kernel_call(
        body,
        (place, held, got, weight),
        [SMEM, whole(held.shape), whole(got.shape), pl.BlockSpec((deep, width), lambda i: (0, i))],
        [jax.ShapeDtypeStruct((cells, channels_in), BF16)],
        [pl.BlockSpec((cells, width), lambda i: (0, i))],
        (channels_in // width,),
        [pltpu.VMEM((cells, deep), BF16)],
        2 * cells * deep * channels_in,
        24,
    )[0]


def per_device(inputs, conv_out, grad_out, relu_mask, norm_gain, weight):
    image_count, row_count, col_count, channels_in = inputs.shape
    channels_out = conv_out.shape[3]
    cell_count = row_count * col_count * X * CORES
    cells = image_count * row_count * col_count
    half = channels_out // 2
    core = lax.axis_index("core")
    place = jnp.stack([lax.axis_index("y"), lax.axis_index("x"), core]).astype(jnp.int32)

    input_flat = inputs.reshape(cells, channels_in)
    sums = channel_sums(conv_out, grad_out, relu_mask)
    got_sums = swapped(sums)
    mine, sent = prepare(
        place,
        *(value.reshape(cells, channels_out) for value in (conv_out, grad_out, relu_mask)),
    )
    input_flat, sent, got_sums = lax.optimization_barrier((input_flat, sent, got_sums))
    theirs = swapped(sent)
    input_other = swapped(input_flat)
    sums = sums + got_sums
    sums = [sums] + [around(sums, steps) for steps in (2, 1, 3)]
    lhs = transposed(input_flat, input_other)
    gain = norm_gain.reshape(1, channels_out)
    even, odd, far = pre_gradient(place, gain, sums, mine, theirs, image_count, cell_count)
    far = around(far, 2)
    up = around(even, 1)
    down = around(odd, X - 1)

    middle = middle_terms(place, even, odd, lhs, col_count)
    *terms, held, sent = all_terms(place, even, odd, up, down, far, lhs, middle, col_count)
    terms = [terms[0]] + [crossed(terms[steps], steps) for steps in (2, 1, 3)]
    weight, held = lax.optimization_barrier((weight, held))
    weight = jnp.transpose(weight, (1, 2, 0)).reshape(9 * channels_out, channels_in)
    got = swapped(sent)
    terms, weight, got = lax.optimization_barrier((terms, weight, got))
    merged = first_sum(terms)
    held, merged = lax.optimization_barrier((held, merged))
    input_grad = input_gradient(place, held, got, weight, col_count)
    merged = exchanged(merged.reshape(Z * 4, 8, 9 * half))
    merged, input_grad = lax.optimization_barrier((merged, input_grad))
    inv_images = 1.0 / (image_count * Z * Y)
    merged = jnp.sum(merged.astype(F32), axis=0) * inv_images
    rows = merged.shape[0] // CORES
    kept = lax.dynamic_slice_in_dim(merged, core * rows, rows, axis=0)
    came = swapped(lax.dynamic_slice_in_dim(merged, (1 - core) * rows, rows, axis=0))
    kept, came = kept.reshape(rows, 9, half), came.reshape(rows, 9, half)
    weight_grad = jnp.concatenate(
        [jnp.where(core == 0, kept, came), jnp.where(core == 0, came, kept)], axis=2
    )

    return (input_grad.reshape(inputs.shape), weight_grad)


def solution(mesh):
    parted = Mesh(mesh.devices.reshape(Z, Y, X, CORES), AXES)
    cells = P(("z", "y"), ("x", "core"), None, None)
    return jax.shard_map(
        per_device,
        mesh=parted,
        in_specs=(cells, cells, cells, cells, P(), P()),
        out_specs=(cells, P(AXES, None, None)),
        check_vma=False,
    )
```

```python
import jax
import jax.numpy as jnp
from jax import lax
from jax.experimental import pallas as pl
from jax.experimental.pallas import tpu as pltpu
from jax.sharding import Mesh, PartitionSpec as P

RATE = 18
EPSILON = 1e-05
F32 = jnp.float32
BF16 = jnp.bfloat16
MIB = 1024 * 1024
AXES = ("z", "y", "x", "core")
Z, Y, X, CORES = 8, 4, 4, 2
SMEM = pl.BlockSpec(memory_space=pltpu.SMEM)


def device(z, y, x, core):
    return ((z * Y + y) * X + x) * CORES + core


def core_of(place_ref):
    return lax.rem(place_ref[0], CORES)


def x_of(place_ref):
    return lax.rem(lax.div(place_ref[0], CORES), X)


def y_of(place_ref):
    return lax.rem(lax.div(place_ref[0], CORES * X), Y)


def swapped(value):
    return lax.ppermute(value, "core", [(0, 1), (1, 0)])


def around(value, steps):
    return lax.ppermute(value, "x", [(source, (source + steps) % X) for source in range(X)])


def crossed(value, steps):
    pairs = []
    for z in range(Z):
        for y in range(Y):
            for x in range(X):
                pairs.append((device(z, y, x, 0), device(z, (y + steps) % Y, x, 0)))
                pairs.append((device(z, y, x, 1), device(z, y, (x + steps) % X, 1)))
    return lax.ppermute(value, AXES, pairs)


def exchanged(value):
    groups = [[device(z, y, x, 0) for z in range(Z) for x in range(X)] for y in range(Y)]
    groups += [[device(z, y, x, 1) for z in range(Z) for y in range(Y)] for x in range(X)]
    return lax.all_to_all(value, AXES, 0, 0, axis_index_groups=groups)


def whole(shape):
    return pl.BlockSpec(shape, lambda *_: (0,) * len(shape))


def kernel_call(body, operands, in_specs, out_shape, out_specs, grid=(1,), scratch=(), flops=0, vmem=8):
    moved = sum(value.size * value.dtype.itemsize for value in operands)
    moved += sum(value.size * value.dtype.itemsize for value in out_shape)
    return pl.pallas_call(
        body,
        grid=grid,
        in_specs=in_specs,
        out_specs=out_specs,
        out_shape=out_shape,
        scratch_shapes=list(scratch),
        compiler_params=pltpu.CompilerParams(vmem_limit_bytes=vmem * MIB),
        cost_estimate=pl.CostEstimate(flops=flops, bytes_accessed=moved, transcendentals=0),
    )(*operands)


def channel_sums(conv, grad, mask):
    values = conv.astype(F32)
    passed = grad.astype(F32) * mask.astype(F32)
    terms = (values, values * values, passed, passed * values)
    return jnp.stack([jnp.sum(term, axis=(1, 2)) for term in terms]).reshape(-1, conv.shape[3])


def prepare(place, conv, grad, mask):
    cells, channels = conv.shape
    half = channels // 2
    steps = 2
    tall = cells // steps

    def body(place_ref, conv_ref, grad_ref, mask_ref, mine_ref, sent_ref):
        first = core_of(place_ref) == 0
        passed = (grad_ref[...].astype(F32) * mask_ref[...].astype(F32)).astype(BF16)
        for which, value in enumerate((conv_ref[...], passed)):
            lower, upper = value[:, :half], value[:, half:]
            mine_ref[which] = jnp.where(first, lower, upper)
            sent_ref[which] = jnp.where(first, upper, lower)

    rows = pl.BlockSpec((tall, channels), lambda i: (i, 0))
    out = jax.ShapeDtypeStruct((2, cells, half), BF16)
    spec = pl.BlockSpec((2, tall, half), lambda i: (0, i, 0))
    return kernel_call(
        body,
        (place, conv, grad, mask),
        [SMEM, rows, rows, rows],
        [out, out],
        [spec, spec],
        (steps,),
        vmem=60,
    )


def pre_gradient(place, gain, sums, mine, theirs, images, cell_count):
    _, cells, half = mine.shape
    each = cells // images

    def body(place_ref, gain_ref, a_ref, b_ref, c_ref, d_ref, mine_ref, theirs_ref, even_ref, odd_ref, far_ref):
        first = core_of(place_ref) == 0
        early = x_of(place_ref) < X // 2
        means = (a_ref[...] + b_ref[...] + c_ref[...] + d_ref[...]) / cell_count
        means = jnp.where(first, means[:, :half], means[:, half:])
        gain_row = jnp.where(first, gain_ref[:, :half], gain_ref[:, half:])
        for image in range(images):
            rows = pl.ds(image * each, each)
            chan_mean, second, passed_mean, product_mean = (
                means[kind * images + image : kind * images + image + 1] for kind in range(4)
            )
            inv_std = 1.0 / jnp.sqrt(second - chan_mean * chan_mean + EPSILON)
            grad_mean = gain_row * passed_mean
            cross_mean = gain_row * (product_mean - chan_mean * passed_mean) * inv_std
            blocks = []
            for ref in (mine_ref, theirs_ref):
                values, passed = ref[0, rows, :].astype(F32), ref[1, rows, :].astype(F32)
                normed = (values - chan_mean) * inv_std
                blocks.append(inv_std * (gain_row * passed - grad_mean - normed * cross_mean))
            even = jnp.where(first, blocks[0], blocks[1])
            odd = jnp.where(first, blocks[1], blocks[0])
            even_ref[rows, :] = even.astype(BF16)
            odd_ref[rows, :] = odd.astype(BF16)
            far_ref[rows, :] = jnp.where(early, odd, even).astype(BF16)

    out = jax.ShapeDtypeStruct((cells, half), BF16)
    return kernel_call(
        body,
        (place, gain, *sums, mine, theirs),
        [SMEM, whole(gain.shape)] + [whole(sums[0].shape)] * 4 + [whole(mine.shape)] * 2,
        [out] * 3,
        [whole(out.shape)] * 3,
    )


def padded_count(cells):
    return -(-cells // 128) * 128


def transposed(own, other):
    cells, channels = own.shape
    deep = padded_count(cells)
    width = 256

    def body(own_ref, other_ref, out_ref):
        for which, ref in enumerate((own_ref, other_ref)):
            block = jnp.concatenate([ref[...], jnp.zeros((deep - cells, width), BF16)], axis=0)
            out_ref[:, which * deep : (which + 1) * deep] = block.T

    spec = pl.BlockSpec((cells, width), lambda i: (0, i))
    return kernel_call(
        body,
        (own, other),
        [spec, spec],
        [jax.ShapeDtypeStruct((channels, 2 * deep), BF16)],
        [pl.BlockSpec((width, 2 * deep), lambda i: (i, 0))],
        (channels // width,),
    )[0]


def column_taps(block, col_count):
    cells, channels = block.shape
    wide = block.astype(F32)
    column = lax.broadcasted_iota(jnp.int32, (cells // col_count, col_count, channels), 1)
    column = column.reshape(cells, channels)
    before = jnp.where(column < col_count - RATE, pltpu.roll(wide, cells - RATE, 0), 0.0)
    after = jnp.where(column >= RATE, pltpu.roll(wide, RATE, 0), 0.0)
    return before.astype(BF16), block, after.astype(BF16)


def fill(stacked, slot, place, block, col_count):
    cells, width = block.shape
    deep = padded_count(cells)
    for spot, tap in enumerate(column_taps(block, col_count)):
        columns = slice((place + spot) * width, (place + spot + 1) * width)
        stacked[slot * deep : slot * deep + cells, columns] = tap


def clear_padding(stacked, cells):
    deep, columns = stacked.shape
    block = deep // 2
    for slot in range(2):
        stacked[slot * block + cells : (slot + 1) * block, :] = jnp.zeros((block - cells, columns), BF16)


def multiply(place_ref, lhs_ref, stacked, total, out_refs):
    columns = stacked.shape[1]
    product = jnp.dot(lhs_ref[...], stacked[...], preferred_element_type=F32)
    total[...] = product.reshape(total.shape)
    tall = total.shape[0] * 32

    @pl.when(core_of(place_ref) == 0)
    def _():
        for steps in range(Y):
            chunk = total[:, lax.rem(y_of(place_ref) + steps, Y), :, :, :]
            out_refs[steps][...] = chunk.reshape(tall, columns).astype(BF16)

    @pl.when(core_of(place_ref) != 0)
    def _():
        for steps in range(X):
            chunk = total[:, :, lax.rem(x_of(place_ref) + steps, X), :, :]
            out_refs[steps][...] = chunk.reshape(tall, columns).astype(BF16)


def product_call(body, place, fixed, lhs, columns, extra):
    channels_in, deep = lhs.shape
    steps = 2
    tall = channels_in // steps
    return kernel_call(
        body,
        (place, *fixed, lhs),
        [SMEM] + [whole(value.shape) for value in fixed] + [pl.BlockSpec((tall, deep), lambda i: (i, 0))],
        [jax.ShapeDtypeStruct((channels_in // 4, columns), BF16)] * 4 + extra,
        [pl.BlockSpec((tall // 4, columns), lambda i: (i, 0))] * 4 + [whole(value.shape) for value in extra],
        (steps,),
        [pltpu.VMEM((deep, columns), BF16), pltpu.VMEM((tall // 128, Y, X, 8, columns), F32)],
        flops=2 * channels_in * deep * columns,
        vmem=24,
    )


def middle_terms(place, even, odd, lhs, col_count):
    cells, width = even.shape

    def body(place_ref, even_ref, odd_ref, lhs_ref, *rest):
        stacked, total = rest[4:]

        @pl.when(pl.program_id(0) == 0)
        def _():
            clear_padding(stacked, cells)
            first = core_of(place_ref) == 0
            even_block, odd_block = even_ref[...], odd_ref[...]
            fill(stacked, 0, 0, jnp.where(first, even_block, odd_block), col_count)
            fill(stacked, 1, 0, jnp.where(first, odd_block, even_block), col_count)

        multiply(place_ref, lhs_ref, stacked, total, rest[:4])

    return product_call(body, place, [even, odd], lhs, 3 * width, [])


def side_terms(place, even, odd, up, down, far, lhs, col_count):
    cells, width = up.shape

    def body(place_ref, even_ref, odd_ref, up_ref, down_ref, far_ref, lhs_ref, *rest):
        mine_ref, theirs_ref, stacked, total = rest[4:]

        @pl.when(pl.program_id(0) == 0)
        def _():
            clear_padding(stacked, cells)
            first = core_of(place_ref) == 0
            early = x_of(place_ref) < X // 2
            far_block = far_ref[...]
            zero = jnp.zeros_like(far_block)
            far_down = jnp.where(early, far_block, zero)
            far_up = jnp.where(early, zero, far_block)
            down_block = jnp.where(x_of(place_ref) < X - 1, down_ref[...], zero)
            up_block = jnp.where(x_of(place_ref) > 0, up_ref[...], zero)
            pairs = ((down_block, far_down), (even_ref[...], odd_ref[...]), (far_up, up_block))
            for side, (lower, upper) in enumerate(pairs):
                mine = jnp.where(first, lower, upper)
                theirs = jnp.where(first, upper, lower)
                mine_ref[side] = mine
                theirs_ref[side] = theirs
                if side != 1:
                    fill(stacked, 0, 3 * (side // 2), mine, col_count)
                    fill(stacked, 1, 3 * (side // 2), theirs, col_count)

        multiply(place_ref, lhs_ref, stacked, total, rest[:4])

    triple = jax.ShapeDtypeStruct((3, cells, width), BF16)
    return product_call(body, place, [even, odd, up, down, far], lhs, 6 * width, [triple, triple])


def first_sum(middle, sides):
    rows, third = middle[0].shape

    def body(*refs):
        out_ref = refs[-1]
        middle_total = sum(ref[...].astype(F32) for ref in refs[:4])
        side_total = sum(ref[...].astype(F32) for ref in refs[4:8])
        out_ref[:, :third] = side_total[:, :third].astype(BF16)
        out_ref[:, third : 2 * third] = middle_total.astype(BF16)
        out_ref[:, 2 * third :] = side_total[:, third:].astype(BF16)

    steps = 2
    spec = lambda columns: pl.BlockSpec((rows // steps, columns), lambda i: (i, 0))
    return kernel_call(
        body,
        (*middle, *sides),
        [spec(third)] * 4 + [spec(2 * third)] * 4,
        [jax.ShapeDtypeStruct((rows, 3 * third), BF16)],
        [spec(3 * third)],
        (steps,),
    )[0]


def input_gradient(place, held, got, weight, col_count):
    _, cells, half = held.shape
    deep, channels_in = weight.shape
    width = 256

    def body(place_ref, held_ref, got_ref, weight_ref, out_ref, stacked):
        @pl.when(pl.program_id(0) == 0)
        def _():
            first = core_of(place_ref) == 0
            for side in range(3):
                mine, theirs = held_ref[side], got_ref[side]
                lower, upper = jnp.where(first, mine, theirs), jnp.where(first, theirs, mine)
                for part, block in enumerate((lower, upper)):
                    for spot, tap in enumerate(column_taps(block, col_count)):
                        start = (2 * (3 * side + spot) + part) * half
                        stacked[:, start : start + half] = tap

        out_ref[...] = jnp.dot(
            stacked[...], weight_ref[...], preferred_element_type=F32
        ).astype(BF16)

    return kernel_call(
        body,
        (place, held, got, weight),
        [SMEM, whole(held.shape), whole(got.shape), pl.BlockSpec((deep, width), lambda i: (0, i))],
        [jax.ShapeDtypeStruct((cells, channels_in), BF16)],
        [pl.BlockSpec((cells, width), lambda i: (0, i))],
        (channels_in // width,),
        [pltpu.VMEM((cells, deep), BF16)],
        2 * cells * deep * channels_in,
        24,
    )[0]


def per_device(inputs, conv_out, grad_out, relu_mask, norm_gain, weight):
    image_count, row_count, col_count, channels_in = inputs.shape
    channels_out = conv_out.shape[3]
    cell_count = row_count * col_count * X * CORES
    cells = image_count * row_count * col_count
    half = channels_out // 2
    core = lax.axis_index("core")
    place = jnp.reshape(lax.axis_index(AXES), (1,)).astype(jnp.int32)

    input_flat = inputs.reshape(cells, channels_in)
    sums = channel_sums(conv_out, grad_out, relu_mask)
    got_sums = swapped(sums)
    mine, sent = prepare(
        place,
        *(value.reshape(cells, channels_out) for value in (conv_out, grad_out, relu_mask)),
    )
    input_flat, sent, got_sums = lax.optimization_barrier((input_flat, sent, got_sums))
    theirs = swapped(sent)
    input_other = swapped(input_flat)
    sums = sums + got_sums
    sums = [sums] + [around(sums, steps) for steps in (2, 1, 3)]
    lhs = transposed(input_flat, input_other)
    gain = norm_gain.reshape(1, channels_out)
    even, odd, far = pre_gradient(place, gain, sums, mine, theirs, image_count, cell_count)
    far = around(far, 2)
    up = around(even, 1)
    down = around(odd, X - 1)

    middle = middle_terms(place, even, odd, lhs, col_count)
    middle = [middle[0]] + [crossed(middle[steps], steps) for steps in (2, 1, 3)]
    lhs, middle[1], middle[2] = lax.optimization_barrier((lhs, middle[1], middle[2]))
    *sides, held, sent = side_terms(place, even, odd, up, down, far, lhs, col_count)
    sides = [sides[0]] + [crossed(sides[steps], steps) for steps in (2, 1, 3)]

    weight, held = lax.optimization_barrier((weight, held))
    weight = jnp.transpose(weight, (1, 2, 0)).reshape(9 * channels_out, channels_in)
    sides, weight = lax.optimization_barrier((sides, weight))
    merged = first_sum(middle, sides)
    got = swapped(sent)
    held, merged = lax.optimization_barrier((held, merged))
    input_grad = input_gradient(place, held, got, weight, col_count)
    merged = exchanged(merged.reshape(Z * 4, 8, 9 * half))
    merged, input_grad = lax.optimization_barrier((merged, input_grad))
    inv_images = 1.0 / (image_count * Z * Y)
    merged = jnp.sum(merged.astype(F32), axis=0) * inv_images
    rows = merged.shape[0] // CORES
    kept = lax.dynamic_slice_in_dim(merged, core * rows, rows, axis=0)
    came = swapped(lax.dynamic_slice_in_dim(merged, (1 - core) * rows, rows, axis=0))
    kept, came = kept.reshape(rows, 9, half), came.reshape(rows, 9, half)
    weight_grad = jnp.concatenate(
        [jnp.where(core == 0, kept, came), jnp.where(core == 0, came, kept)], axis=2
    )

    return (input_grad.reshape(inputs.shape), weight_grad)


def solution(mesh):
    parted = Mesh(mesh.devices.reshape(Z, Y, X, CORES), AXES)
    cells = P(("z", "y"), ("x", "core"), None, None)
    return jax.shard_map(
        per_device,
        mesh=parted,
        in_specs=(cells, cells, cells, cells, P(), P()),
        out_specs=(cells, P(AXES, None, None)),
        check_vma=False,
    )
```

```python
import jax
import jax.numpy as jnp
from jax import lax
from jax.experimental import pallas as pl
from jax.experimental.pallas import tpu as pltpu
from jax.sharding import Mesh, PartitionSpec as P

RATE = 18
EPSILON = 1e-05
F32 = jnp.float32
BF16 = jnp.bfloat16
MIB = 1024 * 1024
AXES = ("z", "y", "x", "core")
Z, Y, X, CORES = 8, 4, 4, 2
SMEM = pl.BlockSpec(memory_space=pltpu.SMEM)


def device(z, y, x, core):
    return ((z * Y + y) * X + x) * CORES + core


def core_of(place_ref):
    return lax.rem(place_ref[0], CORES)


def x_of(place_ref):
    return lax.rem(lax.div(place_ref[0], CORES), X)


def y_of(place_ref):
    return lax.rem(lax.div(place_ref[0], CORES * X), Y)


def swapped(value):
    return lax.ppermute(value, "core", [(0, 1), (1, 0)])


def around(value, steps):
    return lax.ppermute(value, "x", [(source, (source + steps) % X) for source in range(X)])


def crossed(value, steps):
    pairs = []
    for z in range(Z):
        for y in range(Y):
            for x in range(X):
                pairs.append((device(z, y, x, 0), device(z, (y + steps) % Y, x, 0)))
                pairs.append((device(z, y, x, 1), device(z, y, (x + steps) % X, 1)))
    return lax.ppermute(value, AXES, pairs)


def exchanged(value):
    groups = [[device(z, y, x, 0) for z in range(Z) for x in range(X)] for y in range(Y)]
    groups += [[device(z, y, x, 1) for z in range(Z) for y in range(Y)] for x in range(X)]
    return lax.all_to_all(value, AXES, 0, 0, axis_index_groups=groups)


def whole(shape):
    return pl.BlockSpec(shape, lambda *_: (0,) * len(shape))


def kernel_call(body, operands, in_specs, out_shape, out_specs, grid=(1,), scratch=(), flops=0, vmem=8):
    moved = sum(value.size * value.dtype.itemsize for value in operands)
    moved += sum(value.size * value.dtype.itemsize for value in out_shape)
    return pl.pallas_call(
        body,
        grid=grid,
        in_specs=in_specs,
        out_specs=out_specs,
        out_shape=out_shape,
        scratch_shapes=list(scratch),
        compiler_params=pltpu.CompilerParams(vmem_limit_bytes=vmem * MIB),
        cost_estimate=pl.CostEstimate(flops=flops, bytes_accessed=moved, transcendentals=0),
    )(*operands)


def channel_sums(conv, grad, mask):
    values = conv.astype(F32)
    passed = grad.astype(F32) * mask.astype(F32)
    terms = (values, values * values, passed, passed * values)
    return jnp.stack([jnp.sum(term, axis=(1, 2)) for term in terms]).reshape(-1, conv.shape[3])


def prepare(place, conv, grad, mask):
    cells, channels = conv.shape
    half = channels // 2
    steps = 2
    tall = cells // steps

    def body(place_ref, conv_ref, grad_ref, mask_ref, mine_ref, sent_ref):
        first = core_of(place_ref) == 0
        passed = (grad_ref[...].astype(F32) * mask_ref[...].astype(F32)).astype(BF16)
        for which, value in enumerate((conv_ref[...], passed)):
            lower, upper = value[:, :half], value[:, half:]
            mine_ref[which] = jnp.where(first, lower, upper)
            sent_ref[which] = jnp.where(first, upper, lower)

    rows = pl.BlockSpec((tall, channels), lambda i: (i, 0))
    out = jax.ShapeDtypeStruct((2, cells, half), BF16)
    spec = pl.BlockSpec((2, tall, half), lambda i: (0, i, 0))
    return kernel_call(
        body,
        (place, conv, grad, mask),
        [SMEM, rows, rows, rows],
        [out, out],
        [spec, spec],
        (steps,),
        vmem=60,
    )


def pre_gradient(place, gain, sums, mine, theirs, images, cell_count):
    _, cells, half = mine.shape
    each = cells // images

    def body(place_ref, gain_ref, a_ref, b_ref, c_ref, d_ref, mine_ref, theirs_ref, even_ref, odd_ref, far_ref):
        first = core_of(place_ref) == 0
        early = x_of(place_ref) < X // 2
        means = (a_ref[...] + b_ref[...] + c_ref[...] + d_ref[...]) / cell_count
        means = jnp.where(first, means[:, :half], means[:, half:])
        gain_row = jnp.where(first, gain_ref[:, :half], gain_ref[:, half:])
        for image in range(images):
            rows = pl.ds(image * each, each)
            chan_mean, second, passed_mean, product_mean = (
                means[kind * images + image : kind * images + image + 1] for kind in range(4)
            )
            inv_std = 1.0 / jnp.sqrt(second - chan_mean * chan_mean + EPSILON)
            grad_mean = gain_row * passed_mean
            cross_mean = gain_row * (product_mean - chan_mean * passed_mean) * inv_std
            blocks = []
            for ref in (mine_ref, theirs_ref):
                values, passed = ref[0, rows, :].astype(F32), ref[1, rows, :].astype(F32)
                normed = (values - chan_mean) * inv_std
                blocks.append(inv_std * (gain_row * passed - grad_mean - normed * cross_mean))
            even = jnp.where(first, blocks[0], blocks[1])
            odd = jnp.where(first, blocks[1], blocks[0])
            even_ref[rows, :] = even.astype(BF16)
            odd_ref[rows, :] = odd.astype(BF16)
            far_ref[rows, :] = jnp.where(early, odd, even).astype(BF16)

    out = jax.ShapeDtypeStruct((cells, half), BF16)
    return kernel_call(
        body,
        (place, gain, *sums, mine, theirs),
        [SMEM, whole(gain.shape)] + [whole(sums[0].shape)] * 4 + [whole(mine.shape)] * 2,
        [out] * 3,
        [whole(out.shape)] * 3,
    )


def padded_count(cells):
    return -(-cells // 128) * 128


def transposed(own, other):
    cells, channels = own.shape
    deep = padded_count(cells)
    width = 256

    def body(own_ref, other_ref, out_ref):
        for which, ref in enumerate((own_ref, other_ref)):
            block = jnp.concatenate([ref[...], jnp.zeros((deep - cells, width), BF16)], axis=0)
            out_ref[:, which * deep : (which + 1) * deep] = block.T

    spec = pl.BlockSpec((cells, width), lambda i: (0, i))
    return kernel_call(
        body,
        (own, other),
        [spec, spec],
        [jax.ShapeDtypeStruct((channels, 2 * deep), BF16)],
        [pl.BlockSpec((width, 2 * deep), lambda i: (i, 0))],
        (channels // width,),
    )[0]


def column_taps(block, col_count):
    cells, channels = block.shape
    wide = block.astype(F32)
    column = lax.broadcasted_iota(jnp.int32, (cells // col_count, col_count, channels), 1)
    column = column.reshape(cells, channels)
    before = jnp.where(column < col_count - RATE, pltpu.roll(wide, cells - RATE, 0), 0.0)
    after = jnp.where(column >= RATE, pltpu.roll(wide, RATE, 0), 0.0)
    return before.astype(BF16), block, after.astype(BF16)


def fill(stacked, slot, place, block, col_count):
    cells, width = block.shape
    deep = padded_count(cells)
    for spot, tap in enumerate(column_taps(block, col_count)):
        columns = slice((place + spot) * width, (place + spot + 1) * width)
        stacked[slot * deep : slot * deep + cells, columns] = tap


def clear_padding(stacked, cells):
    deep, columns = stacked.shape
    block = deep // 2
    for slot in range(2):
        stacked[slot * block + cells : (slot + 1) * block, :] = jnp.zeros((block - cells, columns), BF16)


def multiply(place_ref, lhs_ref, stacked, total, out_refs):
    columns = stacked.shape[1]
    product = jnp.dot(lhs_ref[...], stacked[...], preferred_element_type=F32)
    total[...] = product.reshape(total.shape)
    tall = total.shape[0] * 32

    @pl.when(core_of(place_ref) == 0)
    def _():
        for steps in range(Y):
            chunk = total[:, lax.rem(y_of(place_ref) + steps, Y), :, :, :]
            out_refs[steps][...] = chunk.reshape(tall, columns).astype(BF16)

    @pl.when(core_of(place_ref) != 0)
    def _():
        for steps in range(X):
            chunk = total[:, :, lax.rem(x_of(place_ref) + steps, X), :, :]
            out_refs[steps][...] = chunk.reshape(tall, columns).astype(BF16)


def product_call(body, place, fixed, lhs, columns, extra):
    channels_in, deep = lhs.shape
    steps = 2
    tall = channels_in // steps
    return kernel_call(
        body,
        (place, *fixed, lhs),
        [SMEM] + [whole(value.shape) for value in fixed] + [pl.BlockSpec((tall, deep), lambda i: (i, 0))],
        [jax.ShapeDtypeStruct((channels_in // 4, columns), BF16)] * 4 + extra,
        [pl.BlockSpec((tall // 4, columns), lambda i: (i, 0))] * 4 + [whole(value.shape) for value in extra],
        (steps,),
        [pltpu.VMEM((deep, columns), BF16), pltpu.VMEM((tall // 128, Y, X, 8, columns), F32)],
        flops=2 * channels_in * deep * columns,
        vmem=24,
    )


def middle_terms(place, even, odd, lhs, col_count):
    cells, width = even.shape

    def body(place_ref, even_ref, odd_ref, lhs_ref, *rest):
        stacked, total = rest[4:]

        @pl.when(pl.program_id(0) == 0)
        def _():
            clear_padding(stacked, cells)
            first = core_of(place_ref) == 0
            even_block, odd_block = even_ref[...], odd_ref[...]
            fill(stacked, 0, 0, jnp.where(first, even_block, odd_block), col_count)
            fill(stacked, 1, 0, jnp.where(first, odd_block, even_block), col_count)

        multiply(place_ref, lhs_ref, stacked, total, rest[:4])

    return product_call(body, place, [even, odd], lhs, 3 * width, [])


def side_terms(place, even, odd, up, down, far, lhs, col_count):
    cells, width = up.shape

    def body(place_ref, even_ref, odd_ref, up_ref, down_ref, far_ref, lhs_ref, *rest):
        mine_ref, theirs_ref, stacked, total = rest[4:]

        @pl.when(pl.program_id(0) == 0)
        def _():
            clear_padding(stacked, cells)
            first = core_of(place_ref) == 0
            early = x_of(place_ref) < X // 2
            far_block = far_ref[...]
            zero = jnp.zeros_like(far_block)
            far_down = jnp.where(early, far_block, zero)
            far_up = jnp.where(early, zero, far_block)
            down_block = jnp.where(x_of(place_ref) < X - 1, down_ref[...], zero)
            up_block = jnp.where(x_of(place_ref) > 0, up_ref[...], zero)
            pairs = ((down_block, far_down), (even_ref[...], odd_ref[...]), (far_up, up_block))
            for side, (lower, upper) in enumerate(pairs):
                mine = jnp.where(first, lower, upper)
                theirs = jnp.where(first, upper, lower)
                mine_ref[side] = mine
                theirs_ref[side] = theirs
                if side != 1:
                    fill(stacked, 0, 3 * (side // 2), mine, col_count)
                    fill(stacked, 1, 3 * (side // 2), theirs, col_count)

        multiply(place_ref, lhs_ref, stacked, total, rest[:4])

    triple = jax.ShapeDtypeStruct((3, cells, width), BF16)
    return product_call(body, place, [even, odd, up, down, far], lhs, 6 * width, [triple, triple])


def first_sum(middle, sides):
    rows, third = middle[0].shape

    def body(*refs):
        out_ref = refs[-1]
        middle_total = sum(ref[...].astype(F32) for ref in refs[:4])
        side_total = sum(ref[...].astype(F32) for ref in refs[4:8])
        out_ref[:, :third] = side_total[:, :third].astype(BF16)
        out_ref[:, third : 2 * third] = middle_total.astype(BF16)
        out_ref[:, 2 * third :] = side_total[:, third:].astype(BF16)

    steps = 2
    spec = lambda columns: pl.BlockSpec((rows // steps, columns), lambda i: (i, 0))
    return kernel_call(
        body,
        (*middle, *sides),
        [spec(third)] * 4 + [spec(2 * third)] * 4,
        [jax.ShapeDtypeStruct((rows, 3 * third), BF16)],
        [spec(3 * third)],
        (steps,),
    )[0]


def input_gradient(place, held, got, weight, col_count):
    _, cells, half = held.shape
    deep, channels_in = weight.shape
    width = 256

    def body(place_ref, held_ref, got_ref, weight_ref, out_ref, stacked):
        @pl.when(pl.program_id(0) == 0)
        def _():
            first = core_of(place_ref) == 0
            for side in range(3):
                mine, theirs = held_ref[side], got_ref[side]
                lower, upper = jnp.where(first, mine, theirs), jnp.where(first, theirs, mine)
                for part, block in enumerate((lower, upper)):
                    for spot, tap in enumerate(column_taps(block, col_count)):
                        start = (2 * (3 * side + spot) + part) * half
                        stacked[:, start : start + half] = tap

        out_ref[...] = jnp.dot(
            stacked[...], weight_ref[...], preferred_element_type=F32
        ).astype(BF16)

    return kernel_call(
        body,
        (place, held, got, weight),
        [SMEM, whole(held.shape), whole(got.shape), pl.BlockSpec((deep, width), lambda i: (0, i))],
        [jax.ShapeDtypeStruct((cells, channels_in), BF16)],
        [pl.BlockSpec((cells, width), lambda i: (0, i))],
        (channels_in // width,),
        [pltpu.VMEM((cells, deep), BF16)],
        2 * cells * deep * channels_in,
        60,
    )[0]


def per_device(inputs, conv_out, grad_out, relu_mask, norm_gain, weight):
    image_count, row_count, col_count, channels_in = inputs.shape
    channels_out = conv_out.shape[3]
    cell_count = row_count * col_count * X * CORES
    cells = image_count * row_count * col_count
    half = channels_out // 2
    core = lax.axis_index("core")
    place = jnp.reshape(lax.axis_index(AXES), (1,)).astype(jnp.int32)

    input_flat = inputs.reshape(cells, channels_in)
    sums = channel_sums(conv_out, grad_out, relu_mask)
    got_sums = swapped(sums)
    mine, sent = prepare(
        place,
        *(value.reshape(cells, channels_out) for value in (conv_out, grad_out, relu_mask)),
    )
    input_flat, sent, got_sums = lax.optimization_barrier((input_flat, sent, got_sums))
    theirs = swapped(sent)
    input_other = swapped(input_flat)
    sums = sums + got_sums
    sums = [sums] + [around(sums, steps) for steps in (2, 1, 3)]
    lhs = transposed(input_flat, input_other)
    gain = norm_gain.reshape(1, channels_out)
    even, odd, far = pre_gradient(place, gain, sums, mine, theirs, image_count, cell_count)
    far = around(far, 2)
    up = around(even, 1)
    down = around(odd, X - 1)

    middle = list(middle_terms(place, even, odd, lhs, col_count))
    weight, middle[0] = lax.optimization_barrier((weight, middle[0]))
    weight = jnp.transpose(weight, (1, 2, 0)).reshape(9 * channels_out, channels_in)
    middle = [middle[0]] + [crossed(middle[steps], steps) for steps in (2, 1, 3)]
    lhs, weight, middle[1], middle[2] = lax.optimization_barrier((lhs, weight, middle[1], middle[2]))
    *sides, held, sent = side_terms(place, even, odd, up, down, far, lhs, col_count)
    sides = [sides[0]] + [crossed(sides[steps], steps) for steps in (2, 1, 3)]
    merged = first_sum(middle, sides)
    got = swapped(sent)
    place, merged = lax.optimization_barrier((place, merged))
    input_grad = input_gradient(place, held, got, weight, col_count)
    merged = exchanged(merged.reshape(Z * 4, 8, 9 * half))
    merged, input_grad = lax.optimization_barrier((merged, input_grad))
    inv_images = 1.0 / (image_count * Z * Y)
    merged = jnp.sum(merged.astype(F32), axis=0) * inv_images
    rows = merged.shape[0] // CORES
    kept = lax.dynamic_slice_in_dim(merged, core * rows, rows, axis=0)
    came = swapped(lax.dynamic_slice_in_dim(merged, (1 - core) * rows, rows, axis=0))
    kept, came = kept.reshape(rows, 9, half), came.reshape(rows, 9, half)
    weight_grad = jnp.concatenate(
        [jnp.where(core == 0, kept, came), jnp.where(core == 0, came, kept)], axis=2
    )

    return (input_grad.reshape(inputs.shape), weight_grad)


def solution(mesh):
    parted = Mesh(mesh.devices.reshape(Z, Y, X, CORES), AXES)
    cells = P(("z", "y"), ("x", "core"), None, None)
    return jax.shard_map(
        per_device,
        mesh=parted,
        in_specs=(cells, cells, cells, cells, P(), P()),
        out_specs=(cells, P(AXES, None, None)),
        check_vma=False,
    )
```

```python
import jax
import jax.numpy as jnp
from jax import lax
from jax.experimental import pallas as pl
from jax.experimental.pallas import tpu as pltpu
from jax.sharding import Mesh, PartitionSpec as P

RATE = 18
EPSILON = 1e-05
F32 = jnp.float32
BF16 = jnp.bfloat16
MIB = 1024 * 1024
AXES = ("z", "y", "x", "core")
Z, Y, X, CORES = 8, 4, 4, 2
SMEM = pl.BlockSpec(memory_space=pltpu.SMEM)


def device(z, y, x, core):
    return ((z * Y + y) * X + x) * CORES + core


def core_of(place_ref):
    return lax.rem(place_ref[0], CORES)


def x_of(place_ref):
    return lax.rem(lax.div(place_ref[0], CORES), X)


def y_of(place_ref):
    return lax.rem(lax.div(place_ref[0], CORES * X), Y)


def swapped(value):
    return lax.ppermute(value, "core", [(0, 1), (1, 0)])


def around(value, steps):
    return lax.ppermute(value, "x", [(source, (source + steps) % X) for source in range(X)])


def crossed(value, steps):
    pairs = []
    for z in range(Z):
        for y in range(Y):
            for x in range(X):
                pairs.append((device(z, y, x, 0), device(z, (y + steps) % Y, x, 0)))
                pairs.append((device(z, y, x, 1), device(z, y, (x + steps) % X, 1)))
    return lax.ppermute(value, AXES, pairs)


def exchanged(value):
    groups = [[device(z, y, x, 0) for z in range(Z) for x in range(X)] for y in range(Y)]
    groups += [[device(z, y, x, 1) for z in range(Z) for y in range(Y)] for x in range(X)]
    return lax.all_to_all(value, AXES, 0, 0, axis_index_groups=groups)


def whole(shape):
    return pl.BlockSpec(shape, lambda *_: (0,) * len(shape))


def kernel_call(body, operands, in_specs, out_shape, out_specs, grid=(1,), scratch=(), flops=0, vmem=8):
    moved = sum(value.size * value.dtype.itemsize for value in operands)
    moved += sum(value.size * value.dtype.itemsize for value in out_shape)
    return pl.pallas_call(
        body,
        grid=grid,
        in_specs=in_specs,
        out_specs=out_specs,
        out_shape=out_shape,
        scratch_shapes=list(scratch),
        compiler_params=pltpu.CompilerParams(vmem_limit_bytes=vmem * MIB),
        cost_estimate=pl.CostEstimate(flops=flops, bytes_accessed=moved, transcendentals=0),
    )(*operands)


def channel_sums(conv, grad, mask):
    values = conv.astype(F32)
    passed = grad.astype(F32) * mask.astype(F32)
    terms = (values, values * values, passed, passed * values)
    return jnp.stack([jnp.sum(term, axis=(1, 2)) for term in terms]).reshape(-1, conv.shape[3])


def prepare(place, conv, grad, mask):
    cells, channels = conv.shape
    half = channels // 2
    steps = 2
    tall = cells // steps

    def body(place_ref, conv_ref, grad_ref, mask_ref, mine_ref, sent_ref):
        first = core_of(place_ref) == 0
        passed = (grad_ref[...].astype(F32) * mask_ref[...].astype(F32)).astype(BF16)
        for which, value in enumerate((conv_ref[...], passed)):
            lower, upper = value[:, :half], value[:, half:]
            mine_ref[which] = jnp.where(first, lower, upper)
            sent_ref[which] = jnp.where(first, upper, lower)

    rows = pl.BlockSpec((tall, channels), lambda i: (i, 0))
    out = jax.ShapeDtypeStruct((2, cells, half), BF16)
    spec = pl.BlockSpec((2, tall, half), lambda i: (0, i, 0))
    return kernel_call(
        body,
        (place, conv, grad, mask),
        [SMEM, rows, rows, rows],
        [out, out],
        [spec, spec],
        (steps,),
        vmem=60,
    )


def pre_gradient(place, gain, sums, mine, theirs, images, cell_count):
    _, cells, half = mine.shape
    each = cells // images

    def body(place_ref, gain_ref, a_ref, b_ref, c_ref, d_ref, mine_ref, theirs_ref, even_ref, odd_ref, far_ref):
        first = core_of(place_ref) == 0
        early = x_of(place_ref) < X // 2
        means = (a_ref[...] + b_ref[...] + c_ref[...] + d_ref[...]) / cell_count
        means = jnp.where(first, means[:, :half], means[:, half:])
        gain_row = jnp.where(first, gain_ref[:, :half], gain_ref[:, half:])
        for image in range(images):
            rows = pl.ds(image * each, each)
            chan_mean, second, passed_mean, product_mean = (
                means[kind * images + image : kind * images + image + 1] for kind in range(4)
            )
            inv_std = 1.0 / jnp.sqrt(second - chan_mean * chan_mean + EPSILON)
            grad_mean = gain_row * passed_mean
            cross_mean = gain_row * (product_mean - chan_mean * passed_mean) * inv_std
            blocks = []
            for ref in (mine_ref, theirs_ref):
                values, passed = ref[0, rows, :].astype(F32), ref[1, rows, :].astype(F32)
                normed = (values - chan_mean) * inv_std
                blocks.append(inv_std * (gain_row * passed - grad_mean - normed * cross_mean))
            even = jnp.where(first, blocks[0], blocks[1])
            odd = jnp.where(first, blocks[1], blocks[0])
            even_ref[rows, :] = even.astype(BF16)
            odd_ref[rows, :] = odd.astype(BF16)
            far_ref[rows, :] = jnp.where(early, odd, even).astype(BF16)

    out = jax.ShapeDtypeStruct((cells, half), BF16)
    return kernel_call(
        body,
        (place, gain, *sums, mine, theirs),
        [SMEM, whole(gain.shape)] + [whole(sums[0].shape)] * 4 + [whole(mine.shape)] * 2,
        [out] * 3,
        [whole(out.shape)] * 3,
    )


def padded_count(cells):
    return -(-cells // 128) * 128


def transposed(own, other):
    cells, channels = own.shape
    deep = padded_count(cells)
    width = 256

    def body(own_ref, other_ref, out_ref):
        for which, ref in enumerate((own_ref, other_ref)):
            block = jnp.concatenate([ref[...], jnp.zeros((deep - cells, width), BF16)], axis=0)
            out_ref[:, which * deep : (which + 1) * deep] = block.T

    spec = pl.BlockSpec((cells, width), lambda i: (0, i))
    return kernel_call(
        body,
        (own, other),
        [spec, spec],
        [jax.ShapeDtypeStruct((channels, 2 * deep), BF16)],
        [pl.BlockSpec((width, 2 * deep), lambda i: (i, 0))],
        (channels // width,),
    )[0]


def column_taps(block, col_count):
    cells, channels = block.shape
    wide = block.astype(F32)
    column = lax.broadcasted_iota(jnp.int32, (cells // col_count, col_count, channels), 1)
    column = column.reshape(cells, channels)
    before = jnp.where(column < col_count - RATE, pltpu.roll(wide, cells - RATE, 0), 0.0)
    after = jnp.where(column >= RATE, pltpu.roll(wide, RATE, 0), 0.0)
    return before.astype(BF16), block, after.astype(BF16)


def fill(stacked, slot, place, block, col_count):
    cells, width = block.shape
    deep = padded_count(cells)
    for spot, tap in enumerate(column_taps(block, col_count)):
        columns = slice((place + spot) * width, (place + spot + 1) * width)
        stacked[slot * deep : slot * deep + cells, columns] = tap


def clear_padding(stacked, cells):
    deep, columns = stacked.shape
    block = deep // 2
    for slot in range(2):
        stacked[slot * block + cells : (slot + 1) * block, :] = jnp.zeros((block - cells, columns), BF16)


def multiply(place_ref, lhs_ref, stacked, total, out_refs):
    columns = stacked.shape[1]
    product = jnp.dot(lhs_ref[...], stacked[...], preferred_element_type=F32)
    total[...] = product.reshape(total.shape)
    tall = total.shape[0] * 32

    @pl.when(core_of(place_ref) == 0)
    def _():
        for steps in range(Y):
            chunk = total[:, lax.rem(y_of(place_ref) + steps, Y), :, :, :]
            out_refs[steps][...] = chunk.reshape(tall, columns).astype(BF16)

    @pl.when(core_of(place_ref) != 0)
    def _():
        for steps in range(X):
            chunk = total[:, :, lax.rem(x_of(place_ref) + steps, X), :, :]
            out_refs[steps][...] = chunk.reshape(tall, columns).astype(BF16)


def product_call(body, place, fixed, lhs, columns, extra):
    channels_in, deep = lhs.shape
    steps = 2
    tall = channels_in // steps
    return kernel_call(
        body,
        (place, *fixed, lhs),
        [SMEM] + [whole(value.shape) for value in fixed] + [pl.BlockSpec((tall, deep), lambda i: (i, 0))],
        [jax.ShapeDtypeStruct((channels_in // 4, columns), BF16)] * 4 + extra,
        [pl.BlockSpec((tall // 4, columns), lambda i: (i, 0))] * 4 + [whole(value.shape) for value in extra],
        (steps,),
        [pltpu.VMEM((deep, columns), BF16), pltpu.VMEM((tall // 128, Y, X, 8, columns), F32)],
        flops=2 * channels_in * deep * columns,
        vmem=24,
    )


def middle_terms(place, even, odd, lhs, col_count):
    cells, width = even.shape

    def body(place_ref, even_ref, odd_ref, lhs_ref, *rest):
        stacked, total = rest[4:]

        @pl.when(pl.program_id(0) == 0)
        def _():
            clear_padding(stacked, cells)
            first = core_of(place_ref) == 0
            even_block, odd_block = even_ref[...], odd_ref[...]
            fill(stacked, 0, 0, jnp.where(first, even_block, odd_block), col_count)
            fill(stacked, 1, 0, jnp.where(first, odd_block, even_block), col_count)

        multiply(place_ref, lhs_ref, stacked, total, rest[:4])

    return product_call(body, place, [even, odd], lhs, 3 * width, [])


def side_terms(place, even, odd, up, down, far, lhs, col_count):
    cells, width = up.shape

    def body(place_ref, even_ref, odd_ref, up_ref, down_ref, far_ref, lhs_ref, *rest):
        mine_ref, theirs_ref, stacked, total = rest[4:]

        @pl.when(pl.program_id(0) == 0)
        def _():
            clear_padding(stacked, cells)
            first = core_of(place_ref) == 0
            early = x_of(place_ref) < X // 2
            far_block = far_ref[...]
            zero = jnp.zeros_like(far_block)
            far_down = jnp.where(early, far_block, zero)
            far_up = jnp.where(early, zero, far_block)
            down_block = jnp.where(x_of(place_ref) < X - 1, down_ref[...], zero)
            up_block = jnp.where(x_of(place_ref) > 0, up_ref[...], zero)
            pairs = ((down_block, far_down), (even_ref[...], odd_ref[...]), (far_up, up_block))
            for side, (lower, upper) in enumerate(pairs):
                mine = jnp.where(first, lower, upper)
                theirs = jnp.where(first, upper, lower)
                mine_ref[side] = mine
                theirs_ref[side] = theirs
                if side != 1:
                    fill(stacked, 0, 3 * (side // 2), mine, col_count)
                    fill(stacked, 1, 3 * (side // 2), theirs, col_count)

        multiply(place_ref, lhs_ref, stacked, total, rest[:4])

    triple = jax.ShapeDtypeStruct((3, cells, width), BF16)
    return product_call(body, place, [even, odd, up, down, far], lhs, 6 * width, [triple, triple])


def first_sum(middle, sides):
    rows, third = middle[0].shape

    def body(*refs):
        out_ref = refs[-1]
        middle_total = sum(ref[...].astype(F32) for ref in refs[:4])
        side_total = sum(ref[...].astype(F32) for ref in refs[4:8])
        out_ref[:, :third] = side_total[:, :third].astype(BF16)
        out_ref[:, third : 2 * third] = middle_total.astype(BF16)
        out_ref[:, 2 * third :] = side_total[:, third:].astype(BF16)

    steps = 2
    spec = lambda columns: pl.BlockSpec((rows // steps, columns), lambda i: (i, 0))
    return kernel_call(
        body,
        (*middle, *sides),
        [spec(third)] * 4 + [spec(2 * third)] * 4,
        [jax.ShapeDtypeStruct((rows, 3 * third), BF16)],
        [spec(3 * third)],
        (steps,),
    )[0]


def input_gradient(place, held, got, weight, col_count):
    _, cells, half = held.shape
    deep, channels_in = weight.shape
    width = 256

    def body(place_ref, held_ref, got_ref, weight_ref, out_ref, stacked):
        @pl.when(pl.program_id(0) == 0)
        def _():
            first = core_of(place_ref) == 0
            for side in range(3):
                mine, theirs = held_ref[side], got_ref[side]
                lower, upper = jnp.where(first, mine, theirs), jnp.where(first, theirs, mine)
                for part, block in enumerate((lower, upper)):
                    for spot, tap in enumerate(column_taps(block, col_count)):
                        start = (2 * (3 * side + spot) + part) * half
                        stacked[:, start : start + half] = tap

        out_ref[...] = jnp.dot(
            stacked[...], weight_ref[...], preferred_element_type=F32
        ).astype(BF16)

    return kernel_call(
        body,
        (place, held, got, weight),
        [SMEM, whole(held.shape), whole(got.shape), pl.BlockSpec((deep, width), lambda i: (0, i))],
        [jax.ShapeDtypeStruct((cells, channels_in), BF16)],
        [pl.BlockSpec((cells, width), lambda i: (0, i))],
        (channels_in // width,),
        [pltpu.VMEM((cells, deep), BF16)],
        2 * cells * deep * channels_in,
        24,
    )[0]


def per_device(inputs, conv_out, grad_out, relu_mask, norm_gain, weight):
    image_count, row_count, col_count, channels_in = inputs.shape
    channels_out = conv_out.shape[3]
    cell_count = row_count * col_count * X * CORES
    cells = image_count * row_count * col_count
    half = channels_out // 2
    core = lax.axis_index("core")
    place = jnp.reshape(lax.axis_index(AXES), (1,)).astype(jnp.int32)

    input_flat = inputs.reshape(cells, channels_in)
    sums = channel_sums(conv_out, grad_out, relu_mask)
    got_sums = swapped(sums)
    mine, sent = prepare(
        place,
        *(value.reshape(cells, channels_out) for value in (conv_out, grad_out, relu_mask)),
    )
    input_flat, sent, got_sums = lax.optimization_barrier((input_flat, sent, got_sums))
    theirs = swapped(sent)
    input_other = swapped(input_flat)
    sums = sums + got_sums
    sums = [sums] + [around(sums, steps) for steps in (2, 1, 3)]
    lhs = transposed(input_flat, input_other)
    gain = norm_gain.reshape(1, channels_out)
    even, odd, far = pre_gradient(place, gain, sums, mine, theirs, image_count, cell_count)
    far = around(far, 2)
    up = around(even, 1)
    down = around(odd, X - 1)

    middle = list(middle_terms(place, even, odd, lhs, col_count))
    side_place, middle[0] = lax.optimization_barrier((place, middle[0]))
    middle = [middle[0]] + [crossed(middle[steps], steps) for steps in (2, 1, 3)]
    *sides, held, sent = side_terms(side_place, even, odd, up, down, far, lhs, col_count)
    sides[1:], sent, middle[1:] = lax.optimization_barrier((sides[1:], sent, middle[1:]))
    got = swapped(sent)
    weight, sides[0] = lax.optimization_barrier((weight, sides[0]))
    weight = jnp.transpose(weight, (1, 2, 0)).reshape(9 * channels_out, channels_in)
    sides = [sides[0]] + [crossed(sides[steps], steps) for steps in (2, 1, 3)]
    sides, weight = lax.optimization_barrier((sides, weight))
    merged = first_sum(middle, sides)
    place, merged = lax.optimization_barrier((place, merged))
    input_grad = input_gradient(place, held, got, weight, col_count)
    merged = exchanged(merged.reshape(Z * 4, 8, 9 * half))
    merged, input_grad = lax.optimization_barrier((merged, input_grad))
    inv_images = 1.0 / (image_count * Z * Y)
    merged = jnp.sum(merged.astype(F32), axis=0) * inv_images
    rows = merged.shape[0] // CORES
    kept = lax.dynamic_slice_in_dim(merged, core * rows, rows, axis=0)
    came = swapped(lax.dynamic_slice_in_dim(merged, (1 - core) * rows, rows, axis=0))
    kept, came = kept.reshape(rows, 9, half), came.reshape(rows, 9, half)
    weight_grad = jnp.concatenate(
        [jnp.where(core == 0, kept, came), jnp.where(core == 0, came, kept)], axis=2
    )

    return (input_grad.reshape(inputs.shape), weight_grad)


def solution(mesh):
    parted = Mesh(mesh.devices.reshape(Z, Y, X, CORES), AXES)
    cells = P(("z", "y"), ("x", "core"), None, None)
    return jax.shard_map(
        per_device,
        mesh=parted,
        in_specs=(cells, cells, cells, cells, P(), P()),
        out_specs=(cells, P(AXES, None, None)),
        check_vma=False,
    )
```

```python
import jax
import jax.numpy as jnp
from jax import lax
from jax.experimental import pallas as pl
from jax.experimental.pallas import tpu as pltpu
from jax.sharding import Mesh, PartitionSpec as P

RATE = 18
EPSILON = 1e-05
F32 = jnp.float32
BF16 = jnp.bfloat16
MIB = 1024 * 1024
AXES = ("z", "y", "x", "core")
Z, Y, X, CORES = 8, 4, 4, 2
SMEM = pl.BlockSpec(memory_space=pltpu.SMEM)


def device(z, y, x, core):
    return ((z * Y + y) * X + x) * CORES + core


def core_of(place_ref):
    return lax.rem(place_ref[0], CORES)


def x_of(place_ref):
    return lax.rem(lax.div(place_ref[0], CORES), X)


def y_of(place_ref):
    return lax.rem(lax.div(place_ref[0], CORES * X), Y)


def swapped(value):
    return lax.ppermute(value, "core", [(0, 1), (1, 0)])


def around(value, steps):
    return lax.ppermute(value, "x", [(source, (source + steps) % X) for source in range(X)])


def crossed(value, steps):
    pairs = []
    for z in range(Z):
        for y in range(Y):
            for x in range(X):
                pairs.append((device(z, y, x, 0), device(z, (y + steps) % Y, x, 0)))
                pairs.append((device(z, y, x, 1), device(z, y, (x + steps) % X, 1)))
    return lax.ppermute(value, AXES, pairs)


def exchanged(value):
    groups = [[device(z, y, x, 0) for z in range(Z) for x in range(X)] for y in range(Y)]
    groups += [[device(z, y, x, 1) for z in range(Z) for y in range(Y)] for x in range(X)]
    return lax.all_to_all(value, AXES, 0, 0, axis_index_groups=groups)


def whole(shape):
    return pl.BlockSpec(shape, lambda *_: (0,) * len(shape))


def kernel_call(body, operands, in_specs, out_shape, out_specs, grid=(1,), scratch=(), flops=0, vmem=8):
    moved = sum(value.size * value.dtype.itemsize for value in operands)
    moved += sum(value.size * value.dtype.itemsize for value in out_shape)
    return pl.pallas_call(
        body,
        grid=grid,
        in_specs=in_specs,
        out_specs=out_specs,
        out_shape=out_shape,
        scratch_shapes=list(scratch),
        compiler_params=pltpu.CompilerParams(vmem_limit_bytes=vmem * MIB),
        cost_estimate=pl.CostEstimate(flops=flops, bytes_accessed=moved, transcendentals=0),
    )(*operands)


def channel_sums(conv, grad, mask):
    values = conv.astype(F32)
    passed = grad.astype(F32) * mask.astype(F32)
    terms = (values, values * values, passed, passed * values)
    return jnp.stack([jnp.sum(term, axis=(1, 2)) for term in terms]).reshape(-1, conv.shape[3])


def prepare(place, conv, grad, mask):
    cells, channels = conv.shape
    half = channels // 2
    steps = 2
    tall = cells // steps

    def body(place_ref, conv_ref, grad_ref, mask_ref, mine_ref, sent_ref):
        first = core_of(place_ref) == 0
        passed = (grad_ref[...].astype(F32) * mask_ref[...].astype(F32)).astype(BF16)
        for which, value in enumerate((conv_ref[...], passed)):
            lower, upper = value[:, :half], value[:, half:]
            mine_ref[which] = jnp.where(first, lower, upper)
            sent_ref[which] = jnp.where(first, upper, lower)

    rows = pl.BlockSpec((tall, channels), lambda i: (i, 0))
    out = jax.ShapeDtypeStruct((2, cells, half), BF16)
    spec = pl.BlockSpec((2, tall, half), lambda i: (0, i, 0))
    return kernel_call(
        body,
        (place, conv, grad, mask),
        [SMEM, rows, rows, rows],
        [out, out],
        [spec, spec],
        (steps,),
        vmem=60,
    )


def pre_gradient(place, gain, sums, mine, theirs, images, cell_count):
    _, cells, half = mine.shape
    each = cells // images

    def body(place_ref, gain_ref, a_ref, b_ref, c_ref, d_ref, mine_ref, theirs_ref, even_ref, odd_ref, far_ref):
        first = core_of(place_ref) == 0
        early = x_of(place_ref) < X // 2
        means = (a_ref[...] + b_ref[...] + c_ref[...] + d_ref[...]) / cell_count
        means = jnp.where(first, means[:, :half], means[:, half:])
        gain_row = jnp.where(first, gain_ref[:, :half], gain_ref[:, half:])
        for image in range(images):
            rows = pl.ds(image * each, each)
            chan_mean, second, passed_mean, product_mean = (
                means[kind * images + image : kind * images + image + 1] for kind in range(4)
            )
            inv_std = 1.0 / jnp.sqrt(second - chan_mean * chan_mean + EPSILON)
            grad_mean = gain_row * passed_mean
            cross_mean = gain_row * (product_mean - chan_mean * passed_mean) * inv_std
            blocks = []
            for ref in (mine_ref, theirs_ref):
                values, passed = ref[0, rows, :].astype(F32), ref[1, rows, :].astype(F32)
                normed = (values - chan_mean) * inv_std
                blocks.append(inv_std * (gain_row * passed - grad_mean - normed * cross_mean))
            even = jnp.where(first, blocks[0], blocks[1])
            odd = jnp.where(first, blocks[1], blocks[0])
            even_ref[rows, :] = even.astype(BF16)
            odd_ref[rows, :] = odd.astype(BF16)
            far_ref[rows, :] = jnp.where(early, odd, even).astype(BF16)

    out = jax.ShapeDtypeStruct((cells, half), BF16)
    return kernel_call(
        body,
        (place, gain, *sums, mine, theirs),
        [SMEM, whole(gain.shape)] + [whole(sums[0].shape)] * 4 + [whole(mine.shape)] * 2,
        [out] * 3,
        [whole(out.shape)] * 3,
    )


def padded_count(cells):
    return -(-cells // 128) * 128


def transposed(own, other):
    cells, channels = own.shape
    deep = padded_count(cells)
    width = 256

    def body(own_ref, other_ref, out_ref):
        for which, ref in enumerate((own_ref, other_ref)):
            block = jnp.concatenate([ref[...], jnp.zeros((deep - cells, width), BF16)], axis=0)
            out_ref[:, which * deep : (which + 1) * deep] = block.T

    spec = pl.BlockSpec((cells, width), lambda i: (0, i))
    return kernel_call(
        body,
        (own, other),
        [spec, spec],
        [jax.ShapeDtypeStruct((channels, 2 * deep), BF16)],
        [pl.BlockSpec((width, 2 * deep), lambda i: (i, 0))],
        (channels // width,),
    )[0]


def column_taps(block, col_count):
    cells, channels = block.shape
    wide = block.astype(F32)
    column = lax.broadcasted_iota(jnp.int32, (cells // col_count, col_count, channels), 1)
    column = column.reshape(cells, channels)
    before = jnp.where(column < col_count - RATE, pltpu.roll(wide, cells - RATE, 0), 0.0)
    after = jnp.where(column >= RATE, pltpu.roll(wide, RATE, 0), 0.0)
    return before.astype(BF16), block, after.astype(BF16)


def fill(stacked, slot, place, block, col_count):
    cells, width = block.shape
    deep = padded_count(cells)
    for spot, tap in enumerate(column_taps(block, col_count)):
        columns = slice((place + spot) * width, (place + spot + 1) * width)
        stacked[slot * deep : slot * deep + cells, columns] = tap


def clear_padding(stacked, cells):
    deep, columns = stacked.shape
    block = deep // 2
    for slot in range(2):
        stacked[slot * block + cells : (slot + 1) * block, :] = jnp.zeros((block - cells, columns), BF16)


def multiply(place_ref, lhs_ref, stacked, total, out_refs):
    columns = stacked.shape[1]
    product = jnp.dot(lhs_ref[...], stacked[...], preferred_element_type=F32)
    total[...] = product.reshape(total.shape)
    tall = total.shape[0] * 32

    @pl.when(core_of(place_ref) == 0)
    def _():
        for steps in range(Y):
            chunk = total[:, lax.rem(y_of(place_ref) + steps, Y), :, :, :]
            out_refs[steps][...] = chunk.reshape(tall, columns).astype(BF16)

    @pl.when(core_of(place_ref) != 0)
    def _():
        for steps in range(X):
            chunk = total[:, :, lax.rem(x_of(place_ref) + steps, X), :, :]
            out_refs[steps][...] = chunk.reshape(tall, columns).astype(BF16)


def product_call(body, place, fixed, lhs, columns, extra):
    channels_in, deep = lhs.shape
    steps = 2
    tall = channels_in // steps
    return kernel_call(
        body,
        (place, *fixed, lhs),
        [SMEM] + [whole(value.shape) for value in fixed] + [pl.BlockSpec((tall, deep), lambda i: (i, 0))],
        [jax.ShapeDtypeStruct((channels_in // 4, columns), BF16)] * 4 + extra,
        [pl.BlockSpec((tall // 4, columns), lambda i: (i, 0))] * 4 + [whole(value.shape) for value in extra],
        (steps,),
        [pltpu.VMEM((deep, columns), BF16), pltpu.VMEM((tall // 128, Y, X, 8, columns), F32)],
        flops=2 * channels_in * deep * columns,
        vmem=24,
    )


def middle_terms(place, even, odd, lhs, col_count):
    cells, width = even.shape

    def body(place_ref, even_ref, odd_ref, lhs_ref, *rest):
        stacked, total = rest[4:]

        @pl.when(pl.program_id(0) == 0)
        def _():
            clear_padding(stacked, cells)
            first = core_of(place_ref) == 0
            even_block, odd_block = even_ref[...], odd_ref[...]
            fill(stacked, 0, 0, jnp.where(first, even_block, odd_block), col_count)
            fill(stacked, 1, 0, jnp.where(first, odd_block, even_block), col_count)

        multiply(place_ref, lhs_ref, stacked, total, rest[:4])

    return product_call(body, place, [even, odd], lhs, 3 * width, [])


def tap_blocks(place_ref, even_ref, odd_ref, up_ref, down_ref, far_ref):
    x = x_of(place_ref)
    far_block = far_ref[...]
    zero = jnp.zeros_like(far_block)
    far_down = jnp.where(x < X // 2, far_block, zero)
    far_up = jnp.where(x < X // 2, zero, far_block)
    down_block = jnp.where(x < X - 1, down_ref[...], zero)
    up_block = jnp.where(x > 0, up_ref[...], zero)
    return (down_block, far_down), (even_ref[...], odd_ref[...]), (far_up, up_block)


def own_blocks(place, even, odd, up, down, far):
    operands = (even, odd, up, down, far)

    def body(place_ref, *refs):
        first = core_of(place_ref) == 0
        for side, (lower, upper) in enumerate(tap_blocks(place_ref, *refs[:5])):
            refs[5][side] = jnp.where(first, lower, upper)

    out = jax.ShapeDtypeStruct((3,) + even.shape, BF16)
    return kernel_call(
        body,
        (place, *operands),
        [SMEM] + [whole(value.shape) for value in operands],
        [out],
        [whole(out.shape)],
    )[0]


def side_terms(place, even, odd, up, down, far, lhs, col_count):
    cells, width = up.shape

    def body(place_ref, even_ref, odd_ref, up_ref, down_ref, far_ref, lhs_ref, *rest):
        theirs_refs = rest[4:6]
        stacked, total = rest[6:]

        @pl.when(pl.program_id(0) == 0)
        def _():
            clear_padding(stacked, cells)
            first = core_of(place_ref) == 0
            blocks = tap_blocks(place_ref, even_ref, odd_ref, up_ref, down_ref, far_ref)
            for side, (lower, upper) in enumerate(blocks):
                theirs = jnp.where(first, upper, lower)
                for part, ref in enumerate(theirs_refs):
                    ref[side] = theirs[part * (cells // 2) : (part + 1) * (cells // 2)]
                if side != 1:
                    mine = jnp.where(first, lower, upper)
                    fill(stacked, 0, 3 * (side // 2), mine, col_count)
                    fill(stacked, 1, 3 * (side // 2), theirs, col_count)

        multiply(place_ref, lhs_ref, stacked, total, rest[:4])

    part = jax.ShapeDtypeStruct((3, cells // 2, width), BF16)
    return product_call(body, place, [even, odd, up, down, far], lhs, 6 * width, [part, part])


def first_sum(middle, sides):
    rows, third = middle[0].shape

    def body(*refs):
        out_ref = refs[-1]
        middle_total = sum(ref[...].astype(F32) for ref in refs[:4])
        side_total = sum(ref[...].astype(F32) for ref in refs[4:8])
        out_ref[:, :third] = side_total[:, :third].astype(BF16)
        out_ref[:, third : 2 * third] = middle_total.astype(BF16)
        out_ref[:, 2 * third :] = side_total[:, third:].astype(BF16)

    steps = 2
    spec = lambda columns: pl.BlockSpec((rows // steps, columns), lambda i: (i, 0))
    return kernel_call(
        body,
        (*middle, *sides),
        [spec(third)] * 4 + [spec(2 * third)] * 4,
        [jax.ShapeDtypeStruct((rows, 3 * third), BF16)],
        [spec(3 * third)],
        (steps,),
    )[0]


def input_gradient(place, held, got, weight, col_count):
    _, cells, half = held.shape
    deep, channels_in = weight.shape
    width = 256

    def body(place_ref, held_ref, *rest):
        got_refs, (weight_ref, out_ref, stacked) = rest[:2], rest[2:]

        @pl.when(pl.program_id(0) == 0)
        def _():
            first = core_of(place_ref) == 0
            for side in range(3):
                mine = held_ref[side]
                theirs = jnp.concatenate([ref[side] for ref in got_refs], axis=0)
                lower, upper = jnp.where(first, mine, theirs), jnp.where(first, theirs, mine)
                for part, block in enumerate((lower, upper)):
                    for spot, tap in enumerate(column_taps(block, col_count)):
                        start = (2 * (3 * side + spot) + part) * half
                        stacked[:, start : start + half] = tap

        out_ref[...] = jnp.dot(
            stacked[...], weight_ref[...], preferred_element_type=F32
        ).astype(BF16)

    return kernel_call(
        body,
        (place, held, *got, weight),
        [SMEM, whole(held.shape)] + [whole(block.shape) for block in got] + [pl.BlockSpec((deep, width), lambda i: (0, i))],
        [jax.ShapeDtypeStruct((cells, channels_in), BF16)],
        [pl.BlockSpec((cells, width), lambda i: (0, i))],
        (channels_in // width,),
        [pltpu.VMEM((cells, deep), BF16)],
        2 * cells * deep * channels_in,
        60,
    )[0]


def per_device(inputs, conv_out, grad_out, relu_mask, norm_gain, weight):
    image_count, row_count, col_count, channels_in = inputs.shape
    channels_out = conv_out.shape[3]
    cell_count = row_count * col_count * X * CORES
    cells = image_count * row_count * col_count
    half = channels_out // 2
    core = lax.axis_index("core")
    place = jnp.reshape(lax.axis_index(AXES), (1,)).astype(jnp.int32)

    input_flat = inputs.reshape(cells, channels_in)
    sums = channel_sums(conv_out, grad_out, relu_mask)
    got_sums = swapped(sums)
    mine, sent = prepare(
        place,
        *(value.reshape(cells, channels_out) for value in (conv_out, grad_out, relu_mask)),
    )
    input_flat, sent, got_sums = lax.optimization_barrier((input_flat, sent, got_sums))
    theirs = swapped(sent)
    input_other = swapped(input_flat)
    sums = sums + got_sums
    sums = [sums] + [around(sums, steps) for steps in (2, 1, 3)]
    lhs = transposed(input_flat, input_other)
    gain = norm_gain.reshape(1, channels_out)
    even, odd, far = pre_gradient(place, gain, sums, mine, theirs, image_count, cell_count)
    far = around(far, 2)
    up = around(even, 1)
    down = around(odd, X - 1)

    middle = list(middle_terms(place, even, odd, lhs, col_count))
    side_place, middle[0] = lax.optimization_barrier((place, middle[0]))
    middle = [middle[0]] + [crossed(middle[steps], steps) for steps in (2, 1, 3)]
    *sides, sent_lower, sent_upper = side_terms(side_place, even, odd, up, down, far, lhs, col_count)
    sent = [sent_lower, sent_upper]
    sides[1:], sent, middle[1:] = lax.optimization_barrier((sides[1:], sent, middle[1:]))
    got = [swapped(block) for block in sent]
    weight, sides[0] = lax.optimization_barrier((weight, sides[0]))
    weight = jnp.transpose(weight, (1, 2, 0)).reshape(9 * channels_out, channels_in)
    sides = [sides[0]] + [crossed(sides[steps], steps) for steps in (2, 1, 3)]
    held_place, weight = lax.optimization_barrier((place, weight))
    held = own_blocks(held_place, even, odd, up, down, far)
    sides, weight, got, held = lax.optimization_barrier((sides, weight, got, held))
    merged = first_sum(middle, sides)
    place, merged = lax.optimization_barrier((place, merged))
    input_grad = input_gradient(place, held, got, weight, col_count)
    merged = exchanged(merged.reshape(Z * 4, 8, 9 * half))
    merged, input_grad = lax.optimization_barrier((merged, input_grad))
    inv_images = 1.0 / (image_count * Z * Y)
    merged = jnp.sum(merged.astype(F32), axis=0) * inv_images
    rows = merged.shape[0] // CORES
    kept = lax.dynamic_slice_in_dim(merged, core * rows, rows, axis=0)
    came = swapped(lax.dynamic_slice_in_dim(merged, (1 - core) * rows, rows, axis=0))
    kept, came = kept.reshape(rows, 9, half), came.reshape(rows, 9, half)
    weight_grad = jnp.concatenate(
        [jnp.where(core == 0, kept, came), jnp.where(core == 0, came, kept)], axis=2
    )

    return (input_grad.reshape(inputs.shape), weight_grad)


def solution(mesh):
    parted = Mesh(mesh.devices.reshape(Z, Y, X, CORES), AXES)
    cells = P(("z", "y"), ("x", "core"), None, None)
    return jax.shard_map(
        per_device,
        mesh=parted,
        in_specs=(cells, cells, cells, cells, P(), P()),
        out_specs=(cells, P(AXES, None, None)),
        check_vma=False,
    )
```

```python
import jax
import jax.numpy as jnp
from jax import lax
from jax.experimental import pallas as pl
from jax.experimental.pallas import tpu as pltpu
from jax.sharding import Mesh, PartitionSpec as P

RATE = 18
EPSILON = 1e-05
F32 = jnp.float32
BF16 = jnp.bfloat16
MIB = 1024 * 1024
AXES = ("z", "y", "x", "core")
Z, Y, X, CORES = 8, 4, 4, 2
SMEM = pl.BlockSpec(memory_space=pltpu.SMEM)


def device(z, y, x, core):
    return ((z * Y + y) * X + x) * CORES + core


def core_of(place_ref):
    return lax.rem(place_ref[0], CORES)


def x_of(place_ref):
    return lax.rem(lax.div(place_ref[0], CORES), X)


def y_of(place_ref):
    return lax.rem(lax.div(place_ref[0], CORES * X), Y)


def swapped(value):
    return lax.ppermute(value, "core", [(0, 1), (1, 0)])


def around(value, steps):
    return lax.ppermute(value, "x", [(source, (source + steps) % X) for source in range(X)])


def crossed(value, steps):
    pairs = []
    for z in range(Z):
        for y in range(Y):
            for x in range(X):
                pairs.append((device(z, y, x, 0), device(z, (y + steps) % Y, x, 0)))
                pairs.append((device(z, y, x, 1), device(z, y, (x + steps) % X, 1)))
    return lax.ppermute(value, AXES, pairs)


def exchanged(value):
    groups = [[device(z, y, x, 0) for z in range(Z) for x in range(X)] for y in range(Y)]
    groups += [[device(z, y, x, 1) for z in range(Z) for y in range(Y)] for x in range(X)]
    return lax.all_to_all(value, AXES, 0, 0, axis_index_groups=groups)


VMEM = pl.BlockSpec(memory_space=pltpu.VMEM)


def whole(shape):
    return pl.BlockSpec(shape, lambda *_: (0,) * len(shape))


def kernel_call(body, operands, in_specs, out_shape, out_specs, grid=(1,), scratch=(), flops=0, vmem=8):
    moved = sum(value.size * value.dtype.itemsize for value in operands)
    moved += sum(value.size * value.dtype.itemsize for value in out_shape)
    return pl.pallas_call(
        body,
        grid=grid,
        in_specs=in_specs,
        out_specs=out_specs,
        out_shape=out_shape,
        scratch_shapes=list(scratch),
        compiler_params=pltpu.CompilerParams(vmem_limit_bytes=vmem * MIB),
        cost_estimate=pl.CostEstimate(flops=flops, bytes_accessed=moved, transcendentals=0),
    )(*operands)


def channel_sums(conv, grad, mask):
    values = conv.astype(F32)
    passed = grad.astype(F32) * mask.astype(F32)
    terms = (values, values * values, passed, passed * values)
    return jnp.stack([jnp.sum(term, axis=(1, 2)) for term in terms]).reshape(-1, conv.shape[3])


def prepare(place, conv, grad, mask):
    cells, channels = conv.shape
    half = channels // 2
    steps = 2
    tall = cells // steps

    def body(place_ref, conv_ref, grad_ref, mask_ref, mine_ref, sent_ref):
        first = core_of(place_ref) == 0
        passed = (grad_ref[...].astype(F32) * mask_ref[...].astype(F32)).astype(BF16)
        for which, value in enumerate((conv_ref[...], passed)):
            lower, upper = value[:, :half], value[:, half:]
            mine_ref[which] = jnp.where(first, lower, upper)
            sent_ref[which] = jnp.where(first, upper, lower)

    rows = pl.BlockSpec((tall, channels), lambda i: (i, 0))
    out = jax.ShapeDtypeStruct((2, cells, half), BF16)
    spec = pl.BlockSpec((2, tall, half), lambda i: (0, i, 0))
    return kernel_call(
        body,
        (place, conv, grad, mask),
        [SMEM, rows, rows, rows],
        [out, out],
        [spec, spec],
        (steps,),
        vmem=60,
    )


def pre_gradient(place, gain, sums, mine, theirs, images, cell_count):
    _, cells, half = mine.shape
    each = cells // images

    def body(place_ref, gain_ref, a_ref, b_ref, c_ref, d_ref, mine_ref, theirs_ref, even_ref, odd_ref, far_ref):
        first = core_of(place_ref) == 0
        early = x_of(place_ref) < X // 2
        means = (a_ref[...] + b_ref[...] + c_ref[...] + d_ref[...]) / cell_count
        means = jnp.where(first, means[:, :half], means[:, half:])
        gain_row = jnp.where(first, gain_ref[:, :half], gain_ref[:, half:])
        for image in range(images):
            rows = pl.ds(image * each, each)
            chan_mean, second, passed_mean, product_mean = (
                means[kind * images + image : kind * images + image + 1] for kind in range(4)
            )
            inv_std = 1.0 / jnp.sqrt(second - chan_mean * chan_mean + EPSILON)
            grad_mean = gain_row * passed_mean
            cross_mean = gain_row * (product_mean - chan_mean * passed_mean) * inv_std
            blocks = []
            for ref in (mine_ref, theirs_ref):
                values, passed = ref[0, rows, :].astype(F32), ref[1, rows, :].astype(F32)
                normed = (values - chan_mean) * inv_std
                blocks.append(inv_std * (gain_row * passed - grad_mean - normed * cross_mean))
            even = jnp.where(first, blocks[0], blocks[1])
            odd = jnp.where(first, blocks[1], blocks[0])
            even_ref[rows, :] = even.astype(BF16)
            odd_ref[rows, :] = odd.astype(BF16)
            far_ref[rows, :] = jnp.where(early, odd, even).astype(BF16)

    out = jax.ShapeDtypeStruct((cells, half), BF16)
    return kernel_call(
        body,
        (place, gain, *sums, mine, theirs),
        [SMEM, whole(gain.shape)] + [whole(sums[0].shape)] * 4 + [whole(mine.shape)] * 2,
        [out] * 3,
        [whole(out.shape)] * 3,
    )


def padded_count(cells):
    return -(-cells // 128) * 128


def transposed(own, other):
    cells, channels = own.shape
    deep = padded_count(cells)
    width = 256

    def body(own_ref, other_ref, out_ref):
        for which, ref in enumerate((own_ref, other_ref)):
            block = jnp.concatenate([ref[...], jnp.zeros((deep - cells, width), BF16)], axis=0)
            out_ref[:, which * deep : (which + 1) * deep] = block.T

    spec = pl.BlockSpec((cells, width), lambda i: (0, i))
    return kernel_call(
        body,
        (own, other),
        [spec, spec],
        [jax.ShapeDtypeStruct((channels, 2 * deep), BF16)],
        [pl.BlockSpec((width, 2 * deep), lambda i: (i, 0))],
        (channels // width,),
    )[0]


def column_taps(block, col_count):
    cells, channels = block.shape
    wide = block.astype(F32)
    column = lax.broadcasted_iota(jnp.int32, (cells // col_count, col_count, channels), 1)
    column = column.reshape(cells, channels)
    before = jnp.where(column < col_count - RATE, pltpu.roll(wide, cells - RATE, 0), 0.0)
    after = jnp.where(column >= RATE, pltpu.roll(wide, RATE, 0), 0.0)
    return before.astype(BF16), block, after.astype(BF16)


def fill(stacked, slot, place, block, col_count):
    cells, width = block.shape
    deep = padded_count(cells)
    for spot, tap in enumerate(column_taps(block, col_count)):
        columns = slice((place + spot) * width, (place + spot + 1) * width)
        stacked[slot * deep : slot * deep + cells, columns] = tap


def clear_padding(stacked, cells):
    deep, columns = stacked.shape
    block = deep // 2
    for slot in range(2):
        stacked[slot * block + cells : (slot + 1) * block, :] = jnp.zeros((block - cells, columns), BF16)


def multiply(place_ref, lhs_ref, stacked, total, out_refs):
    columns = stacked.shape[1]
    groups = total.shape[0]
    for part in range(lhs_ref.shape[0] // (groups * 128)):
        rows = slice(part * groups * 128, (part + 1) * groups * 128)
        out_rows = slice(part * groups * 32, (part + 1) * groups * 32)
        product = jnp.dot(lhs_ref[rows, :], stacked[...], preferred_element_type=F32)
        total[...] = product.reshape(total.shape)

        @pl.when(core_of(place_ref) == 0)
        def _():
            for steps in range(Y):
                chunk = total[:, lax.rem(y_of(place_ref) + steps, Y), :, :, :]
                out_refs[steps][out_rows, :] = chunk.reshape(groups * 32, columns).astype(BF16)

        @pl.when(core_of(place_ref) != 0)
        def _():
            for steps in range(X):
                chunk = total[:, :, lax.rem(x_of(place_ref) + steps, X), :, :]
                out_refs[steps][out_rows, :] = chunk.reshape(groups * 32, columns).astype(BF16)


def product_call(body, place, fixed, lhs, columns, extra):
    channels_in, deep = lhs.shape
    groups = 4
    return kernel_call(
        body,
        (place, *fixed, lhs),
        [SMEM] + [VMEM] * (len(fixed) + 1),
        [jax.ShapeDtypeStruct((channels_in // 4, columns), BF16)] * 4 + extra,
        [VMEM] * (4 + len(extra)),
        (),
        [pltpu.VMEM((deep, columns), BF16), pltpu.VMEM((groups, Y, X, 8, columns), F32)],
        flops=2 * channels_in * deep * columns,
        vmem=24,
    )


def middle_terms(place, even, odd, lhs, col_count):
    cells, width = even.shape

    def body(place_ref, even_ref, odd_ref, lhs_ref, *rest):
        stacked, total = rest[4:]
        clear_padding(stacked, cells)
        first = core_of(place_ref) == 0
        even_block, odd_block = even_ref[...], odd_ref[...]
        fill(stacked, 0, 0, jnp.where(first, even_block, odd_block), col_count)
        fill(stacked, 1, 0, jnp.where(first, odd_block, even_block), col_count)
        multiply(place_ref, lhs_ref, stacked, total, rest[:4])

    return product_call(body, place, [even, odd], lhs, 3 * width, [])


def tap_blocks(place_ref, even_ref, odd_ref, up_ref, down_ref, far_ref):
    x = x_of(place_ref)
    far_block = far_ref[...]
    zero = jnp.zeros_like(far_block)
    far_down = jnp.where(x < X // 2, far_block, zero)
    far_up = jnp.where(x < X // 2, zero, far_block)
    down_block = jnp.where(x < X - 1, down_ref[...], zero)
    up_block = jnp.where(x > 0, up_ref[...], zero)
    return (down_block, far_down), (even_ref[...], odd_ref[...]), (far_up, up_block)


def own_blocks(place, even, odd, up, down, far):
    operands = (even, odd, up, down, far)

    def body(place_ref, *refs):
        first = core_of(place_ref) == 0
        for side, (lower, upper) in enumerate(tap_blocks(place_ref, *refs[:5])):
            refs[5][side] = jnp.where(first, lower, upper)

    out = jax.ShapeDtypeStruct((3,) + even.shape, BF16)
    return kernel_call(
        body,
        (place, *operands),
        [SMEM] + [whole(value.shape) for value in operands],
        [out],
        [whole(out.shape)],
    )[0]


def side_terms(place, even, odd, up, down, far, lhs, col_count):
    cells, width = up.shape

    def body(place_ref, even_ref, odd_ref, up_ref, down_ref, far_ref, lhs_ref, *rest):
        theirs_refs = rest[4:6]
        stacked, total = rest[6:]

        clear_padding(stacked, cells)
        first = core_of(place_ref) == 0
        blocks = tap_blocks(place_ref, even_ref, odd_ref, up_ref, down_ref, far_ref)
        for side, (lower, upper) in enumerate(blocks):
            theirs = jnp.where(first, upper, lower)
            for part, ref in enumerate(theirs_refs):
                ref[side] = theirs[part * (cells // 2) : (part + 1) * (cells // 2)]
            if side != 1:
                mine = jnp.where(first, lower, upper)
                fill(stacked, 0, 3 * (side // 2), mine, col_count)
                fill(stacked, 1, 3 * (side // 2), theirs, col_count)
        multiply(place_ref, lhs_ref, stacked, total, rest[:4])

    part = jax.ShapeDtypeStruct((3, cells // 2, width), BF16)
    return product_call(body, place, [even, odd, up, down, far], lhs, 6 * width, [part, part])


def first_sum(middle, sides):
    rows, third = middle[0].shape

    def body(*refs):
        out_ref = refs[-1]
        middle_total = sum(ref[...].astype(F32) for ref in refs[:4])
        side_total = sum(ref[...].astype(F32) for ref in refs[4:8])
        out_ref[:, :third] = side_total[:, :third].astype(BF16)
        out_ref[:, third : 2 * third] = middle_total.astype(BF16)
        out_ref[:, 2 * third :] = side_total[:, third:].astype(BF16)

    steps = 2
    spec = lambda columns: pl.BlockSpec((rows // steps, columns), lambda i: (i, 0))
    return kernel_call(
        body,
        (*middle, *sides),
        [spec(third)] * 4 + [spec(2 * third)] * 4,
        [jax.ShapeDtypeStruct((rows, 3 * third), BF16)],
        [spec(3 * third)],
        (steps,),
    )[0]


def input_gradient(place, held, got, weight, col_count):
    _, cells, half = held.shape
    deep, channels_in = weight.shape
    width = 256

    def body(place_ref, held_ref, *rest):
        got_refs, (weight_ref, out_ref, stacked) = rest[:2], rest[2:]

        @pl.when(pl.program_id(0) == 0)
        def _():
            first = core_of(place_ref) == 0
            for side in range(3):
                mine = held_ref[side]
                theirs = jnp.concatenate([ref[side] for ref in got_refs], axis=0)
                lower, upper = jnp.where(first, mine, theirs), jnp.where(first, theirs, mine)
                for part, block in enumerate((lower, upper)):
                    for spot, tap in enumerate(column_taps(block, col_count)):
                        start = (2 * (3 * side + spot) + part) * half
                        stacked[:, start : start + half] = tap

        out_ref[...] = jnp.dot(
            stacked[...], weight_ref[...], preferred_element_type=F32
        ).astype(BF16)

    return kernel_call(
        body,
        (place, held, *got, weight),
        [SMEM, whole(held.shape)] + [whole(block.shape) for block in got] + [pl.BlockSpec((deep, width), lambda i: (0, i))],
        [jax.ShapeDtypeStruct((cells, channels_in), BF16)],
        [pl.BlockSpec((cells, width), lambda i: (0, i))],
        (channels_in // width,),
        [pltpu.VMEM((cells, deep), BF16)],
        2 * cells * deep * channels_in,
        60,
    )[0]


def per_device(inputs, conv_out, grad_out, relu_mask, norm_gain, weight):
    image_count, row_count, col_count, channels_in = inputs.shape
    channels_out = conv_out.shape[3]
    cell_count = row_count * col_count * X * CORES
    cells = image_count * row_count * col_count
    half = channels_out // 2
    core = lax.axis_index("core")
    place = jnp.reshape(lax.axis_index(AXES), (1,)).astype(jnp.int32)

    input_flat = inputs.reshape(cells, channels_in)
    sums = channel_sums(conv_out, grad_out, relu_mask)
    got_sums = swapped(sums)
    mine, sent = prepare(
        place,
        *(value.reshape(cells, channels_out) for value in (conv_out, grad_out, relu_mask)),
    )
    input_flat, sent, got_sums = lax.optimization_barrier((input_flat, sent, got_sums))
    theirs = swapped(sent)
    input_other = swapped(input_flat)
    sums = sums + got_sums
    sums = [sums] + [around(sums, steps) for steps in (2, 1, 3)]
    lhs = transposed(input_flat, input_other)
    gain = norm_gain.reshape(1, channels_out)
    even, odd, far = pre_gradient(place, gain, sums, mine, theirs, image_count, cell_count)
    far = around(far, 2)
    up = around(even, 1)
    down = around(odd, X - 1)

    middle = list(middle_terms(place, even, odd, lhs, col_count))
    side_place, middle[0] = lax.optimization_barrier((place, middle[0]))
    middle = [middle[0]] + [crossed(middle[steps], steps) for steps in (2, 1, 3)]
    *sides, sent_lower, sent_upper = side_terms(side_place, even, odd, up, down, far, lhs, col_count)
    sent = [sent_lower, sent_upper]
    sides[1:], sent, middle[1:] = lax.optimization_barrier((sides[1:], sent, middle[1:]))
    got = [swapped(block) for block in sent]
    weight, sides[0] = lax.optimization_barrier((weight, sides[0]))
    weight = jnp.transpose(weight, (1, 2, 0)).reshape(9 * channels_out, channels_in)
    sides = [sides[0]] + [crossed(sides[steps], steps) for steps in (2, 1, 3)]
    held_place, weight = lax.optimization_barrier((place, weight))
    held = own_blocks(held_place, even, odd, up, down, far)
    sides, weight, got, held = lax.optimization_barrier((sides, weight, got, held))
    merged = first_sum(middle, sides)
    place, merged = lax.optimization_barrier((place, merged))
    input_grad = input_gradient(place, held, got, weight, col_count)
    merged = exchanged(merged.reshape(Z * 4, 8, 9 * half))
    merged, input_grad = lax.optimization_barrier((merged, input_grad))
    inv_images = 1.0 / (image_count * Z * Y)
    merged = jnp.sum(merged.astype(F32), axis=0) * inv_images
    rows = merged.shape[0] // CORES
    kept = lax.dynamic_slice_in_dim(merged, core * rows, rows, axis=0)
    came = swapped(lax.dynamic_slice_in_dim(merged, (1 - core) * rows, rows, axis=0))
    kept, came = kept.reshape(rows, 9, half), came.reshape(rows, 9, half)
    weight_grad = jnp.concatenate(
        [jnp.where(core == 0, kept, came), jnp.where(core == 0, came, kept)], axis=2
    )

    return (input_grad.reshape(inputs.shape), weight_grad)


def solution(mesh):
    parted = Mesh(mesh.devices.reshape(Z, Y, X, CORES), AXES)
    cells = P(("z", "y"), ("x", "core"), None, None)
    return jax.shard_map(
        per_device,
        mesh=parted,
        in_specs=(cells, cells, cells, cells, P(), P()),
        out_specs=(cells, P(AXES, None, None)),
        check_vma=False,
    )
```

```python
import jax
import jax.numpy as jnp
from jax import lax
from jax.experimental import pallas as pl
from jax.experimental.pallas import tpu as pltpu
from jax.sharding import Mesh, PartitionSpec as P

RATE = 18
EPSILON = 1e-05
F32 = jnp.float32
BF16 = jnp.bfloat16
MIB = 1024 * 1024
AXES = ("z", "y", "x", "core")
Z, Y, X, CORES = 8, 4, 4, 2
SMEM = pl.BlockSpec(memory_space=pltpu.SMEM)


def device(z, y, x, core):
    return ((z * Y + y) * X + x) * CORES + core


def core_of(place_ref):
    return lax.rem(place_ref[0], CORES)


def x_of(place_ref):
    return lax.rem(lax.div(place_ref[0], CORES), X)


def y_of(place_ref):
    return lax.rem(lax.div(place_ref[0], CORES * X), Y)


def swapped(value):
    return lax.ppermute(value, "core", [(0, 1), (1, 0)])


def around(value, steps):
    return lax.ppermute(value, "x", [(source, (source + steps) % X) for source in range(X)])


def crossed(value, steps):
    pairs = []
    for z in range(Z):
        for y in range(Y):
            for x in range(X):
                pairs.append((device(z, y, x, 0), device(z, (y + steps) % Y, x, 0)))
                pairs.append((device(z, y, x, 1), device(z, y, (x + steps) % X, 1)))
    return lax.ppermute(value, AXES, pairs)


def exchanged(value):
    groups = [[device(z, y, x, 0) for z in range(Z) for x in range(X)] for y in range(Y)]
    groups += [[device(z, y, x, 1) for z in range(Z) for y in range(Y)] for x in range(X)]
    return lax.all_to_all(value, AXES, 0, 0, axis_index_groups=groups)


def whole(shape):
    return pl.BlockSpec(shape, lambda *_: (0,) * len(shape))


def kernel_call(body, operands, in_specs, out_shape, out_specs, grid=(1,), scratch=(), flops=0, vmem=8):
    moved = sum(value.size * value.dtype.itemsize for value in operands)
    moved += sum(value.size * value.dtype.itemsize for value in out_shape)
    return pl.pallas_call(
        body,
        grid=grid,
        in_specs=in_specs,
        out_specs=out_specs,
        out_shape=out_shape,
        scratch_shapes=list(scratch),
        compiler_params=pltpu.CompilerParams(vmem_limit_bytes=vmem * MIB),
        cost_estimate=pl.CostEstimate(flops=flops, bytes_accessed=moved, transcendentals=0),
    )(*operands)


def channel_sums(conv, grad, mask):
    values = conv.astype(F32)
    passed = grad.astype(F32) * mask.astype(F32)
    terms = (values, values * values, passed, passed * values)
    return jnp.stack([jnp.sum(term, axis=(1, 2)) for term in terms]).reshape(-1, conv.shape[3])


def prepare(place, conv, grad, mask):
    cells, channels = conv.shape
    half = channels // 2
    steps = 2
    tall = cells // steps

    def body(place_ref, conv_ref, grad_ref, mask_ref, sent_ref):
        first = core_of(place_ref) == 0
        passed = (grad_ref[...].astype(F32) * mask_ref[...].astype(F32)).astype(BF16)
        for which, value in enumerate((conv_ref[...], passed)):
            sent_ref[which] = jnp.where(first, value[:, half:], value[:, :half])

    rows = pl.BlockSpec((tall, channels), lambda i: (i, 0))
    return kernel_call(
        body,
        (place, conv, grad, mask),
        [SMEM, rows, rows, rows],
        [jax.ShapeDtypeStruct((2, cells, half), BF16)],
        [pl.BlockSpec((2, tall, half), lambda i: (0, i, 0))],
        (steps,),
        vmem=60,
    )[0]


def pre_gradient(place, gain, sums, mine, theirs, images, cell_count):
    _, cells, half = theirs.shape
    each = cells // images

    def body(place_ref, gain_ref, a_ref, b_ref, c_ref, d_ref, conv_ref, passed_ref, theirs_ref, even_ref, odd_ref, far_ref):
        first = core_of(place_ref) == 0
        early = x_of(place_ref) < X // 2
        means = (a_ref[...] + b_ref[...] + c_ref[...] + d_ref[...]) / cell_count
        means = jnp.where(first, means[:, :half], means[:, half:])
        gain_row = jnp.where(first, gain_ref[:, :half], gain_ref[:, half:])
        for image in range(images):
            rows = pl.ds(image * each, each)
            chan_mean, second, passed_mean, product_mean = (
                means[kind * images + image : kind * images + image + 1] for kind in range(4)
            )
            inv_std = 1.0 / jnp.sqrt(second - chan_mean * chan_mean + EPSILON)
            grad_mean = gain_row * passed_mean
            cross_mean = gain_row * (product_mean - chan_mean * passed_mean) * inv_std
            blocks = []
            for conv, grad in ((conv_ref, passed_ref), (theirs_ref.at[0], theirs_ref.at[1])):
                values, passed = conv[rows, :].astype(F32), grad[rows, :].astype(F32)
                normed = (values - chan_mean) * inv_std
                blocks.append(inv_std * (gain_row * passed - grad_mean - normed * cross_mean))
            even = jnp.where(first, blocks[0], blocks[1])
            odd = jnp.where(first, blocks[1], blocks[0])
            even_ref[rows, :] = even.astype(BF16)
            odd_ref[rows, :] = odd.astype(BF16)
            far_ref[rows, :] = jnp.where(early, odd, even).astype(BF16)

    out = jax.ShapeDtypeStruct((cells, half), BF16)
    return kernel_call(
        body,
        (place, gain, *sums, *mine, theirs),
        [SMEM, whole(gain.shape)] + [whole(sums[0].shape)] * 4 + [whole((cells, half))] * 2
        + [whole(theirs.shape)],
        [out] * 3,
        [whole(out.shape)] * 3,
    )


def padded_count(cells):
    return -(-cells // 128) * 128


def transposed(own, other):
    cells, channels = own.shape
    deep = padded_count(cells)
    width = 256

    def body(own_ref, other_ref, out_ref):
        for which, ref in enumerate((own_ref, other_ref)):
            block = jnp.concatenate([ref[...], jnp.zeros((deep - cells, width), BF16)], axis=0)
            out_ref[:, which * deep : (which + 1) * deep] = block.T

    spec = pl.BlockSpec((cells, width), lambda i: (0, i))
    return kernel_call(
        body,
        (own, other),
        [spec, spec],
        [jax.ShapeDtypeStruct((channels, 2 * deep), BF16)],
        [pl.BlockSpec((width, 2 * deep), lambda i: (i, 0))],
        (channels // width,),
    )[0]


def column_taps(block, col_count):
    cells, channels = block.shape
    wide = block.astype(F32)
    column = lax.broadcasted_iota(jnp.int32, (cells // col_count, col_count, channels), 1)
    column = column.reshape(cells, channels)
    before = jnp.where(column < col_count - RATE, pltpu.roll(wide, cells - RATE, 0), 0.0)
    after = jnp.where(column >= RATE, pltpu.roll(wide, RATE, 0), 0.0)
    return before.astype(BF16), block, after.astype(BF16)


def fill(stacked, slot, place, block, col_count):
    cells, width = block.shape
    deep = padded_count(cells)
    for spot, tap in enumerate(column_taps(block, col_count)):
        columns = slice((place + spot) * width, (place + spot + 1) * width)
        stacked[slot * deep : slot * deep + cells, columns] = tap


def clear_padding(stacked, cells):
    deep, columns = stacked.shape
    block = deep // 2
    for slot in range(2):
        stacked[slot * block + cells : (slot + 1) * block, :] = jnp.zeros((block - cells, columns), BF16)


def multiply(place_ref, lhs_ref, stacked, total, out_refs):
    columns = stacked.shape[1]
    product = jnp.dot(lhs_ref[...], stacked[...], preferred_element_type=F32)
    total[...] = product.reshape(total.shape)
    tall = total.shape[0] * 32

    @pl.when(core_of(place_ref) == 0)
    def _():
        for steps in range(Y):
            chunk = total[:, lax.rem(y_of(place_ref) + steps, Y), :, :, :]
            out_refs[steps][...] = chunk.reshape(tall, columns).astype(BF16)

    @pl.when(core_of(place_ref) != 0)
    def _():
        for steps in range(X):
            chunk = total[:, :, lax.rem(x_of(place_ref) + steps, X), :, :]
            out_refs[steps][...] = chunk.reshape(tall, columns).astype(BF16)


def product_call(body, place, fixed, lhs, columns, extra):
    channels_in, deep = lhs.shape
    steps = 2
    tall = channels_in // steps
    return kernel_call(
        body,
        (place, *fixed, lhs),
        [SMEM] + [whole(value.shape) for value in fixed] + [pl.BlockSpec((tall, deep), lambda i: (i, 0))],
        [jax.ShapeDtypeStruct((channels_in // 4, columns), BF16)] * 4 + extra,
        [pl.BlockSpec((tall // 4, columns), lambda i: (i, 0))] * 4 + [whole(value.shape) for value in extra],
        (steps,),
        [pltpu.VMEM((deep, columns), BF16), pltpu.VMEM((tall // 128, Y, X, 8, columns), F32)],
        flops=2 * channels_in * deep * columns,
        vmem=24,
    )


def middle_terms(place, even, odd, lhs, col_count):
    cells, width = even.shape

    def body(place_ref, even_ref, odd_ref, lhs_ref, *rest):
        stacked, total = rest[4:]

        @pl.when(pl.program_id(0) == 0)
        def _():
            clear_padding(stacked, cells)
            first = core_of(place_ref) == 0
            even_block, odd_block = even_ref[...], odd_ref[...]
            fill(stacked, 0, 0, jnp.where(first, even_block, odd_block), col_count)
            fill(stacked, 1, 0, jnp.where(first, odd_block, even_block), col_count)

        multiply(place_ref, lhs_ref, stacked, total, rest[:4])

    return product_call(body, place, [even, odd], lhs, 3 * width, [])


def tap_blocks(place_ref, even_ref, odd_ref, up_ref, down_ref, far_ref):
    x = x_of(place_ref)
    far_block = far_ref[...]
    zero = jnp.zeros_like(far_block)
    far_down = jnp.where(x < X // 2, far_block, zero)
    far_up = jnp.where(x < X // 2, zero, far_block)
    down_block = jnp.where(x < X - 1, down_ref[...], zero)
    up_block = jnp.where(x > 0, up_ref[...], zero)
    return (down_block, far_down), (even_ref[...], odd_ref[...]), (far_up, up_block)


def own_blocks(place, even, odd, up, down, far):
    operands = (even, odd, up, down, far)

    def body(place_ref, *refs):
        first = core_of(place_ref) == 0
        for side, (lower, upper) in enumerate(tap_blocks(place_ref, *refs[:5])):
            refs[5][side] = jnp.where(first, lower, upper)

    out = jax.ShapeDtypeStruct((3,) + even.shape, BF16)
    return kernel_call(
        body,
        (place, *operands),
        [SMEM] + [whole(value.shape) for value in operands],
        [out],
        [whole(out.shape)],
    )[0]


def side_terms(place, even, odd, up, down, far, lhs, col_count):
    cells, width = up.shape

    def body(place_ref, even_ref, odd_ref, up_ref, down_ref, far_ref, lhs_ref, *rest):
        theirs_ref, stacked, total = rest[4:]

        @pl.when(pl.program_id(0) == 0)
        def _():
            clear_padding(stacked, cells)
            first = core_of(place_ref) == 0
            blocks = tap_blocks(place_ref, even_ref, odd_ref, up_ref, down_ref, far_ref)
            for side, (lower, upper) in enumerate(blocks):
                theirs = jnp.where(first, upper, lower)
                theirs_ref[side] = theirs
                if side != 1:
                    mine = jnp.where(first, lower, upper)
                    fill(stacked, 0, 3 * (side // 2), mine, col_count)
                    fill(stacked, 1, 3 * (side // 2), theirs, col_count)

        multiply(place_ref, lhs_ref, stacked, total, rest[:4])

    triple = jax.ShapeDtypeStruct((3, cells, width), BF16)
    return product_call(body, place, [even, odd, up, down, far], lhs, 6 * width, [triple])


def first_sum(middle, sides):
    rows, third = middle[0].shape

    def body(*refs):
        out_ref = refs[-1]
        middle_total = sum(ref[...].astype(F32) for ref in refs[:4])
        side_total = sum(ref[...].astype(F32) for ref in refs[4:8])
        out_ref[:, :third] = side_total[:, :third].astype(BF16)
        out_ref[:, third : 2 * third] = middle_total.astype(BF16)
        out_ref[:, 2 * third :] = side_total[:, third:].astype(BF16)

    steps = 2
    spec = lambda columns: pl.BlockSpec((rows // steps, columns), lambda i: (i, 0))
    return kernel_call(
        body,
        (*middle, *sides),
        [spec(third)] * 4 + [spec(2 * third)] * 4,
        [jax.ShapeDtypeStruct((rows, 3 * third), BF16)],
        [spec(3 * third)],
        (steps,),
    )[0]


def input_gradient(place, held, got, weight, col_count):
    _, cells, half = held.shape
    deep, channels_in = weight.shape
    width = 256

    def body(place_ref, held_ref, got_ref, weight_ref, out_ref, stacked):

        @pl.when(pl.program_id(0) == 0)
        def _():
            first = core_of(place_ref) == 0
            for side in range(3):
                mine, theirs = held_ref[side], got_ref[side]
                lower, upper = jnp.where(first, mine, theirs), jnp.where(first, theirs, mine)
                for part, block in enumerate((lower, upper)):
                    for spot, tap in enumerate(column_taps(block, col_count)):
                        start = (2 * (3 * side + spot) + part) * half
                        stacked[:, start : start + half] = tap

        out_ref[...] = jnp.dot(
            stacked[...], weight_ref[...], preferred_element_type=F32
        ).astype(BF16)

    return kernel_call(
        body,
        (place, held, got, weight),
        [SMEM, whole(held.shape), whole(got.shape)] + [pl.BlockSpec((deep, width), lambda i: (0, i))],
        [jax.ShapeDtypeStruct((cells, channels_in), BF16)],
        [pl.BlockSpec((cells, width), lambda i: (0, i))],
        (channels_in // width,),
        [pltpu.VMEM((cells, deep), BF16)],
        2 * cells * deep * channels_in,
        60,
    )[0]


def per_device(inputs, conv_out, grad_out, relu_mask, norm_gain, weight):
    image_count, row_count, col_count, channels_in = inputs.shape
    channels_out = conv_out.shape[3]
    cell_count = row_count * col_count * X * CORES
    cells = image_count * row_count * col_count
    half = channels_out // 2
    core = lax.axis_index("core")
    place = jnp.reshape(lax.axis_index(AXES), (1,)).astype(jnp.int32)

    input_flat = inputs.reshape(cells, channels_in)
    sums = channel_sums(conv_out, grad_out, relu_mask)
    got_sums = swapped(sums)
    flat = [value.reshape(cells, channels_out) for value in (conv_out, grad_out, relu_mask)]
    sent = prepare(place, *flat)
    input_flat, sent, got_sums = lax.optimization_barrier((input_flat, sent, got_sums))
    theirs = swapped(sent)
    input_other = swapped(input_flat)
    sums = sums + got_sums
    conv_half, grad_half, mask_half = (
        lax.dynamic_slice_in_dim(value, core * half, half, axis=1) for value in flat
    )
    mine = [conv_half, (grad_half.astype(F32) * mask_half.astype(F32)).astype(BF16)]
    sums = [sums] + [around(sums, steps) for steps in (2, 1, 3)]
    lhs = transposed(input_flat, input_other)
    gain = norm_gain.reshape(1, channels_out)
    even, odd, far = pre_gradient(place, gain, sums, mine, theirs, image_count, cell_count)
    far = around(far, 2)
    up = around(even, 1)
    down = around(odd, X - 1)

    middle = list(middle_terms(place, even, odd, lhs, col_count))
    side_place, middle[0] = lax.optimization_barrier((place, middle[0]))
    middle = [middle[0]] + [crossed(middle[steps], steps) for steps in (2, 1, 3)]
    *sides, sent = side_terms(side_place, even, odd, up, down, far, lhs, col_count)
    sides[1:], sent, middle[1:] = lax.optimization_barrier((sides[1:], sent, middle[1:]))
    got = swapped(sent)
    weight, sides[0] = lax.optimization_barrier((weight, sides[0]))
    weight = jnp.transpose(weight, (1, 2, 0)).reshape(9 * channels_out, channels_in)
    sides = [sides[0]] + [crossed(sides[steps], steps) for steps in (2, 1, 3)]
    held_place, weight = lax.optimization_barrier((place, weight))
    held = own_blocks(held_place, even, odd, up, down, far)
    sides, weight, held = lax.optimization_barrier((sides, weight, held))
    merged = first_sum(middle, sides)
    place, merged = lax.optimization_barrier((place, merged))
    input_grad = input_gradient(place, held, got, weight, col_count)
    merged = exchanged(merged.reshape(Z * 4, 8, 9 * half))
    merged, input_grad = lax.optimization_barrier((merged, input_grad))
    inv_images = 1.0 / (image_count * Z * Y)
    merged = jnp.sum(merged.astype(F32), axis=0) * inv_images
    rows = merged.shape[0] // CORES
    kept = lax.dynamic_slice_in_dim(merged, core * rows, rows, axis=0)
    came = swapped(lax.dynamic_slice_in_dim(merged, (1 - core) * rows, rows, axis=0))
    kept, came = kept.reshape(rows, 9, half), came.reshape(rows, 9, half)
    weight_grad = jnp.concatenate(
        [jnp.where(core == 0, kept, came), jnp.where(core == 0, came, kept)], axis=2
    )

    return (input_grad.reshape(inputs.shape), weight_grad)


def solution(mesh):
    parted = Mesh(mesh.devices.reshape(Z, Y, X, CORES), AXES)
    cells = P(("z", "y"), ("x", "core"), None, None)
    return jax.shard_map(
        per_device,
        mesh=parted,
        in_specs=(cells, cells, cells, cells, P(), P()),
        out_specs=(cells, P(AXES, None, None)),
        check_vma=False,
    )
```

```python
import jax
import jax.numpy as jnp
from jax import lax
from jax.experimental import pallas as pl
from jax.experimental.pallas import tpu as pltpu
from jax.sharding import Mesh, PartitionSpec as P

RATE = 18
EPSILON = 1e-05
F32 = jnp.float32
BF16 = jnp.bfloat16
MIB = 1024 * 1024
AXES = ("z", "y", "x", "core")
Z, Y, X, CORES = 8, 4, 4, 2
SMEM = pl.BlockSpec(memory_space=pltpu.SMEM)


def device(z, y, x, core):
    return ((z * Y + y) * X + x) * CORES + core


def core_of(place_ref):
    return lax.rem(place_ref[0], CORES)


def x_of(place_ref):
    return lax.rem(lax.div(place_ref[0], CORES), X)


def y_of(place_ref):
    return lax.rem(lax.div(place_ref[0], CORES * X), Y)


def swapped(value):
    return lax.ppermute(value, "core", [(0, 1), (1, 0)])


def around(value, steps):
    return lax.ppermute(value, "x", [(source, (source + steps) % X) for source in range(X)])


def crossed(value, steps):
    pairs = []
    for z in range(Z):
        for y in range(Y):
            for x in range(X):
                pairs.append((device(z, y, x, 0), device(z, (y + steps) % Y, x, 0)))
                pairs.append((device(z, y, x, 1), device(z, y, (x + steps) % X, 1)))
    return lax.ppermute(value, AXES, pairs)


def exchanged(value):
    groups = [[device(z, y, x, 0) for z in range(Z) for x in range(X)] for y in range(Y)]
    groups += [[device(z, y, x, 1) for z in range(Z) for y in range(Y)] for x in range(X)]
    return lax.all_to_all(value, AXES, 0, 0, axis_index_groups=groups)


def whole(shape):
    return pl.BlockSpec(shape, lambda *_: (0,) * len(shape))


def kernel_call(body, operands, in_specs, out_shape, out_specs, grid=(1,), scratch=(), flops=0, vmem=8):
    moved = sum(value.size * value.dtype.itemsize for value in operands)
    moved += sum(value.size * value.dtype.itemsize for value in out_shape)
    return pl.pallas_call(
        body,
        grid=grid,
        in_specs=in_specs,
        out_specs=out_specs,
        out_shape=out_shape,
        scratch_shapes=list(scratch),
        compiler_params=pltpu.CompilerParams(vmem_limit_bytes=vmem * MIB),
        cost_estimate=pl.CostEstimate(flops=flops, bytes_accessed=moved, transcendentals=0),
    )(*operands)


def channel_sums(conv, grad, mask):
    values = conv.astype(F32)
    passed = grad.astype(F32) * mask.astype(F32)
    terms = (values, values * values, passed, passed * values)
    return jnp.stack([jnp.sum(term, axis=(1, 2)) for term in terms]).reshape(-1, conv.shape[3])


def prepare(place, conv, grad, mask):
    cells, channels = conv.shape
    half = channels // 2
    steps = 2
    tall = cells // steps

    def body(place_ref, conv_ref, grad_ref, mask_ref, mine_ref, sent_ref):
        first = core_of(place_ref) == 0
        passed = (grad_ref[...].astype(F32) * mask_ref[...].astype(F32)).astype(BF16)
        for which, value in enumerate((conv_ref[...], passed)):
            lower, upper = value[:, :half], value[:, half:]
            mine_ref[which] = jnp.where(first, lower, upper)
            sent_ref[which] = jnp.where(first, upper, lower)

    rows = pl.BlockSpec((tall, channels), lambda i: (i, 0))
    out = jax.ShapeDtypeStruct((2, cells, half), BF16)
    spec = pl.BlockSpec((2, tall, half), lambda i: (0, i, 0))
    return kernel_call(
        body,
        (place, conv, grad, mask),
        [SMEM, rows, rows, rows],
        [out, out],
        [spec, spec],
        (steps,),
        vmem=60,
    )


def pre_gradient(token, place, gain, sums, mine, theirs, images, cell_count):
    _, cells, half = mine.shape
    each = cells // images

    def body(_, place_ref, gain_ref, a_ref, b_ref, c_ref, d_ref, mine_ref, theirs_ref, even_ref, odd_ref, far_ref):
        first = core_of(place_ref) == 0
        early = x_of(place_ref) < X // 2
        means = (a_ref[...] + b_ref[...] + c_ref[...] + d_ref[...]) / cell_count
        means = jnp.where(first, means[:, :half], means[:, half:])
        gain_row = jnp.where(first, gain_ref[:, :half], gain_ref[:, half:])
        for image in range(images):
            rows = pl.ds(image * each, each)
            chan_mean, second, passed_mean, product_mean = (
                means[kind * images + image : kind * images + image + 1] for kind in range(4)
            )
            inv_std = 1.0 / jnp.sqrt(second - chan_mean * chan_mean + EPSILON)
            grad_mean = gain_row * passed_mean
            cross_mean = gain_row * (product_mean - chan_mean * passed_mean) * inv_std
            blocks = []
            for ref in (mine_ref, theirs_ref):
                values, passed = ref[0, rows, :].astype(F32), ref[1, rows, :].astype(F32)
                normed = (values - chan_mean) * inv_std
                blocks.append(inv_std * (gain_row * passed - grad_mean - normed * cross_mean))
            even = jnp.where(first, blocks[0], blocks[1])
            odd = jnp.where(first, blocks[1], blocks[0])
            even_ref[rows, :] = even.astype(BF16)
            odd_ref[rows, :] = odd.astype(BF16)
            far_ref[rows, :] = jnp.where(early, odd, even).astype(BF16)

    out = jax.ShapeDtypeStruct((cells, half), BF16)
    return kernel_call(
        body,
        (token, place, gain, *sums, mine, theirs),
        [whole(token.shape), SMEM, whole(gain.shape)] + [whole(sums[0].shape)] * 4 + [whole(mine.shape)] * 2,
        [out] * 3,
        [whole(out.shape)] * 3,
    )


def padded_count(cells):
    return -(-cells // 128) * 128


def transposed(own, other):
    cells, channels = own.shape
    deep = padded_count(cells)
    width = 256

    def body(own_ref, other_ref, out_ref, token_ref):
        token_ref[...] = jnp.zeros_like(token_ref)
        for which, ref in enumerate((own_ref, other_ref)):
            block = jnp.concatenate([ref[...], jnp.zeros((deep - cells, width), BF16)], axis=0)
            out_ref[:, which * deep : (which + 1) * deep] = block.T

    spec = pl.BlockSpec((cells, width), lambda i: (0, i))
    return kernel_call(
        body,
        (own, other),
        [spec, spec],
        [jax.ShapeDtypeStruct((channels, 2 * deep), BF16), jax.ShapeDtypeStruct((8, 128), F32)],
        [pl.BlockSpec((width, 2 * deep), lambda i: (i, 0)), whole((8, 128))],
        (channels // width,),
    )


def column_taps(block, col_count):
    cells, channels = block.shape
    wide = block.astype(F32)
    column = lax.broadcasted_iota(jnp.int32, (cells // col_count, col_count, channels), 1)
    column = column.reshape(cells, channels)
    before = jnp.where(column < col_count - RATE, pltpu.roll(wide, cells - RATE, 0), 0.0)
    after = jnp.where(column >= RATE, pltpu.roll(wide, RATE, 0), 0.0)
    return before.astype(BF16), block, after.astype(BF16)


def fill(stacked, slot, place, block, col_count):
    cells, width = block.shape
    deep = padded_count(cells)
    for spot, tap in enumerate(column_taps(block, col_count)):
        columns = slice((place + spot) * width, (place + spot + 1) * width)
        stacked[slot * deep : slot * deep + cells, columns] = tap


def clear_padding(stacked, cells):
    deep, columns = stacked.shape
    block = deep // 2
    for slot in range(2):
        stacked[slot * block + cells : (slot + 1) * block, :] = jnp.zeros((block - cells, columns), BF16)


def multiply(place_ref, lhs_ref, stacked, total, out_refs):
    columns = stacked.shape[1]
    product = jnp.dot(lhs_ref[...], stacked[...], preferred_element_type=F32)
    total[...] = product.reshape(total.shape)
    tall = total.shape[0] * 32

    @pl.when(core_of(place_ref) == 0)
    def _():
        for steps in range(Y):
            chunk = total[:, lax.rem(y_of(place_ref) + steps, Y), :, :, :]
            out_refs[steps][...] = chunk.reshape(tall, columns).astype(BF16)

    @pl.when(core_of(place_ref) != 0)
    def _():
        for steps in range(X):
            chunk = total[:, :, lax.rem(x_of(place_ref) + steps, X), :, :]
            out_refs[steps][...] = chunk.reshape(tall, columns).astype(BF16)


def product_call(body, place, fixed, lhs, columns, extra):
    channels_in, deep = lhs.shape
    steps = 2
    tall = channels_in // steps
    return kernel_call(
        body,
        (place, *fixed, lhs),
        [SMEM] + [whole(value.shape) for value in fixed] + [pl.BlockSpec((tall, deep), lambda i: (i, 0))],
        [jax.ShapeDtypeStruct((channels_in // 4, columns), BF16)] * 4 + extra,
        [pl.BlockSpec((tall // 4, columns), lambda i: (i, 0))] * 4 + [whole(value.shape) for value in extra],
        (steps,),
        [pltpu.VMEM((deep, columns), BF16), pltpu.VMEM((tall // 128, Y, X, 8, columns), F32)],
        flops=2 * channels_in * deep * columns,
        vmem=24,
    )


def middle_terms(place, even, odd, lhs, col_count):
    cells, width = even.shape

    def body(place_ref, even_ref, odd_ref, lhs_ref, *rest):
        stacked, total = rest[4:]

        @pl.when(pl.program_id(0) == 0)
        def _():
            clear_padding(stacked, cells)
            first = core_of(place_ref) == 0
            even_block, odd_block = even_ref[...], odd_ref[...]
            fill(stacked, 0, 0, jnp.where(first, even_block, odd_block), col_count)
            fill(stacked, 1, 0, jnp.where(first, odd_block, even_block), col_count)

        multiply(place_ref, lhs_ref, stacked, total, rest[:4])

    return product_call(body, place, [even, odd], lhs, 3 * width, [])


def tap_blocks(place_ref, even_ref, odd_ref, far_ref, up_ref, down_ref):
    x = x_of(place_ref)
    far_block = far_ref[...]
    zero = jnp.zeros_like(far_block)
    far_down = jnp.where(x < X // 2, far_block, zero)
    far_up = jnp.where(x < X // 2, zero, far_block)
    down_block = jnp.where(x < X - 1, down_ref[...], zero)
    up_block = jnp.where(x > 0, up_ref[...], zero)
    return (down_block, far_down), (even_ref[...], odd_ref[...]), (far_up, up_block)


def own_blocks(place, even, odd, far, up, down):
    operands = (even, odd, far, up, down)

    def body(place_ref, *refs):
        first = core_of(place_ref) == 0
        for side, (lower, upper) in enumerate(tap_blocks(place_ref, *refs[:5])):
            refs[5][side] = jnp.where(first, lower, upper)

    out = jax.ShapeDtypeStruct((3,) + even.shape, BF16)
    return kernel_call(
        body,
        (place, *operands),
        [SMEM] + [whole(value.shape) for value in operands],
        [out],
        [whole(out.shape)],
    )[0]


def side_terms(place, even, odd, far, up, down, lhs, col_count):
    cells, width = up.shape

    def body(place_ref, even_ref, odd_ref, far_ref, up_ref, down_ref, lhs_ref, *rest):
        theirs_refs = rest[4:6]
        stacked, total = rest[6:]

        @pl.when(pl.program_id(0) == 0)
        def _():
            clear_padding(stacked, cells)
            first = core_of(place_ref) == 0
            blocks = tap_blocks(place_ref, even_ref, odd_ref, far_ref, up_ref, down_ref)
            for side, (lower, upper) in enumerate(blocks):
                theirs = jnp.where(first, upper, lower)
                for part, ref in enumerate(theirs_refs):
                    ref[side] = theirs[part * (cells // 2) : (part + 1) * (cells // 2)]
                if side != 1:
                    mine = jnp.where(first, lower, upper)
                    fill(stacked, 0, 3 * (side // 2), mine, col_count)
                    fill(stacked, 1, 3 * (side // 2), theirs, col_count)

        multiply(place_ref, lhs_ref, stacked, total, rest[:4])

    part = jax.ShapeDtypeStruct((3, cells // 2, width), BF16)
    return product_call(body, place, [even, odd, far, up, down], lhs, 6 * width, [part, part])


def first_sum(middle, sides):
    rows, third = middle[0].shape

    def body(*refs):
        out_ref = refs[-1]
        middle_total = sum(ref[...].astype(F32) for ref in refs[:4])
        side_total = sum(ref[...].astype(F32) for ref in refs[4:8])
        out_ref[:, :third] = side_total[:, :third].astype(BF16)
        out_ref[:, third : 2 * third] = middle_total.astype(BF16)
        out_ref[:, 2 * third :] = side_total[:, third:].astype(BF16)

    steps = 2
    spec = lambda columns: pl.BlockSpec((rows // steps, columns), lambda i: (i, 0))
    return kernel_call(
        body,
        (*middle, *sides),
        [spec(third)] * 4 + [spec(2 * third)] * 4,
        [jax.ShapeDtypeStruct((rows, 3 * third), BF16)],
        [spec(3 * third)],
        (steps,),
    )[0]


def input_gradient(place, held, got, weight, col_count):
    _, cells, half = held.shape
    deep, channels_in = weight.shape
    width = 256

    def body(place_ref, held_ref, *rest):
        got_refs, (weight_ref, out_ref, stacked) = rest[:2], rest[2:]

        @pl.when(pl.program_id(0) == 0)
        def _():
            first = core_of(place_ref) == 0
            for side in range(3):
                mine = held_ref[side]
                theirs = jnp.concatenate([ref[side] for ref in got_refs], axis=0)
                lower, upper = jnp.where(first, mine, theirs), jnp.where(first, theirs, mine)
                for part, block in enumerate((lower, upper)):
                    for spot, tap in enumerate(column_taps(block, col_count)):
                        start = (2 * (3 * side + spot) + part) * half
                        stacked[:, start : start + half] = tap

        out_ref[...] = jnp.dot(
            stacked[...], weight_ref[...], preferred_element_type=F32
        ).astype(BF16)

    return kernel_call(
        body,
        (place, held, *got, weight),
        [SMEM, whole(held.shape)] + [whole(block.shape) for block in got] + [pl.BlockSpec((deep, width), lambda i: (0, i))],
        [jax.ShapeDtypeStruct((cells, channels_in), BF16)],
        [pl.BlockSpec((cells, width), lambda i: (0, i))],
        (channels_in // width,),
        [pltpu.VMEM((cells, deep), BF16)],
        2 * cells * deep * channels_in,
        60,
    )[0]


def per_device(inputs, conv_out, grad_out, relu_mask, norm_gain, weight):
    image_count, row_count, col_count, channels_in = inputs.shape
    channels_out = conv_out.shape[3]
    cell_count = row_count * col_count * X * CORES
    cells = image_count * row_count * col_count
    half = channels_out // 2
    core = lax.axis_index("core")
    place = jnp.reshape(lax.axis_index(AXES), (1,)).astype(jnp.int32)

    input_flat = inputs.reshape(cells, channels_in)
    sums = channel_sums(conv_out, grad_out, relu_mask)
    got_sums = swapped(sums)
    mine, sent = prepare(
        place,
        *(value.reshape(cells, channels_out) for value in (conv_out, grad_out, relu_mask)),
    )
    input_flat, sent, got_sums = lax.optimization_barrier((input_flat, sent, got_sums))
    theirs = swapped(sent)
    input_other = swapped(input_flat)
    sums = sums + got_sums
    sums = [sums] + [around(sums, steps) for steps in (2, 1, 3)]
    lhs, token = transposed(input_flat, input_other)
    gain = norm_gain.reshape(1, channels_out)
    even, odd, far = pre_gradient(token, place, gain, sums, mine, theirs, image_count, cell_count)
    far = around(far, 2)
    up = around(even, 1)
    down = around(odd, X - 1)

    middle = list(middle_terms(place, even, odd, lhs, col_count))
    side_place, middle[0] = lax.optimization_barrier((place, middle[0]))
    middle = [middle[0]] + [crossed(middle[steps], steps) for steps in (2, 1, 3)]
    *sides, sent_lower, sent_upper = side_terms(side_place, even, odd, far, up, down, lhs, col_count)
    sent = [sent_lower, sent_upper]
    sides[1:], sent, middle[1:] = lax.optimization_barrier((sides[1:], sent, middle[1:]))
    got = [swapped(block) for block in sent]
    weight, sides[0] = lax.optimization_barrier((weight, sides[0]))
    weight = jnp.transpose(weight, (1, 2, 0)).reshape(9 * channels_out, channels_in)
    sides = [sides[0]] + [crossed(sides[steps], steps) for steps in (2, 1, 3)]
    held_place, weight = lax.optimization_barrier((place, weight))
    held = own_blocks(held_place, even, odd, far, up, down)
    sides, weight, got, held = lax.optimization_barrier((sides, weight, got, held))
    merged = first_sum(middle, sides)
    place, merged = lax.optimization_barrier((place, merged))
    input_grad = input_gradient(place, held, got, weight, col_count)
    merged = exchanged(merged.reshape(Z * 4, 8, 9 * half))
    merged, input_grad = lax.optimization_barrier((merged, input_grad))
    inv_images = 1.0 / (image_count * Z * Y)
    merged = jnp.sum(merged.astype(F32), axis=0) * inv_images
    rows = merged.shape[0] // CORES
    kept = lax.dynamic_slice_in_dim(merged, core * rows, rows, axis=0)
    came = swapped(lax.dynamic_slice_in_dim(merged, (1 - core) * rows, rows, axis=0))
    kept, came = kept.reshape(rows, 9, half), came.reshape(rows, 9, half)
    weight_grad = jnp.concatenate(
        [jnp.where(core == 0, kept, came), jnp.where(core == 0, came, kept)], axis=2
    )

    return (input_grad.reshape(inputs.shape), weight_grad)


def solution(mesh):
    parted = Mesh(mesh.devices.reshape(Z, Y, X, CORES), AXES)
    cells = P(("z", "y"), ("x", "core"), None, None)
    return jax.shard_map(
        per_device,
        mesh=parted,
        in_specs=(cells, cells, cells, cells, P(), P()),
        out_specs=(cells, P(AXES, None, None)),
        check_vma=False,
    )
```

```python
import jax
import jax.numpy as jnp
from jax import lax
from jax.experimental import pallas as pl
from jax.experimental.pallas import tpu as pltpu
from jax.sharding import Mesh, PartitionSpec as P

RATE = 18
EPSILON = 1e-05
F32 = jnp.float32
BF16 = jnp.bfloat16
MIB = 1024 * 1024
AXES = ("z", "y", "x", "core")
Z, Y, X, CORES = 8, 4, 4, 2
SMEM = pl.BlockSpec(memory_space=pltpu.SMEM)


def device(z, y, x, core):
    return ((z * Y + y) * X + x) * CORES + core


def core_of(place_ref):
    return lax.rem(place_ref[0], CORES)


def x_of(place_ref):
    return lax.rem(lax.div(place_ref[0], CORES), X)


def y_of(place_ref):
    return lax.rem(lax.div(place_ref[0], CORES * X), Y)


def swapped(value):
    return lax.ppermute(value, "core", [(0, 1), (1, 0)])


def around(value, steps):
    return lax.ppermute(value, "x", [(source, (source + steps) % X) for source in range(X)])


def crossed(value, steps):
    pairs = []
    for z in range(Z):
        for y in range(Y):
            for x in range(X):
                pairs.append((device(z, y, x, 0), device(z, (y + steps) % Y, x, 0)))
                pairs.append((device(z, y, x, 1), device(z, y, (x + steps) % X, 1)))
    return lax.ppermute(value, AXES, pairs)


def exchanged(value):
    groups = [[device(z, y, x, 0) for z in range(Z) for x in range(X)] for y in range(Y)]
    groups += [[device(z, y, x, 1) for z in range(Z) for y in range(Y)] for x in range(X)]
    return lax.all_to_all(value, AXES, 0, 0, axis_index_groups=groups)


def whole(shape):
    return pl.BlockSpec(shape, lambda *_: (0,) * len(shape))


def kernel_call(body, operands, in_specs, out_shape, out_specs, grid=(1,), scratch=(), flops=0, vmem=8):
    moved = sum(value.size * value.dtype.itemsize for value in operands)
    moved += sum(value.size * value.dtype.itemsize for value in out_shape)
    return pl.pallas_call(
        body,
        grid=grid,
        in_specs=in_specs,
        out_specs=out_specs,
        out_shape=out_shape,
        scratch_shapes=list(scratch),
        compiler_params=pltpu.CompilerParams(vmem_limit_bytes=vmem * MIB),
        cost_estimate=pl.CostEstimate(flops=flops, bytes_accessed=moved, transcendentals=0),
    )(*operands)


def channel_sums(conv, grad, mask):
    values = conv.astype(F32)
    passed = grad.astype(F32) * mask.astype(F32)
    terms = (values, values * values, passed, passed * values)
    return jnp.stack([jnp.sum(term, axis=(1, 2)) for term in terms]).reshape(-1, conv.shape[3])


def prepare(place, conv, grad, mask):
    cells, channels = conv.shape
    half = channels // 2
    steps = 2
    tall = cells // steps

    def body(place_ref, conv_ref, grad_ref, mask_ref, mine_ref, sent_ref):
        first = core_of(place_ref) == 0
        passed = (grad_ref[...].astype(F32) * mask_ref[...].astype(F32)).astype(BF16)
        for which, value in enumerate((conv_ref[...], passed)):
            lower, upper = value[:, :half], value[:, half:]
            mine_ref[which] = jnp.where(first, lower, upper)
            sent_ref[which] = jnp.where(first, upper, lower)

    rows = pl.BlockSpec((tall, channels), lambda i: (i, 0))
    out = jax.ShapeDtypeStruct((2, cells, half), BF16)
    spec = pl.BlockSpec((2, tall, half), lambda i: (0, i, 0))
    return kernel_call(
        body,
        (place, conv, grad, mask),
        [SMEM, rows, rows, rows],
        [out, out],
        [spec, spec],
        (steps,),
        vmem=60,
    )


def pre_gradient(token, place, gain, sums, mine, theirs, images, cell_count):
    _, cells, half = mine.shape
    each = cells // images

    def body(_, place_ref, gain_ref, a_ref, b_ref, c_ref, d_ref, mine_ref, theirs_ref, even_ref, odd_ref, far_ref):
        first = core_of(place_ref) == 0
        early = x_of(place_ref) < X // 2
        means = (a_ref[...] + b_ref[...] + c_ref[...] + d_ref[...]) / cell_count
        means = jnp.where(first, means[:, :half], means[:, half:])
        gain_row = jnp.where(first, gain_ref[:, :half], gain_ref[:, half:])
        for image in range(images):
            rows = pl.ds(image * each, each)
            chan_mean, second, passed_mean, product_mean = (
                means[kind * images + image : kind * images + image + 1] for kind in range(4)
            )
            inv_std = 1.0 / jnp.sqrt(second - chan_mean * chan_mean + EPSILON)
            grad_mean = gain_row * passed_mean
            cross_mean = gain_row * (product_mean - chan_mean * passed_mean) * inv_std
            blocks = []
            for ref in (mine_ref, theirs_ref):
                values, passed = ref[0, rows, :].astype(F32), ref[1, rows, :].astype(F32)
                normed = (values - chan_mean) * inv_std
                blocks.append(inv_std * (gain_row * passed - grad_mean - normed * cross_mean))
            even = jnp.where(first, blocks[0], blocks[1])
            odd = jnp.where(first, blocks[1], blocks[0])
            even_ref[rows, :] = even.astype(BF16)
            odd_ref[rows, :] = odd.astype(BF16)
            far_ref[rows, :] = jnp.where(early, odd, even).astype(BF16)

    out = jax.ShapeDtypeStruct((cells, half), BF16)
    return kernel_call(
        body,
        (token, place, gain, *sums, mine, theirs),
        [whole(token.shape), SMEM, whole(gain.shape)] + [whole(sums[0].shape)] * 4 + [whole(mine.shape)] * 2,
        [out] * 3,
        [whole(out.shape)] * 3,
    )


def padded_count(cells):
    return -(-cells // 128) * 128


def transposed(own, other):
    cells, channels = own.shape
    deep = padded_count(cells)
    width = 256

    def body(own_ref, other_ref, out_ref, token_ref):
        token_ref[...] = jnp.zeros_like(token_ref)
        for which, ref in enumerate((own_ref, other_ref)):
            block = jnp.concatenate([ref[...], jnp.zeros((deep - cells, width), BF16)], axis=0)
            out_ref[:, which * deep : (which + 1) * deep] = block.T

    spec = pl.BlockSpec((cells, width), lambda i: (0, i))
    return kernel_call(
        body,
        (own, other),
        [spec, spec],
        [jax.ShapeDtypeStruct((channels, 2 * deep), BF16), jax.ShapeDtypeStruct((8, 128), F32)],
        [pl.BlockSpec((width, 2 * deep), lambda i: (i, 0)), whole((8, 128))],
        (channels // width,),
    )


def column_taps(block, col_count):
    cells, channels = block.shape
    wide = block.astype(F32)
    column = lax.broadcasted_iota(jnp.int32, (cells // col_count, col_count, channels), 1)
    column = column.reshape(cells, channels)
    before = jnp.where(column < col_count - RATE, pltpu.roll(wide, cells - RATE, 0), 0.0)
    after = jnp.where(column >= RATE, pltpu.roll(wide, RATE, 0), 0.0)
    return before.astype(BF16), block, after.astype(BF16)


def fill(stacked, slot, place, block, col_count):
    cells, width = block.shape
    deep = padded_count(cells)
    for spot, tap in enumerate(column_taps(block, col_count)):
        columns = slice((place + spot) * width, (place + spot + 1) * width)
        stacked[slot * deep : slot * deep + cells, columns] = tap


def clear_padding(stacked, cells):
    deep, columns = stacked.shape
    block = deep // 2
    for slot in range(2):
        stacked[slot * block + cells : (slot + 1) * block, :] = jnp.zeros((block - cells, columns), BF16)


def multiply(place_ref, lhs_ref, stacked, total, out_refs):
    columns = stacked.shape[1]
    product = jnp.dot(lhs_ref[...], stacked[...], preferred_element_type=F32)
    total[...] = product.reshape(total.shape)
    tall = total.shape[0] * 32

    @pl.when(core_of(place_ref) == 0)
    def _():
        for steps in range(Y):
            chunk = total[:, lax.rem(y_of(place_ref) + steps, Y), :, :, :]
            out_refs[steps][...] = chunk.reshape(tall, columns).astype(BF16)

    @pl.when(core_of(place_ref) != 0)
    def _():
        for steps in range(X):
            chunk = total[:, :, lax.rem(x_of(place_ref) + steps, X), :, :]
            out_refs[steps][...] = chunk.reshape(tall, columns).astype(BF16)


def product_call(body, place, fixed, lhs, columns, extra):
    channels_in, deep = lhs.shape
    steps = 2
    tall = channels_in // steps
    return kernel_call(
        body,
        (place, *fixed, lhs),
        [SMEM] + [whole(value.shape) for value in fixed] + [pl.BlockSpec((tall, deep), lambda i: (i, 0))],
        [jax.ShapeDtypeStruct((channels_in // 4, columns), BF16)] * 4 + extra,
        [pl.BlockSpec((tall // 4, columns), lambda i: (i, 0))] * 4 + [whole(value.shape) for value in extra],
        (steps,),
        [pltpu.VMEM((deep, columns), BF16), pltpu.VMEM((tall // 128, Y, X, 8, columns), F32)],
        flops=2 * channels_in * deep * columns,
        vmem=24,
    )


def middle_terms(place, even, odd, lhs, col_count):
    cells, width = even.shape

    def body(place_ref, even_ref, odd_ref, lhs_ref, *rest):
        stacked, total = rest[4:]

        @pl.when(pl.program_id(0) == 0)
        def _():
            clear_padding(stacked, cells)
            first = core_of(place_ref) == 0
            even_block, odd_block = even_ref[...], odd_ref[...]
            fill(stacked, 0, 0, jnp.where(first, even_block, odd_block), col_count)
            fill(stacked, 1, 0, jnp.where(first, odd_block, even_block), col_count)

        multiply(place_ref, lhs_ref, stacked, total, rest[:4])

    return product_call(body, place, [even, odd], lhs, 3 * width, [])


def tap_blocks(place_ref, even_ref, odd_ref, up_ref, down_ref, far_ref):
    x = x_of(place_ref)
    far_block = far_ref[...]
    zero = jnp.zeros_like(far_block)
    far_down = jnp.where(x < X // 2, far_block, zero)
    far_up = jnp.where(x < X // 2, zero, far_block)
    down_block = jnp.where(x < X - 1, down_ref[...], zero)
    up_block = jnp.where(x > 0, up_ref[...], zero)
    return (down_block, far_down), (even_ref[...], odd_ref[...]), (far_up, up_block)


def own_blocks(place, even, odd, up, down, far):
    operands = (even, odd, up, down, far)

    def body(place_ref, *refs):
        first = core_of(place_ref) == 0
        for side, (lower, upper) in enumerate(tap_blocks(place_ref, *refs[:5])):
            refs[5][side] = jnp.where(first, lower, upper)

    out = jax.ShapeDtypeStruct((3,) + even.shape, BF16)
    return kernel_call(
        body,
        (place, *operands),
        [SMEM] + [whole(value.shape) for value in operands],
        [out],
        [whole(out.shape)],
    )[0]


def side_terms(place, even, odd, up, down, far, lhs, col_count):
    cells, width = up.shape

    def body(place_ref, even_ref, odd_ref, up_ref, down_ref, far_ref, lhs_ref, *rest):
        theirs_refs = rest[4:6]
        stacked, total = rest[6:]

        @pl.when(pl.program_id(0) == 0)
        def _():
            clear_padding(stacked, cells)
            first = core_of(place_ref) == 0
            blocks = tap_blocks(place_ref, even_ref, odd_ref, up_ref, down_ref, far_ref)
            for side, (lower, upper) in enumerate(blocks):
                theirs = jnp.where(first, upper, lower)
                for part, ref in enumerate(theirs_refs):
                    ref[side] = theirs[part * (cells // 2) : (part + 1) * (cells // 2)]
                if side != 1:
                    mine = jnp.where(first, lower, upper)
                    fill(stacked, 0, 3 * (side // 2), mine, col_count)
                    fill(stacked, 1, 3 * (side // 2), theirs, col_count)

        multiply(place_ref, lhs_ref, stacked, total, rest[:4])

    part = jax.ShapeDtypeStruct((3, cells // 2, width), BF16)
    return product_call(body, place, [even, odd, up, down, far], lhs, 6 * width, [part, part])


def first_sum(middle, sides):
    rows, third = middle[0].shape

    def body(*refs):
        out_ref = refs[-1]
        middle_total = sum(ref[...].astype(F32) for ref in refs[:4])
        side_total = sum(ref[...].astype(F32) for ref in refs[4:8])
        out_ref[:, :third] = side_total[:, :third].astype(BF16)
        out_ref[:, third : 2 * third] = middle_total.astype(BF16)
        out_ref[:, 2 * third :] = side_total[:, third:].astype(BF16)

    steps = 2
    spec = lambda columns: pl.BlockSpec((rows // steps, columns), lambda i: (i, 0))
    return kernel_call(
        body,
        (*middle, *sides),
        [spec(third)] * 4 + [spec(2 * third)] * 4,
        [jax.ShapeDtypeStruct((rows, 3 * third), BF16)],
        [spec(3 * third)],
        (steps,),
    )[0]


def input_gradient(place, held, got, weight, col_count):
    _, cells, half = held.shape
    deep, channels_in = weight.shape
    width = 256

    def body(place_ref, held_ref, *rest):
        got_refs, (weight_ref, out_ref, stacked) = rest[:2], rest[2:]

        @pl.when(pl.program_id(0) == 0)
        def _():
            first = core_of(place_ref) == 0
            for side in range(3):
                mine = held_ref[side]
                theirs = jnp.concatenate([ref[side] for ref in got_refs], axis=0)
                lower, upper = jnp.where(first, mine, theirs), jnp.where(first, theirs, mine)
                for part, block in enumerate((lower, upper)):
                    for spot, tap in enumerate(column_taps(block, col_count)):
                        start = (2 * (3 * side + spot) + part) * half
                        stacked[:, start : start + half] = tap

        out_ref[...] = jnp.dot(
            stacked[...], weight_ref[...], preferred_element_type=F32
        ).astype(BF16)

    return kernel_call(
        body,
        (place, held, *got, weight),
        [SMEM, whole(held.shape)] + [whole(block.shape) for block in got] + [pl.BlockSpec((deep, width), lambda i: (0, i))],
        [jax.ShapeDtypeStruct((cells, channels_in), BF16)],
        [pl.BlockSpec((cells, width), lambda i: (0, i))],
        (channels_in // width,),
        [pltpu.VMEM((cells, deep), BF16)],
        2 * cells * deep * channels_in,
        60,
    )[0]


def per_device(inputs, conv_out, grad_out, relu_mask, norm_gain, weight):
    image_count, row_count, col_count, channels_in = inputs.shape
    channels_out = conv_out.shape[3]
    cell_count = row_count * col_count * X * CORES
    cells = image_count * row_count * col_count
    half = channels_out // 2
    core = lax.axis_index("core")
    place = jnp.reshape(lax.axis_index(AXES), (1,)).astype(jnp.int32)

    input_flat = inputs.reshape(cells, channels_in)
    sums = channel_sums(conv_out, grad_out, relu_mask)
    got_sums = swapped(sums)
    mine, sent = prepare(
        place,
        *(value.reshape(cells, channels_out) for value in (conv_out, grad_out, relu_mask)),
    )
    input_flat, sent, got_sums = lax.optimization_barrier((input_flat, sent, got_sums))
    theirs = swapped(sent)
    input_other = swapped(input_flat)
    sums = sums + got_sums
    sums = [sums] + [around(sums, steps) for steps in (2, 1, 3)]
    lhs, token = transposed(input_flat, input_other)
    gain = norm_gain.reshape(1, channels_out)
    even, odd, far = pre_gradient(token, place, gain, sums, mine, theirs, image_count, cell_count)
    far = around(far, 2)
    up = around(even, 1)
    down = around(odd, X - 1)

    middle = list(middle_terms(place, even, odd, lhs, col_count))
    side_place, middle[0] = lax.optimization_barrier((place, middle[0]))
    middle = [middle[0]] + [crossed(middle[steps], steps) for steps in (2, 1, 3)]
    *sides, sent_lower, sent_upper = side_terms(side_place, even, odd, up, down, far, lhs, col_count)
    sent = [sent_lower, sent_upper]
    sides[1:], sent, middle[1:] = lax.optimization_barrier((sides[1:], sent, middle[1:]))
    got = [swapped(block) for block in sent]
    weight, sides[0] = lax.optimization_barrier((weight, sides[0]))
    weight = jnp.transpose(weight, (1, 2, 0)).reshape(9 * channels_out, channels_in)
    sides = [sides[0]] + [crossed(sides[steps], steps) for steps in (2, 1, 3)]
    held_place, weight = lax.optimization_barrier((place, weight))
    held = own_blocks(held_place, even, odd, up, down, far)
    sides, weight, got, held = lax.optimization_barrier((sides, weight, got, held))
    merged = first_sum(middle, sides)
    place, merged = lax.optimization_barrier((place, merged))
    input_grad = input_gradient(place, held, got, weight, col_count)
    merged = exchanged(merged.reshape(Z * 4, 8, 9 * half))
    merged, input_grad = lax.optimization_barrier((merged, input_grad))
    inv_images = 1.0 / (image_count * Z * Y)
    merged = jnp.sum(merged.astype(F32), axis=0) * inv_images
    rows = merged.shape[0] // CORES
    kept = lax.dynamic_slice_in_dim(merged, core * rows, rows, axis=0)
    came = swapped(lax.dynamic_slice_in_dim(merged, (1 - core) * rows, rows, axis=0))
    kept, came = kept.reshape(rows, 9, half), came.reshape(rows, 9, half)
    weight_grad = jnp.concatenate(
        [jnp.where(core == 0, kept, came), jnp.where(core == 0, came, kept)], axis=2
    )

    return (input_grad.reshape(inputs.shape), weight_grad)


def solution(mesh):
    parted = Mesh(mesh.devices.reshape(Z, Y, X, CORES), AXES)
    cells = P(("z", "y"), ("x", "core"), None, None)
    return jax.shard_map(
        per_device,
        mesh=parted,
        in_specs=(cells, cells, cells, cells, P(), P()),
        out_specs=(cells, P(AXES, None, None)),
        check_vma=False,
    )
```

```python
import jax
import jax.numpy as jnp
from jax import lax
from jax.experimental import pallas as pl
from jax.experimental.pallas import tpu as pltpu
from jax.sharding import Mesh, PartitionSpec as P

RATE = 18
EPSILON = 1e-05
F32 = jnp.float32
BF16 = jnp.bfloat16
MIB = 1024 * 1024
AXES = ("z", "y", "x", "core")
Z, Y, X, CORES = 8, 4, 4, 2
SMEM = pl.BlockSpec(memory_space=pltpu.SMEM)


def device(z, y, x, core):
    return ((z * Y + y) * X + x) * CORES + core


def core_of(place_ref):
    return lax.rem(place_ref[0], CORES)


def x_of(place_ref):
    return lax.rem(lax.div(place_ref[0], CORES), X)


def y_of(place_ref):
    return lax.rem(lax.div(place_ref[0], CORES * X), Y)


def swapped(value):
    return lax.ppermute(value, "core", [(0, 1), (1, 0)])


def around(value, steps):
    return lax.ppermute(value, "x", [(source, (source + steps) % X) for source in range(X)])


def crossed(value, steps):
    pairs = []
    for z in range(Z):
        for y in range(Y):
            for x in range(X):
                pairs.append((device(z, y, x, 0), device(z, (y + steps) % Y, x, 0)))
                pairs.append((device(z, y, x, 1), device(z, y, (x + steps) % X, 1)))
    return lax.ppermute(value, AXES, pairs)


def exchanged(value):
    groups = [[device(z, y, x, 0) for z in range(Z) for x in range(X)] for y in range(Y)]
    groups += [[device(z, y, x, 1) for z in range(Z) for y in range(Y)] for x in range(X)]
    return lax.all_to_all(value, AXES, 0, 0, axis_index_groups=groups)


def whole(shape):
    return pl.BlockSpec(shape, lambda *_: (0,) * len(shape))


def kernel_call(body, operands, in_specs, out_shape, out_specs, grid=(1,), scratch=(), flops=0, vmem=8):
    moved = sum(value.size * value.dtype.itemsize for value in operands)
    moved += sum(value.size * value.dtype.itemsize for value in out_shape)
    return pl.pallas_call(
        body,
        grid=grid,
        in_specs=in_specs,
        out_specs=out_specs,
        out_shape=out_shape,
        scratch_shapes=list(scratch),
        compiler_params=pltpu.CompilerParams(vmem_limit_bytes=vmem * MIB),
        cost_estimate=pl.CostEstimate(flops=flops, bytes_accessed=moved, transcendentals=0),
    )(*operands)


def channel_sums(conv, grad, mask):
    values = conv.astype(F32)
    passed = grad.astype(F32) * mask.astype(F32)
    terms = (values, values * values, passed, passed * values)
    return jnp.stack([jnp.sum(term, axis=(1, 2)) for term in terms]).reshape(-1, conv.shape[3])


def prepare(place, conv, grad, mask):
    cells, channels = conv.shape
    half = channels // 2
    steps = 2
    tall = cells // steps

    def body(place_ref, conv_ref, grad_ref, mask_ref, mine_ref, sent_ref):
        first = core_of(place_ref) == 0
        passed = (grad_ref[...].astype(F32) * mask_ref[...].astype(F32)).astype(BF16)
        for which, value in enumerate((conv_ref[...], passed)):
            lower, upper = value[:, :half], value[:, half:]
            mine_ref[which] = jnp.where(first, lower, upper)
            sent_ref[which] = jnp.where(first, upper, lower)

    rows = pl.BlockSpec((tall, channels), lambda i: (i, 0))
    out = jax.ShapeDtypeStruct((2, cells, half), BF16)
    spec = pl.BlockSpec((2, tall, half), lambda i: (0, i, 0))
    return kernel_call(
        body,
        (place, conv, grad, mask),
        [SMEM, rows, rows, rows],
        [out, out],
        [spec, spec],
        (steps,),
        vmem=60,
    )


def pre_gradient(token, place, gain, sums, mine, theirs, images, cell_count):
    _, cells, half = mine.shape
    each = cells // images

    def body(_, place_ref, gain_ref, a_ref, b_ref, c_ref, d_ref, mine_ref, theirs_ref, even_ref, odd_ref, far_ref):
        first = core_of(place_ref) == 0
        early = x_of(place_ref) < X // 2
        means = (a_ref[...] + b_ref[...] + c_ref[...] + d_ref[...]) / cell_count
        means = jnp.where(first, means[:, :half], means[:, half:])
        gain_row = jnp.where(first, gain_ref[:, :half], gain_ref[:, half:])
        for image in range(images):
            rows = pl.ds(image * each, each)
            chan_mean, second, passed_mean, product_mean = (
                means[kind * images + image : kind * images + image + 1] for kind in range(4)
            )
            inv_std = 1.0 / jnp.sqrt(second - chan_mean * chan_mean + EPSILON)
            grad_mean = gain_row * passed_mean
            cross_mean = gain_row * (product_mean - chan_mean * passed_mean) * inv_std
            blocks = []
            for ref in (mine_ref, theirs_ref):
                values, passed = ref[0, rows, :].astype(F32), ref[1, rows, :].astype(F32)
                normed = (values - chan_mean) * inv_std
                blocks.append(inv_std * (gain_row * passed - grad_mean - normed * cross_mean))
            even = jnp.where(first, blocks[0], blocks[1])
            odd = jnp.where(first, blocks[1], blocks[0])
            even_ref[rows, :] = even.astype(BF16)
            odd_ref[rows, :] = odd.astype(BF16)
            far_ref[rows, :] = jnp.where(early, odd, even).astype(BF16)

    out = jax.ShapeDtypeStruct((cells, half), BF16)
    return kernel_call(
        body,
        (token, place, gain, *sums, mine, theirs),
        [whole(token.shape), SMEM, whole(gain.shape)] + [whole(sums[0].shape)] * 4 + [whole(mine.shape)] * 2,
        [out] * 3,
        [whole(out.shape)] * 3,
    )


def padded_count(cells):
    return -(-cells // 128) * 128


def transposed(own, other):
    cells, channels = own.shape
    deep = padded_count(cells)
    width = 256

    def body(own_ref, other_ref, out_ref, token_ref):
        token_ref[...] = jnp.zeros_like(token_ref)
        for which, ref in enumerate((own_ref, other_ref)):
            block = jnp.concatenate([ref[...], jnp.zeros((deep - cells, width), BF16)], axis=0)
            out_ref[:, which * deep : (which + 1) * deep] = block.T

    spec = pl.BlockSpec((cells, width), lambda i: (0, i))
    return kernel_call(
        body,
        (own, other),
        [spec, spec],
        [jax.ShapeDtypeStruct((channels, 2 * deep), BF16), jax.ShapeDtypeStruct((8, 128), F32)],
        [pl.BlockSpec((width, 2 * deep), lambda i: (i, 0)), whole((8, 128))],
        (channels // width,),
    )


def column_taps(block, col_count):
    cells, channels = block.shape
    wide = block.astype(F32)
    column = lax.broadcasted_iota(jnp.int32, (cells // col_count, col_count, channels), 1)
    column = column.reshape(cells, channels)
    before = jnp.where(column < col_count - RATE, pltpu.roll(wide, cells - RATE, 0), 0.0)
    after = jnp.where(column >= RATE, pltpu.roll(wide, RATE, 0), 0.0)
    return before.astype(BF16), block, after.astype(BF16)


def fill(stacked, slot, place, block, col_count):
    cells, width = block.shape
    deep = padded_count(cells)
    for spot, tap in enumerate(column_taps(block, col_count)):
        columns = slice((place + spot) * width, (place + spot + 1) * width)
        stacked[slot * deep : slot * deep + cells, columns] = tap


def clear_padding(stacked, cells):
    deep, columns = stacked.shape
    block = deep // 2
    for slot in range(2):
        stacked[slot * block + cells : (slot + 1) * block, :] = jnp.zeros((block - cells, columns), BF16)


def multiply(place_ref, lhs_ref, stacked, total, out_refs):
    columns = stacked.shape[1]
    product = jnp.dot(lhs_ref[...], stacked[...], preferred_element_type=F32)
    total[...] = product.reshape(total.shape)
    tall = total.shape[0] * 32

    @pl.when(core_of(place_ref) == 0)
    def _():
        for steps in range(Y):
            chunk = total[:, lax.rem(y_of(place_ref) + steps, Y), :, :, :]
            out_refs[steps][...] = chunk.reshape(tall, columns).astype(BF16)

    @pl.when(core_of(place_ref) != 0)
    def _():
        for steps in range(X):
            chunk = total[:, :, lax.rem(x_of(place_ref) + steps, X), :, :]
            out_refs[steps][...] = chunk.reshape(tall, columns).astype(BF16)


def product_call(body, place, fixed, lhs, columns, extra):
    channels_in, deep = lhs.shape
    steps = 2
    tall = channels_in // steps
    return kernel_call(
        body,
        (place, *fixed, lhs),
        [SMEM] + [whole(value.shape) for value in fixed] + [pl.BlockSpec((tall, deep), lambda i: (i, 0))],
        [jax.ShapeDtypeStruct((channels_in // 4, columns), BF16)] * 4 + extra,
        [pl.BlockSpec((tall // 4, columns), lambda i: (i, 0))] * 4 + [whole(value.shape) for value in extra],
        (steps,),
        [pltpu.VMEM((deep, columns), BF16), pltpu.VMEM((tall // 128, Y, X, 8, columns), F32)],
        flops=2 * channels_in * deep * columns,
        vmem=10,
    )


def middle_terms(place, even, odd, lhs, col_count):
    cells, width = even.shape

    def body(place_ref, even_ref, odd_ref, lhs_ref, *rest):
        stacked, total = rest[4:]

        @pl.when(pl.program_id(0) == 0)
        def _():
            clear_padding(stacked, cells)
            first = core_of(place_ref) == 0
            even_block, odd_block = even_ref[...], odd_ref[...]
            fill(stacked, 0, 0, jnp.where(first, even_block, odd_block), col_count)
            fill(stacked, 1, 0, jnp.where(first, odd_block, even_block), col_count)

        multiply(place_ref, lhs_ref, stacked, total, rest[:4])

    return product_call(body, place, [even, odd], lhs, 3 * width, [])


def tap_blocks(place_ref, even_ref, odd_ref, far_ref, up_ref, down_ref):
    x = x_of(place_ref)
    far_block = far_ref[...]
    zero = jnp.zeros_like(far_block)
    far_down = jnp.where(x < X // 2, far_block, zero)
    far_up = jnp.where(x < X // 2, zero, far_block)
    down_block = jnp.where(x < X - 1, down_ref[...], zero)
    up_block = jnp.where(x > 0, up_ref[...], zero)
    return (down_block, far_down), (even_ref[...], odd_ref[...]), (far_up, up_block)


def own_blocks(place, even, odd, far, up, down):
    operands = (even, odd, far, up, down)

    def body(place_ref, *refs):
        first = core_of(place_ref) == 0
        for side, (lower, upper) in enumerate(tap_blocks(place_ref, *refs[:5])):
            refs[5][side] = jnp.where(first, lower, upper)

    out = jax.ShapeDtypeStruct((3,) + even.shape, BF16)
    return kernel_call(
        body,
        (place, *operands),
        [SMEM] + [whole(value.shape) for value in operands],
        [out],
        [whole(out.shape)],
    )[0]


def side_terms(place, even, odd, far, up, down, lhs, col_count):
    cells, width = up.shape

    def body(place_ref, even_ref, odd_ref, far_ref, up_ref, down_ref, lhs_ref, *rest):
        theirs_refs = rest[4:6]
        stacked, total = rest[6:]

        @pl.when(pl.program_id(0) == 0)
        def _():
            clear_padding(stacked, cells)
            first = core_of(place_ref) == 0
            blocks = tap_blocks(place_ref, even_ref, odd_ref, far_ref, up_ref, down_ref)
            for side, (lower, upper) in enumerate(blocks):
                theirs = jnp.where(first, upper, lower)
                for part, ref in enumerate(theirs_refs):
                    ref[side] = theirs[part * (cells // 2) : (part + 1) * (cells // 2)]
                if side != 1:
                    mine = jnp.where(first, lower, upper)
                    fill(stacked, 0, 3 * (side // 2), mine, col_count)
                    fill(stacked, 1, 3 * (side // 2), theirs, col_count)

        multiply(place_ref, lhs_ref, stacked, total, rest[:4])

    part = jax.ShapeDtypeStruct((3, cells // 2, width), BF16)
    return product_call(body, place, [even, odd, far, up, down], lhs, 6 * width, [part, part])


def first_sum(middle, sides):
    rows, third = middle[0].shape

    def body(*refs):
        out_ref = refs[-1]
        middle_total = sum(ref[...].astype(F32) for ref in refs[:4])
        side_total = sum(ref[...].astype(F32) for ref in refs[4:8])
        out_ref[:, :third] = side_total[:, :third].astype(BF16)
        out_ref[:, third : 2 * third] = middle_total.astype(BF16)
        out_ref[:, 2 * third :] = side_total[:, third:].astype(BF16)

    steps = 2
    spec = lambda columns: pl.BlockSpec((rows // steps, columns), lambda i: (i, 0))
    return kernel_call(
        body,
        (*middle, *sides),
        [spec(third)] * 4 + [spec(2 * third)] * 4,
        [jax.ShapeDtypeStruct((rows, 3 * third), BF16)],
        [spec(3 * third)],
        (steps,),
    )[0]


def input_gradient(place, held, got, weight, col_count):
    _, cells, half = held.shape
    deep, channels_in = weight.shape
    width = 256

    def body(place_ref, held_ref, *rest):
        got_refs, (weight_ref, out_ref, stacked) = rest[:2], rest[2:]

        @pl.when(pl.program_id(0) == 0)
        def _():
            first = core_of(place_ref) == 0
            for side in range(3):
                mine = held_ref[side]
                theirs = jnp.concatenate([ref[side] for ref in got_refs], axis=0)
                lower, upper = jnp.where(first, mine, theirs), jnp.where(first, theirs, mine)
                for part, block in enumerate((lower, upper)):
                    for spot, tap in enumerate(column_taps(block, col_count)):
                        start = (2 * (3 * side + spot) + part) * half
                        stacked[:, start : start + half] = tap

        out_ref[...] = jnp.dot(
            stacked[...], weight_ref[...], preferred_element_type=F32
        ).astype(BF16)

    return kernel_call(
        body,
        (place, held, *got, weight),
        [SMEM, whole(held.shape)] + [whole(block.shape) for block in got] + [pl.BlockSpec((deep, width), lambda i: (0, i))],
        [jax.ShapeDtypeStruct((cells, channels_in), BF16)],
        [pl.BlockSpec((cells, width), lambda i: (0, i))],
        (channels_in // width,),
        [pltpu.VMEM((cells, deep), BF16)],
        2 * cells * deep * channels_in,
        60,
    )[0]


def per_device(inputs, conv_out, grad_out, relu_mask, norm_gain, weight):
    image_count, row_count, col_count, channels_in = inputs.shape
    channels_out = conv_out.shape[3]
    cell_count = row_count * col_count * X * CORES
    cells = image_count * row_count * col_count
    half = channels_out // 2
    core = lax.axis_index("core")
    place = jnp.reshape(lax.axis_index(AXES), (1,)).astype(jnp.int32)

    input_flat = inputs.reshape(cells, channels_in)
    sums = channel_sums(conv_out, grad_out, relu_mask)
    got_sums = swapped(sums)
    mine, sent = prepare(
        place,
        *(value.reshape(cells, channels_out) for value in (conv_out, grad_out, relu_mask)),
    )
    input_flat, sent, got_sums = lax.optimization_barrier((input_flat, sent, got_sums))
    theirs = swapped(sent)
    input_other = swapped(input_flat)
    sums = sums + got_sums
    sums = [sums] + [around(sums, steps) for steps in (2, 1, 3)]
    lhs, token = transposed(input_flat, input_other)
    gain = norm_gain.reshape(1, channels_out)
    even, odd, far = pre_gradient(token, place, gain, sums, mine, theirs, image_count, cell_count)
    far = around(far, 2)
    up = around(even, 1)
    down = around(odd, X - 1)

    middle = list(middle_terms(place, even, odd, lhs, col_count))
    side_place, middle[0] = lax.optimization_barrier((place, middle[0]))
    middle = [middle[0]] + [crossed(middle[steps], steps) for steps in (2, 1, 3)]
    *sides, sent_lower, sent_upper = side_terms(side_place, even, odd, far, up, down, lhs, col_count)
    sent = [sent_lower, sent_upper]
    sides[1:], sent, middle[1:] = lax.optimization_barrier((sides[1:], sent, middle[1:]))
    got = [swapped(block) for block in sent]
    weight, sides[0] = lax.optimization_barrier((weight, sides[0]))
    weight = jnp.transpose(weight, (1, 2, 0)).reshape(9 * channels_out, channels_in)
    sides = [sides[0]] + [crossed(sides[steps], steps) for steps in (2, 1, 3)]
    held_place, weight = lax.optimization_barrier((place, weight))
    held = own_blocks(held_place, even, odd, far, up, down)
    sides, weight, got, held = lax.optimization_barrier((sides, weight, got, held))
    merged = first_sum(middle, sides)
    place, merged = lax.optimization_barrier((place, merged))
    input_grad = input_gradient(place, held, got, weight, col_count)
    merged = exchanged(merged.reshape(Z * 4, 8, 9 * half))
    merged, input_grad = lax.optimization_barrier((merged, input_grad))
    inv_images = 1.0 / (image_count * Z * Y)
    merged = jnp.sum(merged.astype(F32), axis=0) * inv_images
    rows = merged.shape[0] // CORES
    kept = lax.dynamic_slice_in_dim(merged, core * rows, rows, axis=0)
    came = swapped(lax.dynamic_slice_in_dim(merged, (1 - core) * rows, rows, axis=0))
    kept, came = kept.reshape(rows, 9, half), came.reshape(rows, 9, half)
    weight_grad = jnp.concatenate(
        [jnp.where(core == 0, kept, came), jnp.where(core == 0, came, kept)], axis=2
    )

    return (input_grad.reshape(inputs.shape), weight_grad)


def solution(mesh):
    parted = Mesh(mesh.devices.reshape(Z, Y, X, CORES), AXES)
    cells = P(("z", "y"), ("x", "core"), None, None)
    return jax.shard_map(
        per_device,
        mesh=parted,
        in_specs=(cells, cells, cells, cells, P(), P()),
        out_specs=(cells, P(AXES, None, None)),
        check_vma=False,
    )
```

```python
import jax
import jax.numpy as jnp
from jax import lax
from jax.experimental import pallas as pl
from jax.experimental.pallas import tpu as pltpu
from jax.sharding import Mesh, PartitionSpec as P

RATE = 18
EPSILON = 1e-05
F32 = jnp.float32
BF16 = jnp.bfloat16
MIB = 1024 * 1024
AXES = ("z", "y", "x", "core")
Z, Y, X, CORES = 8, 4, 4, 2
SMEM = pl.BlockSpec(memory_space=pltpu.SMEM)


def device(z, y, x, core):
    return ((z * Y + y) * X + x) * CORES + core


def core_of(place_ref):
    return lax.rem(place_ref[0], CORES)


def x_of(place_ref):
    return lax.rem(lax.div(place_ref[0], CORES), X)


def y_of(place_ref):
    return lax.rem(lax.div(place_ref[0], CORES * X), Y)


def swapped(value):
    return lax.ppermute(value, "core", [(0, 1), (1, 0)])


def around(value, steps):
    return lax.ppermute(value, "x", [(source, (source + steps) % X) for source in range(X)])


def crossed(value, steps):
    pairs = []
    for z in range(Z):
        for y in range(Y):
            for x in range(X):
                pairs.append((device(z, y, x, 0), device(z, (y + steps) % Y, x, 0)))
                pairs.append((device(z, y, x, 1), device(z, y, (x + steps) % X, 1)))
    return lax.ppermute(value, AXES, pairs)


def exchanged(value):
    groups = [[device(z, y, x, 0) for z in range(Z) for x in range(X)] for y in range(Y)]
    groups += [[device(z, y, x, 1) for z in range(Z) for y in range(Y)] for x in range(X)]
    return lax.all_to_all(value, AXES, 0, 0, axis_index_groups=groups)


def whole(shape):
    return pl.BlockSpec(shape, lambda *_: (0,) * len(shape))


def kernel_call(body, operands, in_specs, out_shape, out_specs, grid=(1,), scratch=(), flops=0, vmem=8):
    moved = sum(value.size * value.dtype.itemsize for value in operands)
    moved += sum(value.size * value.dtype.itemsize for value in out_shape)
    return pl.pallas_call(
        body,
        grid=grid,
        in_specs=in_specs,
        out_specs=out_specs,
        out_shape=out_shape,
        scratch_shapes=list(scratch),
        compiler_params=pltpu.CompilerParams(vmem_limit_bytes=vmem * MIB),
        cost_estimate=pl.CostEstimate(flops=flops, bytes_accessed=moved, transcendentals=0),
    )(*operands)


def channel_sums(conv, grad, mask):
    values = conv.astype(F32)
    passed = grad.astype(F32) * mask.astype(F32)
    terms = (values, values * values, passed, passed * values)
    return jnp.stack([jnp.sum(term, axis=(1, 2)) for term in terms]).reshape(-1, conv.shape[3])


def prepare(place, conv, grad, mask):
    cells, channels = conv.shape
    half = channels // 2
    steps = 2
    tall = cells // steps

    def body(place_ref, conv_ref, grad_ref, mask_ref, mine_ref, sent_ref):
        first = core_of(place_ref) == 0
        passed = (grad_ref[...].astype(F32) * mask_ref[...].astype(F32)).astype(BF16)
        for which, value in enumerate((conv_ref[...], passed)):
            lower, upper = value[:, :half], value[:, half:]
            mine_ref[which] = jnp.where(first, lower, upper)
            sent_ref[which] = jnp.where(first, upper, lower)

    rows = pl.BlockSpec((tall, channels), lambda i: (i, 0))
    out = jax.ShapeDtypeStruct((2, cells, half), BF16)
    spec = pl.BlockSpec((2, tall, half), lambda i: (0, i, 0))
    return kernel_call(
        body,
        (place, conv, grad, mask),
        [SMEM, rows, rows, rows],
        [out, out],
        [spec, spec],
        (steps,),
        vmem=60,
    )


def pre_gradient(token, place, gain, sums, mine, theirs, images, cell_count):
    _, cells, half = mine.shape
    each = cells // images

    def body(_, place_ref, gain_ref, a_ref, b_ref, c_ref, d_ref, mine_ref, theirs_ref, even_ref, odd_ref, far_ref):
        first = core_of(place_ref) == 0
        early = x_of(place_ref) < X // 2
        means = (a_ref[...] + b_ref[...] + c_ref[...] + d_ref[...]) / cell_count
        means = jnp.where(first, means[:, :half], means[:, half:])
        gain_row = jnp.where(first, gain_ref[:, :half], gain_ref[:, half:])
        for image in range(images):
            rows = pl.ds(image * each, each)
            chan_mean, second, passed_mean, product_mean = (
                means[kind * images + image : kind * images + image + 1] for kind in range(4)
            )
            inv_std = 1.0 / jnp.sqrt(second - chan_mean * chan_mean + EPSILON)
            grad_mean = gain_row * passed_mean
            cross_mean = gain_row * (product_mean - chan_mean * passed_mean) * inv_std
            blocks = []
            for ref in (mine_ref, theirs_ref):
                values, passed = ref[0, rows, :].astype(F32), ref[1, rows, :].astype(F32)
                normed = (values - chan_mean) * inv_std
                blocks.append(inv_std * (gain_row * passed - grad_mean - normed * cross_mean))
            even = jnp.where(first, blocks[0], blocks[1])
            odd = jnp.where(first, blocks[1], blocks[0])
            even_ref[rows, :] = even.astype(BF16)
            odd_ref[rows, :] = odd.astype(BF16)
            far_ref[rows, :] = jnp.where(early, odd, even).astype(BF16)

    out = jax.ShapeDtypeStruct((cells, half), BF16)
    return kernel_call(
        body,
        (token, place, gain, *sums, mine, theirs),
        [whole(token.shape), SMEM, whole(gain.shape)] + [whole(sums[0].shape)] * 4 + [whole(mine.shape)] * 2,
        [out] * 3,
        [whole(out.shape)] * 3,
    )


def padded_count(cells):
    return -(-cells // 128) * 128


def transposed(own, other):
    cells, channels = own.shape
    deep = padded_count(cells)
    width = 256

    def body(own_ref, other_ref, out_ref, token_ref):
        token_ref[...] = jnp.zeros_like(token_ref)
        for which, ref in enumerate((own_ref, other_ref)):
            block = jnp.concatenate([ref[...], jnp.zeros((deep - cells, width), BF16)], axis=0)
            out_ref[:, which * deep : (which + 1) * deep] = block.T

    spec = pl.BlockSpec((cells, width), lambda i: (0, i))
    return kernel_call(
        body,
        (own, other),
        [spec, spec],
        [jax.ShapeDtypeStruct((channels, 2 * deep), BF16), jax.ShapeDtypeStruct((8, 128), F32)],
        [pl.BlockSpec((width, 2 * deep), lambda i: (i, 0)), whole((8, 128))],
        (channels // width,),
    )


def column_taps(block, col_count):
    cells, channels = block.shape
    wide = block.astype(F32)
    column = lax.broadcasted_iota(jnp.int32, (cells // col_count, col_count, channels), 1)
    column = column.reshape(cells, channels)
    before = jnp.where(column < col_count - RATE, pltpu.roll(wide, cells - RATE, 0), 0.0)
    after = jnp.where(column >= RATE, pltpu.roll(wide, RATE, 0), 0.0)
    return before.astype(BF16), block, after.astype(BF16)


def fill(stacked, slot, place, block, col_count):
    cells, width = block.shape
    deep = padded_count(cells)
    for spot, tap in enumerate(column_taps(block, col_count)):
        columns = slice((place + spot) * width, (place + spot + 1) * width)
        stacked[slot * deep : slot * deep + cells, columns] = tap


def clear_padding(stacked, cells):
    deep, columns = stacked.shape
    block = deep // 2
    for slot in range(2):
        stacked[slot * block + cells : (slot + 1) * block, :] = jnp.zeros((block - cells, columns), BF16)


def multiply(place_ref, lhs_ref, stacked, total, out_refs):
    columns = stacked.shape[1]
    product = jnp.dot(lhs_ref[...], stacked[...], preferred_element_type=F32)
    total[...] = product.reshape(total.shape)
    tall = total.shape[0] * 32

    @pl.when(core_of(place_ref) == 0)
    def _():
        for steps in range(Y):
            chunk = total[:, lax.rem(y_of(place_ref) + steps, Y), :, :, :]
            out_refs[steps][...] = chunk.reshape(tall, columns).astype(BF16)

    @pl.when(core_of(place_ref) != 0)
    def _():
        for steps in range(X):
            chunk = total[:, :, lax.rem(x_of(place_ref) + steps, X), :, :]
            out_refs[steps][...] = chunk.reshape(tall, columns).astype(BF16)


def product_call(body, place, fixed, lhs, columns, extra):
    channels_in, deep = lhs.shape
    steps = 2
    tall = channels_in // steps
    return kernel_call(
        body,
        (place, *fixed, lhs),
        [SMEM] + [whole(value.shape) for value in fixed] + [pl.BlockSpec((tall, deep), lambda i: (i, 0))],
        [jax.ShapeDtypeStruct((channels_in // 4, columns), BF16)] * 4 + extra,
        [pl.BlockSpec((tall // 4, columns), lambda i: (i, 0))] * 4 + [whole(value.shape) for value in extra],
        (steps,),
        [pltpu.VMEM((deep, columns), BF16), pltpu.VMEM((tall // 128, Y, X, 8, columns), F32)],
        flops=2 * channels_in * deep * columns,
        vmem=24,
    )


def middle_terms(place, even, odd, lhs, col_count):
    cells, width = even.shape

    def body(place_ref, even_ref, odd_ref, lhs_ref, *rest):
        stacked, total = rest[4:]

        @pl.when(pl.program_id(0) == 0)
        def _():
            clear_padding(stacked, cells)
            first = core_of(place_ref) == 0
            even_block, odd_block = even_ref[...], odd_ref[...]
            fill(stacked, 0, 0, jnp.where(first, even_block, odd_block), col_count)
            fill(stacked, 1, 0, jnp.where(first, odd_block, even_block), col_count)

        multiply(place_ref, lhs_ref, stacked, total, rest[:4])

    return product_call(body, place, [even, odd], lhs, 3 * width, [])


def side_terms(place, even, odd, up, down, far, lhs, col_count):
    cells, width = up.shape

    def body(place_ref, even_ref, odd_ref, up_ref, down_ref, far_ref, lhs_ref, *rest):
        mine_ref, theirs_ref, stacked, total = rest[4:]

        @pl.when(pl.program_id(0) == 0)
        def _():
            clear_padding(stacked, cells)
            first = core_of(place_ref) == 0
            early = x_of(place_ref) < X // 2
            far_block = far_ref[...]
            zero = jnp.zeros_like(far_block)
            far_down = jnp.where(early, far_block, zero)
            far_up = jnp.where(early, zero, far_block)
            down_block = jnp.where(x_of(place_ref) < X - 1, down_ref[...], zero)
            up_block = jnp.where(x_of(place_ref) > 0, up_ref[...], zero)
            pairs = ((down_block, far_down), (even_ref[...], odd_ref[...]), (far_up, up_block))
            for side, (lower, upper) in enumerate(pairs):
                mine = jnp.where(first, lower, upper)
                theirs = jnp.where(first, upper, lower)
                mine_ref[side] = mine
                theirs_ref[side] = theirs
                if side != 1:
                    fill(stacked, 0, 3 * (side // 2), mine, col_count)
                    fill(stacked, 1, 3 * (side // 2), theirs, col_count)

        multiply(place_ref, lhs_ref, stacked, total, rest[:4])

    triple = jax.ShapeDtypeStruct((3, cells, width), BF16)
    return product_call(body, place, [even, odd, up, down, far], lhs, 6 * width, [triple, triple])


def first_sum(middle, sides):
    rows, third = middle[0].shape

    def body(*refs):
        out_ref = refs[-1]
        middle_total = sum(ref[...].astype(F32) for ref in refs[:4])
        side_total = sum(ref[...].astype(F32) for ref in refs[4:8])
        out_ref[:, :third] = side_total[:, :third].astype(BF16)
        out_ref[:, third : 2 * third] = middle_total.astype(BF16)
        out_ref[:, 2 * third :] = side_total[:, third:].astype(BF16)

    steps = 2
    spec = lambda columns: pl.BlockSpec((rows // steps, columns), lambda i: (i, 0))
    return kernel_call(
        body,
        (*middle, *sides),
        [spec(third)] * 4 + [spec(2 * third)] * 4,
        [jax.ShapeDtypeStruct((rows, 3 * third), BF16)],
        [spec(3 * third)],
        (steps,),
    )[0]


def input_gradient(place, held, got, weight, col_count):
    _, cells, half = held.shape
    deep, channels_in = weight.shape
    width = 256

    def body(place_ref, held_ref, got_ref, weight_ref, out_ref, stacked):
        @pl.when(pl.program_id(0) == 0)
        def _():
            first = core_of(place_ref) == 0
            for side in range(3):
                mine, theirs = held_ref[side], got_ref[side]
                lower, upper = jnp.where(first, mine, theirs), jnp.where(first, theirs, mine)
                for part, block in enumerate((lower, upper)):
                    for spot, tap in enumerate(column_taps(block, col_count)):
                        start = (2 * (3 * side + spot) + part) * half
                        stacked[:, start : start + half] = tap

        out_ref[...] = jnp.dot(
            stacked[...], weight_ref[...], preferred_element_type=F32
        ).astype(BF16)

    return kernel_call(
        body,
        (place, held, got, weight),
        [SMEM, whole(held.shape), whole(got.shape), pl.BlockSpec((deep, width), lambda i: (0, i))],
        [jax.ShapeDtypeStruct((cells, channels_in), BF16)],
        [pl.BlockSpec((cells, width), lambda i: (0, i))],
        (channels_in // width,),
        [pltpu.VMEM((cells, deep), BF16)],
        2 * cells * deep * channels_in,
        24,
    )[0]


def per_device(inputs, conv_out, grad_out, relu_mask, norm_gain, weight):
    image_count, row_count, col_count, channels_in = inputs.shape
    channels_out = conv_out.shape[3]
    cell_count = row_count * col_count * X * CORES
    cells = image_count * row_count * col_count
    half = channels_out // 2
    core = lax.axis_index("core")
    place = jnp.reshape(lax.axis_index(AXES), (1,)).astype(jnp.int32)

    input_flat = inputs.reshape(cells, channels_in)
    sums = channel_sums(conv_out, grad_out, relu_mask)
    got_sums = swapped(sums)
    mine, sent = prepare(
        place,
        *(value.reshape(cells, channels_out) for value in (conv_out, grad_out, relu_mask)),
    )
    input_flat, sent, got_sums = lax.optimization_barrier((input_flat, sent, got_sums))
    theirs = swapped(sent)
    input_other = swapped(input_flat)
    sums = sums + got_sums
    sums = [sums] + [around(sums, steps) for steps in (2, 1, 3)]
    lhs, token = transposed(input_flat, input_other)
    gain = norm_gain.reshape(1, channels_out)
    even, odd, far = pre_gradient(token, place, gain, sums, mine, theirs, image_count, cell_count)
    far = around(far, 2)
    up = around(even, 1)
    down = around(odd, X - 1)

    middle = list(middle_terms(place, even, odd, lhs, col_count))
    side_place, middle[0] = lax.optimization_barrier((place, middle[0]))
    middle = [middle[0]] + [crossed(middle[steps], steps) for steps in (2, 1, 3)]
    *sides, held, sent = side_terms(side_place, even, odd, up, down, far, lhs, col_count)
    sides[1:], sent, middle[1:] = lax.optimization_barrier((sides[1:], sent, middle[1:]))
    got = swapped(sent)
    weight, sides[0] = lax.optimization_barrier((weight, sides[0]))
    weight = jnp.transpose(weight, (1, 2, 0)).reshape(9 * channels_out, channels_in)
    sides = [sides[0]] + [crossed(sides[steps], steps) for steps in (2, 1, 3)]
    sides, weight = lax.optimization_barrier((sides, weight))
    merged = first_sum(middle, sides)
    place, merged = lax.optimization_barrier((place, merged))
    input_grad = input_gradient(place, held, got, weight, col_count)
    merged = exchanged(merged.reshape(Z * 4, 8, 9 * half))
    merged, input_grad = lax.optimization_barrier((merged, input_grad))
    inv_images = 1.0 / (image_count * Z * Y)
    merged = jnp.sum(merged.astype(F32), axis=0) * inv_images
    rows = merged.shape[0] // CORES
    kept = lax.dynamic_slice_in_dim(merged, core * rows, rows, axis=0)
    came = swapped(lax.dynamic_slice_in_dim(merged, (1 - core) * rows, rows, axis=0))
    kept, came = kept.reshape(rows, 9, half), came.reshape(rows, 9, half)
    weight_grad = jnp.concatenate(
        [jnp.where(core == 0, kept, came), jnp.where(core == 0, came, kept)], axis=2
    )

    return (input_grad.reshape(inputs.shape), weight_grad)


def solution(mesh):
    parted = Mesh(mesh.devices.reshape(Z, Y, X, CORES), AXES)
    cells = P(("z", "y"), ("x", "core"), None, None)
    return jax.shard_map(
        per_device,
        mesh=parted,
        in_specs=(cells, cells, cells, cells, P(), P()),
        out_specs=(cells, P(AXES, None, None)),
        check_vma=False,
    )
```
